32 devices in a mesh: tm: 4 (over z), clip: 8 (over y, x, core).
Axes of the slice: x: 2, y: 2, z: 4, core: 2. Of those that a mesh axis runs over, the one named last changes fastest.
Arguments:
- tokens: bfloat16 [4, 128, 196, 384], P('tm', 'clip'), may hold values from -6 to 6
- cotangent: bfloat16 [4, 128, 196, 384], P('tm', 'clip'), may hold values from -6 to 6
- lane_frames: int32 [128], P('clip'), may hold values from 0 to 32, as said below
- pre_gain: bfloat16 [384], replicated, may hold values from 0.5 to 1.5
- pre_bias: bfloat16 [384], replicated, may hold values from -3 to 3
- w_project: bfloat16 [384, 1152], replicated, may hold values from -0.3125 to 0.3125
- query_bias: bfloat16 [384], replicated, may hold values from -3 to 3
- value_bias: bfloat16 [384], replicated, may hold values from -3 to 3
- w_out: bfloat16 [384, 384], replicated, may hold values from -1.25 to 1.25
- out_bias: bfloat16 [384], replicated, may hold values from -3 to 3
- mid_gain: bfloat16 [384], replicated, may hold values from 0.5 to 1.5
- mid_bias: bfloat16 [384], replicated, may hold values from -3 to 3
- w_up: bfloat16 [384, 1536], replicated, may hold values from -0.3125 to 0.3125
- up_bias: bfloat16 [1536], replicated, may hold values from -3 to 3
- w_down: bfloat16 [1536, 384], replicated, may hold values from -0.15625 to 0.15625
- down_bias: bfloat16 [384], replicated, may hold values from -3 to 3
Outputs:
- layer_output: bfloat16 [4, 128, 196, 384], P('tm', 'clip')
- input_grad: bfloat16 [4, 128, 196, 384], P('tm', 'clip')
- grad_pre_gain: float32 [384], replicated
- grad_pre_bias: float32 [384], replicated
- grad_w_project: float32 [384, 1152], replicated
- grad_query_bias: float32 [384], replicated
- grad_value_bias: float32 [384], replicated
- grad_w_out: float32 [384, 384], replicated
- grad_out_bias: float32 [384], replicated
- grad_mid_gain: float32 [384], replicated
- grad_mid_bias: float32 [384], replicated
- grad_w_up: float32 [384, 1536], replicated
- grad_up_bias: float32 [1536], replicated
- grad_w_down: float32 [1536, 384], replicated
- grad_down_bias: float32 [384], replicated
The draws below stay inside these ranges and needn't reach their ends.
Inputs may be any that keep to these rules, and one draw needn't show every extreme that they name: `lane_frames`: each value is 0, 8, 16 or 32. A clip of f frames fills f / 8 consecutive lanes of one clip index, starting at a lane that is a multiple of f / 8 within that index's 16 lanes, and each of those lanes holds f; 0 marks an empty lane; the first lane of every clip index holds a clip.
All inputs are finite; a program needn't handle non-finite values.
Results may differ from the reference program's by a relative error of at most 0.012.
Values may be sent and summed in bfloat16 or wider, within the bound.
A program may use at most 320 MiB of HBM per device.

```python
import jax
import jax.numpy as jnp
from jax import lax

D = 384
HEAD_DIM = 64
FF = 1536
SPATIAL = 196
LANES_ALL = 128
N_TM = 4


def draw_lane_frames(key, part):
    key = jax.random.fold_in(key, 7)
    patterns = jnp.array([[32, 32, 32, 32], [16, 16, 16, 16], [16, 16, 8, 8], [8, 8, 8, 8], [8, 8, 16, 16], [16, 16, 0, 0], [8, 0, 0, 0], [8, 8, 0, 0], [8, 8, 8, 8], [16, 16, 8, 8]], dtype=jnp.int32)
    block_total = LANES_ALL // 4
    chosen = jax.random.randint(key, (block_total,), 0, 10)
    chosen = chosen.at[0].set(0).at[block_total - 1].set(6)
    return patterns[chosen].reshape(-1)


def block_levels(own_key, dims, split, least, high):
    loudness = 1.0
    for position, shards_of in split:
        heights = jax.random.uniform(jax.random.fold_in(jax.random.fold_in(own_key, 6), position), (shards_of,), jnp.float32, least / len(split), high / len(split))
        loudness = loudness * jnp.repeat(jnp.exp(heights), dims[position] // shards_of).reshape((-1,) + (1,) * (len(dims) - 1 - position))
    return loudness


def noise(key, extent, deviation, bound, shards=(), held_as=jnp.bfloat16):
    result = deviation * jax.random.normal(key, extent, jnp.float32)
    if shards:
        result = result * block_levels(key, extent, shards, -0.22, 0.18)
    return jnp.clip(result, -bound, bound).astype(held_as)


def setup_inputs(seed: int = 0) -> dict:
    key_list = jax.random.split(jax.random.key(seed), 17)
    return {
        "tokens": noise(key_list[0], (N_TM, LANES_ALL, SPATIAL, D), 1.0, 6.0, ((0, 4), (1, 8))),
        "cotangent": noise(key_list[1], (N_TM, LANES_ALL, SPATIAL, D), 1.0, 6.0, ((0, 4), (1, 8))),
        "lane_frames": draw_lane_frames(jax.random.fold_in(key_list[16], 71), 0),
        "pre_gain": jnp.clip(1.0 + 0.1 * jax.random.normal(key_list[3], (D,), jnp.float32), 0.5, 1.5).astype(jnp.bfloat16),
        "pre_bias": noise(key_list[4], (D,), 0.3, 3.0),
        "w_project": noise(key_list[5], (D, 3 * D), D ** -0.5, 0.3125),
        "query_bias": noise(key_list[6], (D,), 0.5, 3.0),
        "value_bias": noise(key_list[7], (D,), 0.5, 3.0),
        "w_out": noise(key_list[8], (D, D), (D // 16) ** -0.5, 1.25),
        "out_bias": noise(key_list[9], (D,), 0.3, 3.0),
        "mid_gain": jnp.clip(1.0 + 0.1 * jax.random.normal(key_list[10], (D,), jnp.float32), 0.5, 1.5).astype(jnp.bfloat16),
        "mid_bias": noise(key_list[11], (D,), 0.3, 3.0),
        "w_up": noise(key_list[12], (D, FF), D ** -0.5, 0.3125),
        "up_bias": noise(key_list[13], (FF,), 0.5, 3.0),
        "w_down": noise(key_list[14], (FF, D), FF ** -0.5, 0.15625),
        "down_bias": noise(key_list[15], (D,), 0.3, 3.0),
    }


epsilon = 1e-06
masked_low = -1e+30

@jax.custom_vjp
def low(v):
    return lax.optimization_barrier(v.astype(jnp.bfloat16)).astype(jnp.float32)

@jax.custom_vjp
def low_back(v):
    return v

def low_keep(v):
    return (low(v), None)

def low_pass(kept, grad):
    return (grad,)

def back_keep(v):
    return (v, None)

def back_low(kept, grad):
    return (low(grad),)
low.defvjp(low_keep, low_pass)
low_back.defvjp(back_keep, back_low)

def layer_norm(inputs, norm_gain, norm_bias):
    center = inputs - lax.optimization_barrier(jnp.mean(inputs, -1, keepdims=True))
    spread = lax.optimization_barrier(jnp.mean(center * center, -1, keepdims=True))
    return center * lax.rsqrt(spread + epsilon) * norm_gain + norm_bias

def neighbours(slot_data, features):
    padded = jnp.pad(slot_data, ((1, 1), (0, 0), (0, 0)))
    joined = jnp.concatenate([padded[:-2], padded[1:-1], padded[2:]], 1)
    return joined.reshape(slot_data.shape[0], 3 * slot_data.shape[1], features // HEAD_DIM, HEAD_DIM)

def block_layer(params, inputs, lower_ok, upper_ok, occupied):
    pre_gain, pre_bias, w_project, query_bias, value_bias, w_out, out_bias, mid_gain, mid_bias, w_up, up_bias, w_down, down_bias = params
    highest = lax.Precision.HIGHEST
    slot_count, spatial, features = inputs.shape
    flat_rows = inputs.reshape(-1, features)
    normed = low(layer_norm(flat_rows, pre_gain, pre_bias))
    projected = jnp.dot(normed, w_project, precision=highest)
    queries = low(low_back(projected[:, :features] + query_bias))
    key_rows = low(low_back(projected[:, features:2 * features]))
    value_rows = low(low_back(projected[:, 2 * features:] + value_bias))
    query_heads = queries.reshape(slot_count, spatial, features // HEAD_DIM, HEAD_DIM)
    key_heads = neighbours(key_rows.reshape(slot_count, spatial, features), features)
    value_heads = neighbours(value_rows.reshape(slot_count, spatial, features), features)
    scores = jnp.einsum('gqhe,gkhe->ghqk', query_heads, key_heads, precision=highest) * HEAD_DIM ** (-0.5)
    scores = low_back(scores)
    full_rows = jnp.ones((slot_count, spatial), jnp.bool_)
    key_keep = jnp.concatenate([lower_ok[:, None] & full_rows, full_rows, upper_ok[:, None] & full_rows], 1)
    scores = jnp.where(key_keep[:, None, None, :], scores, masked_low)
    attn_probs = low(jax.nn.softmax(scores, -1))
    attended = jnp.einsum('ghqk,gkhe->gqhe', attn_probs, value_heads, precision=highest)
    attended = low(low_back(attended.reshape(-1, features)))
    residual = flat_rows + low_back(jnp.dot(attended, w_out, precision=highest) + out_bias)
    normed_two = low(layer_norm(residual, mid_gain, mid_bias))
    hidden = low_back(jnp.dot(normed_two, w_up, precision=highest) + up_bias)
    activated = low(jax.nn.gelu(hidden, approximate=False))
    layer_sum = residual + low_back(jnp.dot(activated, w_down, precision=highest) + down_bias)
    row_keep = jnp.repeat(occupied, spatial)[:, None]
    return jnp.where(row_keep, layer_sum, flat_rows).reshape(inputs.shape)

def reference(tokens, cotangent, lane_frames, pre_gain, pre_bias, w_project, query_bias, value_bias, w_out, out_bias, mid_gain, mid_bias, w_up, up_bias, w_down, down_bias):
    params = tuple((weight.astype(jnp.float32) for weight in (pre_gain, pre_bias, w_project, query_bias, value_bias, w_out, out_bias, mid_gain, mid_bias, w_up, up_bias, w_down, down_bias)))
    block_count = LANES_ALL // 4

    def by_blocks(source):
        arranged = source.astype(jnp.float32).reshape(N_TM, block_count, 4, SPATIAL, D)
        return jnp.transpose(arranged, (1, 2, 0, 3, 4)).reshape(block_count, 4 * N_TM, SPATIAL, D)

    def unblock(source):
        arranged = source.reshape(block_count, 4, N_TM, SPATIAL, D)
        return jnp.transpose(arranged, (2, 0, 1, 3, 4)).reshape(N_TM, LANES_ALL, SPATIAL, D).astype(jnp.bfloat16)
    tm_index = jnp.arange(N_TM, dtype=jnp.int32)[None, :]
    lane_span = jnp.maximum(lane_frames // (2 * N_TM), 1)[:, None]
    lane_offset = jnp.arange(LANES_ALL, dtype=jnp.int32)[:, None] % lane_span
    occupied = (lane_frames > 0)[:, None] & (tm_index >= 0)
    has_lower = occupied & ((tm_index > 0) | (lane_offset > 0))
    has_upper = occupied & ((tm_index < N_TM - 1) | (lane_offset < lane_span - 1))
    zero_grads = jax.tree.map(jnp.zeros_like, params)

    def scan_step(summed, pieces):
        inputs, cotangents, lower_ok, upper_ok, filled = pieces
        block_out, backward = jax.vjp(lambda weights, block: block_layer(weights, block, lower_ok, upper_ok, filled), params, inputs)
        grad_params, grad_inputs = backward(cotangents)
        return (jax.tree.map(jnp.add, summed, grad_params), (block_out, grad_inputs))
    grad_sums, (outputs, grad_inputs) = lax.scan(scan_step, zero_grads, (by_blocks(tokens), by_blocks(cotangent), has_lower.reshape(block_count, 4 * N_TM), has_upper.reshape(block_count, 4 * N_TM), occupied.reshape(block_count, 4 * N_TM)))
    return (unblock(outputs), unblock(grad_inputs), grad_sums[0], grad_sums[1], grad_sums[2], grad_sums[3], grad_sums[4], grad_sums[5], grad_sums[6], grad_sums[7], grad_sums[8], grad_sums[9], grad_sums[10], grad_sums[11], grad_sums[12])
```

```python
import functools

import jax
import jax.numpy as jnp
from jax import lax
from jax.experimental import pallas as pl
from jax.experimental.pallas import tpu as pltpu
from jax.sharding import PartitionSpec as P

HEAD_DIM = 64
GROUP = 4
EPSILON = 1e-06
FAR = 1e30
F32 = jnp.float32
BF16 = jnp.bfloat16
NN = (((1,), (0,)), ((), ()))
NT = (((1,), (1,)), ((), ()))
TN = (((0,), (0,)), ((), ()))


def dot(a, b, dims=NN):
    return lax.dot_general(a, b, dims, preferred_element_type=F32)


def row_mean(value):
    return jnp.sum(value, -1, keepdims=True) * (1.0 / value.shape[-1])


def normalise(x):
    center = x - row_mean(x)
    rate = lax.rsqrt(row_mean(center * center) + EPSILON)
    return center * rate, rate


def norm_back(grad, xhat, rate, gain):
    e = grad * gain
    return rate * (e - row_mean(e) - xhat * row_mean(e * xhat))


def gelu_parts(h):
    bell = jnp.exp(-0.5 * (h * h))
    t = 1.0 / (1.0 + 0.23164190 * jnp.abs(h))
    poly = t * (0.127414796 + t * (-0.142248368 + t * (0.7107068705 + t * (-0.7265760135 + t * 0.5307027145))))
    tail = poly * bell
    phi = jnp.where(h >= 0.0, 1.0 - tail, tail)
    return h * phi, phi + h * (bell * 0.3989422804014327)


def column_sum(value):
    return jnp.sum(value, 0, keepdims=True)


def block_kernel(
    first, spatial, features, hidden, tm_count,
    tm_ref, low_ok_ref, up_ok_ref, full_ref,
    tok_ref, low_ref, low_wrap_ref, up_ref, up_wrap_ref, cot_ref,
    pre_gain_ref, pre_bias_ref, wq_t_ref, w_project_ref, query_bias_ref, value_bias_ref,
    w_out_ref, out_bias_ref, mid_gain_ref, mid_bias_ref, w_up_ref, up_bias_ref, w_down_ref, down_bias_ref,
    *rest,
):
    count = 6
    if first:
        olds = (None,) * count
        rest = rest[0:]
    else:
        olds = rest[:count]
        rest = rest[count + 2 :]
    (out_ref, own_ref, gl_ref, gu_ref, a_project, a_out, a_up, a_down, a_small, a_upb) = rest[:10]
    (n1_s, k_s, v_s, kt_s, vt_s, qt_s, p_s, inv_s, att_s, attt_s, res_s, n2_s, act_s, gh_s, dao_s, dres_s, dq_s, dkv_s, dt_s) = rest[10:]
    f = features
    pad = n1_s.shape[1] // GROUP
    heads = f // HEAD_DIM
    tm = tm_ref[0]
    at_low, at_high = tm == 0, tm == tm_count - 1
    pre_gain, pre_bias = pre_gain_ref[...], pre_bias_ref[...]
    mid_gain, mid_bias = mid_gain_ref[...], mid_bias_ref[...]

    for old, new in zip(olds, (a_project, a_out, a_up, a_down, a_small, a_upb)):
        if old is None:
            new[...] = jnp.zeros_like(new)
        else:
            new[...] = old[...]

    def neighbour_rows(j):
        below = jnp.where(at_low, low_wrap_ref[0, jnp.maximum(j - 1, 0)].astype(F32), low_ref[0, j].astype(F32))
        above = jnp.where(at_high, up_wrap_ref[0, jnp.minimum(j, GROUP - 2)].astype(F32), up_ref[0, j].astype(F32))
        return below, above

    def rows_of(j):
        return pl.ds(pl.multiple_of(j * pad, pad), spatial)

    for ref in (n1_s, att_s, dao_s, dq_s, dkv_s, res_s, dres_s):
        for j in range(GROUP):
            if len(ref.shape) == 3:
                ref[:, pl.ds(j * pad + pad - 16, 16), :] = jnp.zeros((ref.shape[0], 16, ref.shape[2]), ref.dtype)
            else:
                ref[pl.ds(j * pad + pad - 16, 16), :] = jnp.zeros((16, ref.shape[1]), ref.dtype)

    def forward(j, carry):
        below, above = neighbour_rows(j)
        for s, x in enumerate((below, tok_ref[0, j].astype(F32), above)):
            xhat, _ = normalise(x)
            n1 = (xhat * pre_gain + pre_bias).astype(BF16)
            n1_s[s, rows_of(j), :] = n1
            kv = dot(n1, w_project_ref[:, f:])
            k = kv[:, :f].astype(BF16)
            v = (kv[:, f:] + value_bias_ref[...]).astype(BF16)
            k_s[s, j] = k
            v_s[s, j] = v
            kt_s[s, j] = k.T
            vt_s[s, j] = v.T
            if s == 1:
                qt = (dot(wq_t_ref[...], n1, NT) + query_bias_ref[...]).astype(BF16)
                qt_s[j] = qt * jnp.asarray(HEAD_DIM ** (-0.5), BF16)
        low_ok, up_ok = low_ok_ref[j] > 0, up_ok_ref[j] > 0
        low_far, up_far = jnp.where(low_ok, 0.0, FAR), jnp.where(up_ok, 0.0, FAR)
        zero_half = jnp.zeros((HEAD_DIM, spatial), BF16)
        for h in range(heads):
            pair = slice(h // 2 * 2 * HEAD_DIM, (h // 2 + 1) * 2 * HEAD_DIM)
            mine = slice(h * HEAD_DIM, (h + 1) * HEAD_DIM)
            qh = qt_s[j, mine, :]
            qz = jnp.concatenate([qh, zero_half] if h % 2 == 0 else [zero_half, qh], 0)
            scores = [dot(k_s[s, j, :, pair], qz) for s in range(3)]
            tops = [jnp.max(x, 0, keepdims=True) for x in scores]
            top = jnp.maximum(jnp.maximum(tops[0] - low_far, tops[2] - up_far), tops[1])
            total, attended = None, None
            for s, shift in enumerate((top + low_far, top, top + up_far)):
                prob = jnp.exp(scores[s] - shift)
                part = column_sum(prob)
                total = part if total is None else total + part
                low_prob = prob.astype(BF16)
                p_s[j, h, s] = low_prob
                got = dot(vt_s[s, j, mine, :], low_prob)
                attended = got if attended is None else attended + got
            inverse = 1.0 / total
            inv_s[j, h : h + 1, :] = inverse
            attt_s[j, mine, :] = (attended * inverse).astype(BF16)
        att_s[rows_of(j), :] = attt_s[j].T
        res_s[rows_of(j), :] = tok_ref[0, j].astype(F32)
        return carry

    lax.fori_loop(0, GROUP, forward, 0)

    residual = res_s[...] + dot(att_s[...], w_out_ref[...]) + out_bias_ref[...]
    res_s[...] = residual
    xhat2, rate2 = normalise(residual)
    n2_s[...] = (xhat2 * mid_gain + mid_bias).astype(BF16)
    for j in range(GROUP):
        full = full_ref[j] > 0
        g = cot_ref[0, j]
        dao_s[pl.ds(j * pad, spatial), :] = jnp.where(full, g.astype(F32), 0.0).astype(BF16)

    wide = 256

    def mlp(c, carry):
        cols = pl.ds(pl.multiple_of(c * wide, wide), wide)
        h = dot(n2_s[...], w_up_ref[:, cols]) + up_bias_ref[:, cols]
        act, slope = gelu_parts(h)
        act_s[:, cols] = act.astype(BF16)
        gh = (dot(dao_s[...], w_down_ref[cols, :], NT) * slope).astype(BF16)
        gh_s[:, cols] = gh
        a_upb[:, cols] += column_sum(gh.astype(F32))
        return carry

    lax.fori_loop(0, hidden // wide, mlp, 0)
    a_up[...] += dot(n2_s[...], gh_s[...], TN)
    a_down[...] += dot(dao_s[...], act_s[...], TN)
    total_out = dot(act_s[...], w_down_ref[...]) + down_bias_ref[...] + res_s[...]
    grad_n2 = dot(gh_s[...], w_up_ref[...], NT)
    for j in range(GROUP):
        full = full_ref[j] > 0
        mine = total_out[j * pad : j * pad + spatial]
        out_ref[0, j] = jnp.where(full, mine, tok_ref[0, j].astype(F32)).astype(BF16)
    g = dao_s[...].astype(F32)
    xhat2, rate2 = normalise(res_s[...])
    dres = g + norm_back(grad_n2, xhat2, rate2, mid_gain)
    dres_s[...] = dres
    dao = dres.astype(BF16)
    dao_s[...] = dao
    a_small[3:4, :] += column_sum(dao.astype(F32))
    a_small[4:5, :] += column_sum(grad_n2 * xhat2)
    a_small[5:6, :] += column_sum(grad_n2)
    a_small[6:7, :] += column_sum(g)
    a_out[...] += dot(att_s[...], dao, TN)

    def backward(j, carry):
        dot_rows = dao_s[rows_of(j), :]
        dt = dot(w_out_ref[...], dot_rows, NT).astype(BF16)
        zero_half = jnp.zeros((HEAD_DIM, spatial), BF16)
        for h in range(heads):
            pair = slice(h // 2 * 2 * HEAD_DIM, (h // 2 + 1) * 2 * HEAD_DIM)
            mine = slice(h * HEAD_DIM, (h + 1) * HEAD_DIM)
            dh = dt[mine, :].astype(F32) * inv_s[j, h : h + 1, :]
            delta = column_sum(dh * attt_s[j, mine, :].astype(F32))
            dh = dh.astype(BF16)
            dz = jnp.concatenate([dh, zero_half] if h % 2 == 0 else [zero_half, dh], 0)
            qh = qt_s[j, mine, :]
            grad_q = None
            for s in range(3):
                prob = p_s[j, h, s]
                grad_prob = dot(v_s[s, j, :, pair], dz)
                grad_score = (prob.astype(F32) * (grad_prob - delta)).astype(BF16)
                dt_s[1 + s, mine, :] = dot(qh, grad_score, NT).astype(BF16)
                dt_s[4 + s, mine, :] = dot(dh, prob, NT).astype(BF16)
                got = dot(kt_s[s, j, mine, :], grad_score)
                grad_q = got if grad_q is None else grad_q + got
            dt_s[0, mine, :] = (grad_q * HEAD_DIM ** (-0.5)).astype(BF16)
        dq_s[rows_of(j), :] = dt_s[0].T
        for s in range(3):
            dkv_s[s, rows_of(j), :f] = dt_s[1 + s].T
            dkv_s[s, rows_of(j), f:] = dt_s[4 + s].T
        return carry

    lax.fori_loop(0, GROUP, backward, 0)

    dq = dq_s[...]
    a_project[:, :f] += dot(n1_s[1], dq, TN)
    a_small[2:3, :] += column_sum(dq.astype(F32))
    for s in range(3):
        dkv = dkv_s[s]
        a_project[:, f:] += dot(n1_s[s], dkv, TN)
        a_small[7:8, :] += column_sum(dkv[:, f:].astype(F32))

    def finish(j, carry):
        below, above = neighbour_rows(j)
        for s, x in enumerate((below, tok_ref[0, j].astype(F32), above)):
            grad = dot(dkv_s[s, rows_of(j), :], w_project_ref[:, f:], NT)
            if s == 1:
                grad += dot(dq_s[rows_of(j), :], w_project_ref[:, :f], NT)
            xhat, rate = normalise(x)
            a_small[0:1, :] += column_sum(grad * xhat)
            a_small[1:2, :] += column_sum(grad)
            back = norm_back(grad, xhat, rate, pre_gain)
            if s == 1:
                straight = jnp.where(full_ref[j] > 0, 0.0, cot_ref[0, j].astype(F32))
                own_ref[0, j] = (back + dres_s[rows_of(j), :] + straight).astype(BF16)
            else:
                (gl_ref if s == 0 else gu_ref)[0, j] = back.astype(BF16)
        return carry

    lax.fori_loop(0, GROUP, finish, 0)


def block_call(c, lanes, spatial, features, hidden, tm_count, scalars, streams, weights, previous):
    first = previous is None
    f = features
    pad = -(-spatial // 16) * 16
    rows = GROUP * pad
    smem = pl.BlockSpec(memory_space=pltpu.SMEM)
    vmem = pl.BlockSpec(memory_space=pltpu.VMEM)
    block = pl.BlockSpec((1, GROUP, spatial, f), lambda i: (0, c, 0, 0))
    whole = pl.BlockSpec((1, GROUP, spatial, f), lambda i: (0, 0, 0, 0))
    wrap = pl.BlockSpec((1, GROUP - 1, spatial, f), lambda i: (0, 0, 0, 0))
    in_specs = [smem] * 4 + [block, whole, wrap, whole, wrap, block] + [vmem] * len(weights)
    accumulators = [(f, 3 * f), (f, f), (f, hidden), (f, hidden), (8, f), (1, hidden)]
    out_shape = (
        [jax.ShapeDtypeStruct((1, lanes, spatial, f), BF16)] * 2
        + [jax.ShapeDtypeStruct((1, GROUP, spatial, f), BF16)] * 2
        + [jax.ShapeDtypeStruct(s, F32) for s in accumulators]
    )
    out_specs = [block, block, whole, whole] + [vmem] * len(accumulators)
    operands = list(scalars) + list(streams) + list(weights)
    aliases = {}
    if not first:
        base = len(operands)
        operands += list(previous)
        in_specs += [vmem] * len(accumulators) + [pl.BlockSpec(memory_space=pl.ANY)] * 2
        aliases = {base + i: 4 + i for i in range(len(accumulators))}
        aliases[base + len(accumulators)] = 0
        aliases[base + len(accumulators) + 1] = 1
    lane = lambda *s: pltpu.VMEM(s, BF16)
    scratch = [
        lane(3, rows, f), lane(3, GROUP, spatial, f), lane(3, GROUP, spatial, f),
        lane(3, GROUP, f, spatial), lane(3, GROUP, f, spatial), lane(GROUP, f, spatial),
        lane(GROUP, f // HEAD_DIM, 3, spatial, spatial), pltpu.VMEM((GROUP, 8, spatial), F32),
        lane(rows, f), lane(GROUP, f, spatial), pltpu.VMEM((rows, f), F32), lane(rows, f),
        lane(rows, hidden), lane(rows, hidden), lane(rows, f), pltpu.VMEM((rows, f), F32),
        lane(rows, f), lane(3, rows, 2 * f), lane(7, f, spatial),
    ]
    return pl.pallas_call(
        functools.partial(block_kernel, first, spatial, f, hidden, tm_count),
        grid=(1,),
        in_specs=in_specs,
        out_specs=out_specs,
        out_shape=out_shape,
        scratch_shapes=scratch,
        input_output_aliases=aliases,
        name="layer_block",
        compiler_params=pltpu.CompilerParams(vmem_limit_bytes=63 * 1024 * 1024),
        cost_estimate=pl.CostEstimate(flops=25 * 10**9, bytes_accessed=20 * 10**6, transcendentals=0),
    )(*operands)


def body(
    tokens, cotangent, lane_frames, pre_gain, pre_bias, w_project, query_bias, value_bias,
    w_out, out_bias, mid_gain, mid_bias, w_up, up_bias, w_down, down_bias,
):
    lanes, spatial, f = tokens.shape[1:]
    hidden = w_up.shape[1]
    tm_count = lax.axis_size("tm")
    tm_index = lax.axis_index("tm")
    lane_span = jnp.maximum(lane_frames // (2 * tm_count), 1)
    lane_offset = jnp.arange(lanes, dtype=jnp.int32) % lane_span
    occupied = lane_frames > 0
    low_ok = (occupied & ((tm_index > 0) | (lane_offset > 0))).astype(jnp.int32)
    up_ok = (occupied & ((tm_index < tm_count - 1) | (lane_offset < lane_span - 1))).astype(jnp.int32)
    full = occupied.astype(jnp.int32)
    tm_arr = tm_index.astype(jnp.int32).reshape(1)
    row = lambda v: v.astype(F32).reshape(1, -1)
    weights = (
        row(pre_gain), row(pre_bias), w_project[:, :f].T, w_project,
        query_bias.astype(F32).reshape(-1, 1), row(value_bias), w_out, row(out_bias),
        row(mid_gain), row(mid_bias), w_up, row(up_bias), w_down, row(down_bias),
    )
    last = tm_count - 1
    rising = [(i, i + 1) for i in range(last)]
    falling = [(i + 1, i) for i in range(last)]
    round_up, round_down = [(last, 0)], [(0, last)]
    send = lambda v, pairs: lax.ppermute(v, "tm", pairs)

    blocks = lanes // GROUP
    streams = []
    token = None
    for c in range(blocks):
        mine = tokens[:, c * GROUP : (c + 1) * GROUP]
        if token is not None:
            mine, _ = lax.optimization_barrier((mine, token))
        low = send(mine, rising)
        up = send(mine, falling)
        low_wrap = send(mine[:, : GROUP - 1], round_up)
        up_wrap = send(mine[:, 1:], round_down)
        streams.append((low, low_wrap, up, up_wrap))
        token = (low, low_wrap, up, up_wrap)

    previous, returned = None, []
    for c in range(blocks):
        lane = slice(c * GROUP, (c + 1) * GROUP)
        low, low_wrap, up, up_wrap = streams[c]
        got = block_call(
            c, lanes, spatial, f, hidden, tm_count, (tm_arr, low_ok[lane], up_ok[lane], full[lane]),
            (tokens, low, low_wrap, up, up_wrap, cotangent), weights, previous,
        )
        out, own, gl, gu = got[:4]
        previous = tuple(got[4:]) + (out, own)
        from_above = send(gl, falling)
        from_above_wrap = send(gl[:, 1:], round_down)
        from_below = send(gu, rising)
        from_below_wrap = send(gu[:, : GROUP - 1], round_up)
        returned.append((from_above, from_above_wrap, from_below, from_below_wrap))

    g_project, g_out, g_up, g_down, g_small, g_upb = previous[:6]
    pieces = [g_project.reshape(-1, f), g_out, g_up.reshape(-1, f), g_down.reshape(-1, f), g_small, g_upb.reshape(-1, f)]
    sizes = [p.shape[0] for p in pieces]
    packed = jnp.concatenate(pieces, 0).astype(BF16)
    packed = lax.psum(packed, ("tm", "clip")).astype(F32)
    parts, at = [], 0
    for n in sizes:
        parts.append(packed[at : at + n])
        at += n
    g_project, g_out, g_up, g_down, g_small, g_upb = parts
    g_project = g_project.reshape(f, 3 * f)
    g_up = g_up.reshape(f, hidden)
    g_down = g_down.reshape(f, hidden).T
    g_upb = g_upb.reshape(hidden)

    received = []
    for above, above_wrap, below, below_wrap in returned:
        one = jnp.zeros_like(above_wrap[:, :1])
        received.append(
            above.astype(F32) + below.astype(F32)
            + jnp.concatenate([above_wrap, one], 1).astype(F32)
            + jnp.concatenate([one, below_wrap], 1).astype(F32)
        )
    input_grad = (own.astype(F32) + jnp.concatenate(received, 1)).astype(BF16)
    return (
        out, input_grad, g_small[0], g_small[1], g_project, g_small[2], g_small[7], g_out, g_small[3],
        g_small[4], g_small[5], g_up, g_upb, g_down, g_small[6],
    )


def solution(mesh):
    spread = P("tm", "clip", None, None)
    return jax.shard_map(
        body,
        mesh=mesh,
        in_specs=(spread, spread, P("clip")) + (P(),) * 13,
        out_specs=(spread, spread) + (P(),) * 13,
        check_vma=False,
    )
```

```python
import functools

import jax
import jax.numpy as jnp
from jax import lax
from jax.experimental import pallas as pl
from jax.experimental.pallas import tpu as pltpu
from jax.sharding import PartitionSpec as P

HEAD_DIM = 64
GROUP = 2
WRAP = 4
MESH = pl.DeviceIdType.MESH
EPSILON = 1e-06
FAR = 1e30
F32 = jnp.float32
BF16 = jnp.bfloat16
NN = (((1,), (0,)), ((), ()))
NT = (((1,), (1,)), ((), ()))
TN = (((0,), (0,)), ((), ()))


def dot(a, b, dims=NN):
    return lax.dot_general(a, b, dims, preferred_element_type=F32)


def row_mean(value):
    return jnp.sum(value, -1, keepdims=True) * (1.0 / value.shape[-1])


def normalise(x):
    center = x - row_mean(x)
    rate = lax.rsqrt(row_mean(center * center) + EPSILON)
    return center * rate, rate


def norm_back(grad, xhat, rate, gain):
    e = grad * gain
    return rate * (e - row_mean(e) - xhat * row_mean(e * xhat))


def gelu_parts(h):
    bell = jnp.exp(-0.5 * (h * h))
    t = 1.0 / (1.0 + 0.23164190 * jnp.abs(h))
    poly = t * (0.127414796 + t * (-0.142248368 + t * (0.7107068705 + t * (-0.7265760135 + t * 0.5307027145))))
    tail = poly * bell
    phi = jnp.where(h >= 0.0, 1.0 - tail, tail)
    return h * phi, phi + h * (bell * 0.3989422804014327)


def column_sum(value):
    return jnp.sum(value, 0, keepdims=True)


def layer_kernel(
    lanes, spatial, features, hidden, tm_count,
    low_ok_ref, up_ok_ref, full_ref, tok_hbm, tok_ref, cot_ref,
    pre_gain_ref, pre_bias_ref, wq_t_ref, w_project_ref, query_bias_ref, value_bias_ref,
    w_out_ref, out_bias_ref, mid_gain_ref, mid_bias_ref, w_up_ref, up_bias_ref, w_down_ref, down_bias_ref,
    out_ref, own_ref, above_ref, below_ref, a_project, a_out, a_up, a_down, a_small, a_upb,
    low_s, up_s, gl_s, gu_s, n1_s, k_s, v_s, kt_s, vt_s, qt_s, p_s, inv_s, att_s, attt_s, res_s, n2_s, act_s, gh_s,
    dao_s, dres_s, dq_s, dkv_s, dt_s,
    send_up, send_down, recv_low, recv_up, send_gl, send_gu, recv_above, recv_below,
):
    f = features
    pad = n1_s.shape[1] // GROUP
    heads = f // HEAD_DIM
    tm = lax.axis_index("tm")
    last = tm_count - 1
    at_low, at_high = tm == 0, tm == last
    higher, lower = lax.rem(tm + 1, tm_count), lax.rem(tm + last, tm_count)
    step_up, step_down = (tm + 1) // tm_count, (tm_count - tm) // tm_count
    pre_gain, pre_bias = pre_gain_ref[...], pre_bias_ref[...]
    mid_gain, mid_bias = mid_gain_ref[...], mid_bias_ref[...]

    def has_low(l):
        return jnp.logical_or(tm > 0, lax.rem(l, WRAP) != 0)

    def has_up(l):
        return jnp.logical_or(tm < last, lax.rem(l, WRAP) != WRAP - 1)

    def copy(src, dst, send, recv, device):
        return pltpu.make_async_remote_copy(
            src_ref=src, dst_ref=dst, send_sem=send, recv_sem=recv, device_id={"tm": device}, device_id_type=MESH
        )

    def rising(l):
        return copy(tok_hbm.at[0, l], low_s.at[l + step_up], send_up.at[l], recv_low.at[l + step_up], higher)

    def falling(l):
        return copy(tok_hbm.at[0, l], up_s.at[l - step_down], send_down.at[l], recv_up.at[l - step_down], lower)

    def returning_low(l):
        return copy(gl_s.at[l], above_ref.at[0, l - step_down], send_gl.at[l], recv_above.at[l - step_down], lower)

    def returning_up(l):
        return copy(gu_s.at[l], below_ref.at[0, l + step_up], send_gu.at[l], recv_below.at[l + step_up], higher)

    barrier = pltpu.get_barrier_semaphore()
    for device in (lower, higher):
        pl.semaphore_signal(barrier, inc=1, device_id={"tm": device}, device_id_type=MESH)
    pl.semaphore_wait(barrier, 2)

    def start_tokens(l, carry):
        pl.when(has_up(l))(lambda: rising(l).start())
        pl.when(has_low(l))(lambda: falling(l).start())
        return carry

    lax.fori_loop(0, lanes, start_tokens, 0)

    def fill(l, carry):
        @pl.when(jnp.logical_not(has_low(l)))
        def _():
            low_s[l] = jnp.zeros(low_s.shape[1:], BF16)

        @pl.when(jnp.logical_not(has_up(l)))
        def _():
            up_s[l] = jnp.zeros(up_s.shape[1:], BF16)

        return carry

    lax.fori_loop(0, lanes, fill, 0)

    for new in (a_project, a_out, a_up, a_down, a_small, a_upb):
        new[...] = jnp.zeros_like(new)

    def rows_of(j):
        return pl.ds(pl.multiple_of(j * pad, pad), spatial)

    for ref in (n1_s, att_s, dao_s, dq_s, dkv_s, res_s, dres_s):
        for j in range(GROUP):
            if len(ref.shape) == 3:
                ref[:, pl.ds(j * pad + pad - 16, 16), :] = jnp.zeros((ref.shape[0], 16, ref.shape[2]), ref.dtype)
            else:
                ref[pl.ds(j * pad + pad - 16, 16), :] = jnp.zeros((16, ref.shape[1]), ref.dtype)

    def group(g, carry):
        base = g * GROUP

        def arrive(j, carry):
            l = base + j
            pl.when(has_low(l))(lambda: copy(tok_hbm.at[0, l], low_s.at[l], send_up.at[l], recv_low.at[l], lower).wait_recv())
            pl.when(has_up(l))(lambda: copy(tok_hbm.at[0, l], up_s.at[l], send_down.at[l], recv_up.at[l], higher).wait_recv())
            return carry

        lax.fori_loop(0, GROUP, arrive, 0)

        def forward(j, carry):
            below, above = low_s[base + j].astype(F32), up_s[base + j].astype(F32)
            for s, x in enumerate((below, tok_ref[0, base + j].astype(F32), above)):
                xhat, _ = normalise(x)
                n1 = (xhat * pre_gain + pre_bias).astype(BF16)
                n1_s[s, rows_of(j), :] = n1
                kv = dot(n1, w_project_ref[:, f:])
                k = kv[:, :f].astype(BF16)
                v = (kv[:, f:] + value_bias_ref[...]).astype(BF16)
                k_s[s, j] = k
                v_s[s, j] = v
                kt_s[s, j] = k.T
                vt_s[s, j] = v.T
                if s == 1:
                    qt = (dot(wq_t_ref[...], n1, NT) + query_bias_ref[...]).astype(BF16)
                    qt_s[j] = qt * jnp.asarray(HEAD_DIM ** (-0.5), BF16)
            low_ok, up_ok = low_ok_ref[base + j] > 0, up_ok_ref[base + j] > 0
            low_far, up_far = jnp.where(low_ok, 0.0, FAR), jnp.where(up_ok, 0.0, FAR)
            zero_half = jnp.zeros((HEAD_DIM, spatial), BF16)
            for h in range(heads):
                pair = slice(h // 2 * 2 * HEAD_DIM, (h // 2 + 1) * 2 * HEAD_DIM)
                mine = slice(h * HEAD_DIM, (h + 1) * HEAD_DIM)
                qh = qt_s[j, mine, :]
                qz = jnp.concatenate([qh, zero_half] if h % 2 == 0 else [zero_half, qh], 0)
                scores = [dot(k_s[s, j, :, pair], qz) for s in range(3)]
                tops = [jnp.max(x, 0, keepdims=True) for x in scores]
                top = jnp.maximum(jnp.maximum(tops[0] - low_far, tops[2] - up_far), tops[1])
                total, attended = None, None
                for s, shift in enumerate((top + low_far, top, top + up_far)):
                    prob = jnp.exp(scores[s] - shift)
                    part = column_sum(prob)
                    total = part if total is None else total + part
                    low_prob = prob.astype(BF16)
                    p_s[j, h, s] = low_prob
                    got = dot(vt_s[s, j, mine, :], low_prob)
                    attended = got if attended is None else attended + got
                inverse = 1.0 / total
                inv_s[j, h : h + 1, :] = inverse
                attt_s[j, mine, :] = (attended * inverse).astype(BF16)
            att_s[rows_of(j), :] = attt_s[j].T
            res_s[rows_of(j), :] = tok_ref[0, base + j].astype(F32)
            return carry

        lax.fori_loop(0, GROUP, forward, 0)

        residual = res_s[...] + dot(att_s[...], w_out_ref[...]) + out_bias_ref[...]
        res_s[...] = residual
        xhat2, rate2 = normalise(residual)
        n2_s[...] = (xhat2 * mid_gain + mid_bias).astype(BF16)
        for j in range(GROUP):
            full = full_ref[base + j] > 0
            g = cot_ref[0, base + j]
            dao_s[pl.ds(j * pad, spatial), :] = jnp.where(full, g.astype(F32), 0.0).astype(BF16)

        wide = 256

        def mlp(c, carry):
            cols = pl.ds(pl.multiple_of(c * wide, wide), wide)
            h = dot(n2_s[...], w_up_ref[:, cols]) + up_bias_ref[:, cols]
            act, slope = gelu_parts(h)
            act_s[:, cols] = act.astype(BF16)
            gh = (dot(dao_s[...], w_down_ref[cols, :], NT) * slope).astype(BF16)
            gh_s[:, cols] = gh
            a_upb[:, cols] += column_sum(gh.astype(F32))
            return carry

        lax.fori_loop(0, hidden // wide, mlp, 0)
        a_up[...] += dot(n2_s[...], gh_s[...], TN)
        a_down[...] += dot(dao_s[...], act_s[...], TN)
        total_out = dot(act_s[...], w_down_ref[...]) + down_bias_ref[...] + res_s[...]
        grad_n2 = dot(gh_s[...], w_up_ref[...], NT)
        for j in range(GROUP):
            full = full_ref[base + j] > 0
            mine = total_out[j * pad : j * pad + spatial]
            out_ref[0, base + j] = jnp.where(full, mine, tok_ref[0, base + j].astype(F32)).astype(BF16)
        g = dao_s[...].astype(F32)
        xhat2, rate2 = normalise(res_s[...])
        dres = g + norm_back(grad_n2, xhat2, rate2, mid_gain)
        dres_s[...] = dres
        dao = dres.astype(BF16)
        dao_s[...] = dao
        a_small[3:4, :] += column_sum(dao.astype(F32))
        a_small[4:5, :] += column_sum(grad_n2 * xhat2)
        a_small[5:6, :] += column_sum(grad_n2)
        a_small[6:7, :] += column_sum(g)
        a_out[...] += dot(att_s[...], dao, TN)

        def backward(j, carry):
            dot_rows = dao_s[rows_of(j), :]
            dt = dot(w_out_ref[...], dot_rows, NT).astype(BF16)
            zero_half = jnp.zeros((HEAD_DIM, spatial), BF16)
            for h in range(heads):
                pair = slice(h // 2 * 2 * HEAD_DIM, (h // 2 + 1) * 2 * HEAD_DIM)
                mine = slice(h * HEAD_DIM, (h + 1) * HEAD_DIM)
                dh = dt[mine, :].astype(F32) * inv_s[j, h : h + 1, :]
                delta = column_sum(dh * attt_s[j, mine, :].astype(F32))
                dh = dh.astype(BF16)
                dz = jnp.concatenate([dh, zero_half] if h % 2 == 0 else [zero_half, dh], 0)
                qh = qt_s[j, mine, :]
                grad_q = None
                for s in range(3):
                    prob = p_s[j, h, s]
                    grad_prob = dot(v_s[s, j, :, pair], dz)
                    grad_score = (prob.astype(F32) * (grad_prob - delta)).astype(BF16)
                    dt_s[1 + s, mine, :] = dot(qh, grad_score, NT).astype(BF16)
                    dt_s[4 + s, mine, :] = dot(dh, prob, NT).astype(BF16)
                    got = dot(kt_s[s, j, mine, :], grad_score)
                    grad_q = got if grad_q is None else grad_q + got
                dt_s[0, mine, :] = (grad_q * HEAD_DIM ** (-0.5)).astype(BF16)
            dq_s[rows_of(j), :] = dt_s[0].T
            for s in range(3):
                dkv_s[s, rows_of(j), :f] = dt_s[1 + s].T
                dkv_s[s, rows_of(j), f:] = dt_s[4 + s].T
            return carry

        lax.fori_loop(0, GROUP, backward, 0)

        dq = dq_s[...]
        a_project[:, :f] += dot(n1_s[1], dq, TN)
        a_small[2:3, :] += column_sum(dq.astype(F32))
        for s in range(3):
            dkv = dkv_s[s]
            a_project[:, f:] += dot(n1_s[s], dkv, TN)
            a_small[7:8, :] += column_sum(dkv[:, f:].astype(F32))

        def finish(j, carry):
            below, above = low_s[base + j].astype(F32), up_s[base + j].astype(F32)
            for s, x in enumerate((below, tok_ref[0, base + j].astype(F32), above)):
                grad = dot(dkv_s[s, rows_of(j), :], w_project_ref[:, f:], NT)
                if s == 1:
                    grad += dot(dq_s[rows_of(j), :], w_project_ref[:, :f], NT)
                xhat, rate = normalise(x)
                a_small[0:1, :] += column_sum(grad * xhat)
                a_small[1:2, :] += column_sum(grad)
                back = norm_back(grad, xhat, rate, pre_gain)
                if s == 1:
                    straight = jnp.where(full_ref[base + j] > 0, 0.0, cot_ref[0, base + j].astype(F32))
                    own_ref[0, base + j] = (back + dres_s[rows_of(j), :] + straight).astype(BF16)
                else:
                    (gl_s if s == 0 else gu_s)[base + j] = back.astype(BF16)
            return carry

        lax.fori_loop(0, GROUP, finish, 0)

        def give_back(j, carry):
            l = base + j
            pl.when(has_low(l))(lambda: returning_low(l).start())
            pl.when(has_up(l))(lambda: returning_up(l).start())
            return carry

        lax.fori_loop(0, GROUP, give_back, 0)
        return carry

    lax.fori_loop(0, lanes // GROUP, group, 0)

    def settle(l, carry):
        @pl.when(has_up(l))
        def _():
            rising(l).wait_send()
            returning_up(l).wait_send()
            copy(gl_s.at[l], above_ref.at[0, l], send_gl.at[l], recv_above.at[l], higher).wait_recv()

        @pl.when(has_low(l))
        def _():
            falling(l).wait_send()
            returning_low(l).wait_send()
            copy(gu_s.at[l], below_ref.at[0, l], send_gu.at[l], recv_below.at[l], lower).wait_recv()

        return carry

    lax.fori_loop(0, lanes, settle, 0)


def finish_kernel(tm_ref, own_ref, above_ref, below_ref, out_ref):
    i = pl.program_id(0)
    tm, last = tm_ref[0], tm_ref[1]
    lane = lax.rem(i, WRAP)
    has_above = jnp.logical_or(tm < last, lane != WRAP - 1)
    has_below = jnp.logical_or(tm > 0, lane != 0)
    total = own_ref[...].astype(F32)
    total += jnp.where(has_above, above_ref[...].astype(F32), 0.0)
    total += jnp.where(has_below, below_ref[...].astype(F32), 0.0)
    out_ref[...] = total.astype(BF16)


def layer_call(lanes, spatial, f, hidden, tm_count, scalars, tokens, cotangent, weights):
    pad = -(-spatial // 16) * 16
    rows = GROUP * pad
    smem = pl.BlockSpec(memory_space=pltpu.SMEM)
    vmem = pl.BlockSpec(memory_space=pltpu.VMEM)
    hbm = pl.BlockSpec(memory_space=pl.ANY)
    accumulators = [(f, 3 * f), (f, f), (f, hidden), (f, hidden), (8, f), (1, hidden)]
    whole = jax.ShapeDtypeStruct((1, lanes, spatial, f), BF16)
    lane = lambda *s: pltpu.VMEM(s, BF16)
    dma = pltpu.SemaphoreType.DMA((lanes,))
    scratch = [
        lane(lanes, spatial, f), lane(lanes, spatial, f), lane(lanes, spatial, f), lane(lanes, spatial, f),
        lane(3, rows, f), lane(3, GROUP, spatial, f), lane(3, GROUP, spatial, f),
        lane(3, GROUP, f, spatial), lane(3, GROUP, f, spatial), lane(GROUP, f, spatial),
        lane(GROUP, f // HEAD_DIM, 3, spatial, spatial), pltpu.VMEM((GROUP, 8, spatial), F32),
        lane(rows, f), lane(GROUP, f, spatial), pltpu.VMEM((rows, f), F32), lane(rows, f),
        lane(rows, hidden), lane(rows, hidden), lane(rows, f), pltpu.VMEM((rows, f), F32),
        lane(rows, f), lane(3, rows, 2 * f), lane(7, f, spatial),
    ] + [dma] * 8
    return pl.pallas_call(
        functools.partial(layer_kernel, lanes, spatial, f, hidden, tm_count),
        in_specs=[smem] * 3 + [hbm] + [vmem] * (2 + len(weights)),
        out_specs=[vmem, vmem, hbm, hbm] + [vmem] * len(accumulators),
        out_shape=[whole] * 4 + [jax.ShapeDtypeStruct(s, F32) for s in accumulators],
        scratch_shapes=scratch,
        name="layer",
        compiler_params=pltpu.CompilerParams(
            vmem_limit_bytes=63 * 1024 * 1024, collective_id=0, has_side_effects=True
        ),
        cost_estimate=pl.CostEstimate(flops=100 * 10**9, bytes_accessed=40 * 10**6, transcendentals=0),
    )(*scalars, tokens, tokens, cotangent, *weights)


def body(
    tokens, cotangent, lane_frames, pre_gain, pre_bias, w_project, query_bias, value_bias,
    w_out, out_bias, mid_gain, mid_bias, w_up, up_bias, w_down, down_bias,
):
    lanes, spatial, f = tokens.shape[1:]
    hidden = w_up.shape[1]
    tm_count = lax.axis_size("tm")
    tm_index = lax.axis_index("tm")
    lane_span = jnp.maximum(lane_frames // (2 * tm_count), 1)
    lane_offset = jnp.arange(lanes, dtype=jnp.int32) % lane_span
    occupied = lane_frames > 0
    low_ok = (occupied & ((tm_index > 0) | (lane_offset > 0))).astype(jnp.int32)
    up_ok = (occupied & ((tm_index < tm_count - 1) | (lane_offset < lane_span - 1))).astype(jnp.int32)
    full = occupied.astype(jnp.int32)
    row = lambda v: v.astype(F32).reshape(1, -1)
    weights = (
        row(pre_gain), row(pre_bias), w_project[:, :f].T, w_project,
        query_bias.astype(F32).reshape(-1, 1), row(value_bias), w_out, row(out_bias),
        row(mid_gain), row(mid_bias), w_up, row(up_bias), w_down, row(down_bias),
    )
    got = layer_call(lanes, spatial, f, hidden, tm_count, (low_ok, up_ok, full), tokens, cotangent, weights)
    out, own, above, below = got[:4]
    block = pl.BlockSpec((1, 1, spatial, f), lambda i: (0, i, 0, 0))
    tm_arr = jnp.stack([tm_index, jnp.asarray(tm_count - 1, tm_index.dtype)]).astype(jnp.int32)
    input_grad = pl.pallas_call(
        finish_kernel,
        grid=(lanes,),
        in_specs=[pl.BlockSpec(memory_space=pltpu.SMEM), block, block, block],
        out_specs=block,
        out_shape=jax.ShapeDtypeStruct(tokens.shape, BF16),
        name="finish",
    )(tm_arr, own, above, below)

    g_project, g_out, g_up, g_down, g_small, g_upb = got[4:]
    pieces = [g_project.reshape(-1, f), g_out, g_up.reshape(-1, f), g_down.reshape(-1, f), g_small, g_upb.reshape(-1, f)]
    sizes = [p.shape[0] for p in pieces]
    packed = jnp.concatenate(pieces, 0).astype(BF16)
    packed = lax.psum(packed, ("tm", "clip")).astype(F32)
    parts, at = [], 0
    for n in sizes:
        parts.append(packed[at : at + n])
        at += n
    g_project, g_out, g_up, g_down, g_small, g_upb = parts
    g_project = g_project.reshape(f, 3 * f)
    g_up = g_up.reshape(f, hidden)
    g_down = g_down.reshape(f, hidden).T
    g_upb = g_upb.reshape(hidden)
    return (
        out, input_grad, g_small[0], g_small[1], g_project, g_small[2], g_small[7], g_out, g_small[3],
        g_small[4], g_small[5], g_up, g_upb, g_down, g_small[6],
    )


def solution(mesh):
    spread = P("tm", "clip", None, None)
    return jax.shard_map(
        body,
        mesh=mesh,
        in_specs=(spread, spread, P("clip")) + (P(),) * 13,
        out_specs=(spread, spread) + (P(),) * 13,
        check_vma=False,
    )
```

```python
import functools

import jax
import jax.numpy as jnp
from jax import lax
from jax.experimental import pallas as pl
from jax.experimental.pallas import tpu as pltpu
from jax.sharding import PartitionSpec as P

HEAD_DIM = 64
GROUP = 2
WRAP = 4
MESH = pl.DeviceIdType.MESH
EPSILON = 1e-06
FAR = 1e30
F32 = jnp.float32
BF16 = jnp.bfloat16
NN = (((1,), (0,)), ((), ()))
NT = (((1,), (1,)), ((), ()))
TN = (((0,), (0,)), ((), ()))


def dot(a, b, dims=NN):
    return lax.dot_general(a, b, dims, preferred_element_type=F32)


def row_mean(value):
    return jnp.sum(value, -1, keepdims=True) * (1.0 / value.shape[-1])


def normalise(x):
    center = x - row_mean(x)
    rate = lax.rsqrt(row_mean(center * center) + EPSILON)
    return center * rate, rate


def norm_back(grad, xhat, rate, gain):
    e = grad * gain
    return rate * (e - row_mean(e) - xhat * row_mean(e * xhat))


def gelu_parts(h):
    bell = jnp.exp(-0.5 * (h * h))
    t = 1.0 / (1.0 + 0.23164190 * jnp.abs(h))
    poly = t * (0.127414796 + t * (-0.142248368 + t * (0.7107068705 + t * (-0.7265760135 + t * 0.5307027145))))
    tail = poly * bell
    phi = jnp.where(h >= 0.0, 1.0 - tail, tail)
    return h * phi, phi + h * (bell * 0.3989422804014327)


def column_sum(value):
    return jnp.sum(value, 0, keepdims=True)


class Reduction:
    def __init__(
        self, f, hidden, tm, tm_count, masks, bit, across, others, sums, sends,
        r_core, r_one, r_two, r_tm, own_chunk, gathered, small, r_small, send_sems, recv_sems, local_sems,
    ):
        self.f, self.hidden, self.tm, self.tm_count = f, hidden, tm, tm_count
        self.masks, self.bit, self.across, self.others = masks, bit, across, others
        self.sums, self.sends = sums, sends
        self.r_core, self.r_one, self.r_two, self.r_tm = r_core, r_one, r_two, r_tm
        self.own_chunk, self.gathered, self.small, self.r_small = own_chunk, gathered, small, r_small
        self.send_sems, self.recv_sems, self.local_sems = send_sems, recv_sems, local_sems
        self.used, self.trades = 0, 0
        half = (len(masks) - 1) // 2
        self.extra = masks[2 : 1 + half] + masks[2 + half :]
        one, two = masks[1], masks[1 + half]
        wide = hidden // 2
        self.pieces = [
            (1, 0, hidden, one, two), (2, 0, hidden, two, one), (0, 0, wide, one, two), (0, wide, wide, two, one),
        ]
        self.core = {a: None for a in range(3)}

    def sem(self, n=1):
        at = self.used
        self.used += n
        return at

    def copy(self, src, dst, at, device):
        return pltpu.make_async_remote_copy(
            src_ref=src, dst_ref=dst, send_sem=self.send_sems.at[at], recv_sem=self.recv_sems.at[at],
            device_id=device, device_id_type=MESH,
        )

    def rows(self, at, count):
        return pl.ds(pl.multiple_of(at, 16), count)

    def start_core(self, arrays):
        count = self.f // 2
        away = self.rows((1 - self.bit[1]) * count, count)
        for a in arrays:
            self.sends[a][away, :] = self.sums[a][away, :].astype(BF16)
            copy = self.copy(self.sends[a].at[away, :], self.r_core.at[a], a, {"clip": self.across[1]})
            copy.start()

    def run(self):
        f = self.f
        self.used = 3
        halves = [f // 2, f // 4, f // 8]
        flying = []

        def exchange_small(device):
            at = self.sem()
            slot = self.trades
            self.trades += 1
            copy = self.copy(self.small, self.r_small.at[slot], at, device)
            copy.start()
            return copy, slot

        def join_small(pair):
            copy, at = pair
            copy.wait()
            self.small[...] += self.r_small[at]

        trading = exchange_small({"clip": self.across[1]})
        base = self.bit[1] * halves[0]
        away = self.rows((1 - self.bit[1]) * halves[0], halves[0])
        for a in (1, 2, 0):
            self.copy(self.sends[a].at[away, :], self.r_core.at[a], a, {"clip": self.across[1]}).wait()
        join_small(trading)

        def add(a, cols, at, count, got):
            where = self.rows(at, count)
            self.sums[a][where, cols] += got.astype(F32)

        def half_step(level, bases, boxes, which):
            count = halves[level]
            sent, new = [], []
            for i, (a, c, n, *ms) in enumerate(self.pieces):
                m = ms[which]
                cols = slice(c, c + n)
                away = self.rows(bases[i] + (1 - self.bit[m]) * count, count)
                if level == 1:
                    got = self.r_core[a, pl.ds(pl.multiple_of((1 - self.bit[m]) * count, 16), count), cols]
                    add(a, cols, bases[i] + (1 - self.bit[m]) * count, count, got)
                self.sends[a][away, cols] = self.sums[a][away, cols].astype(BF16)
                copy = self.copy(
                    self.sends[a].at[away, cols], boxes.at[a, :, cols], self.sem(), {"clip": self.across[m]}
                )
                copy.start()
                sent.append(copy)
                new.append(bases[i] + self.bit[m] * count)
            for i, (a, c, n, *ms) in enumerate(self.pieces):
                cols = slice(c, c + n)
                if level == 1:
                    m = ms[which]
                    got = self.r_core[a, pl.ds(pl.multiple_of(self.bit[m] * count, 16), count), cols]
                    add(a, cols, new[i], count, got)
            for i, (a, c, n, *ms) in enumerate(self.pieces):
                sent[i].wait()
                cols = slice(c, c + n)
                add(a, cols, new[i], count, boxes[a, :, cols])
            return new

        trading = exchange_small({"clip": self.across[self.masks[1]]})
        bases = half_step(1, [base] * 4, self.r_one, 0)
        join_small(trading)
        trading = exchange_small({"clip": self.across[self.pieces[0][4]]})
        bases = half_step(2, bases, self.r_two, 1)
        join_small(trading)
        count = halves[2]
        for n_extra, m in enumerate(self.extra):
            trading = exchange_small({"clip": self.across[m]})
            sent = []
            for i, (a, c, n, *ms) in enumerate(self.pieces):
                cols = slice(c, c + n)
                here = self.rows(bases[i], count)
                box = self.own_chunk.at[1 + n_extra, a, :, cols]
                self.sends[a][here, cols] = self.sums[a][here, cols].astype(BF16)
                copy = self.copy(self.sends[a].at[here, cols], box, self.sem(), {"clip": self.across[m]})
                copy.start()
                sent.append((copy, box))
            for i, (a, c, n, *ms) in enumerate(self.pieces):
                copy, box = sent[i]
                copy.wait()
                cols = slice(c, c + n)
                here = self.rows(bases[i], count)
                self.sums[a][here, cols] = self.sends[a][here, cols].astype(F32) + box[...].astype(F32)
            join_small(trading)

        chunks = []
        for first in (0, 2):
            for q in range(4):
                a, c, n = self.pieces[first + q // 2][:3]
                cols = slice(c + (q % 2) * (n // 2), c + (q % 2) * (n // 2) + n // 2)
                chunks.append((first // 2, q, a, cols, bases[first + q // 2], n // 2))
        parts = self.tm_count
        arrival = {0: self.sem(parts), 1: self.sem(parts)}
        departure = {}
        for which, q, a, cols, at, n in chunks:
            departure[which, q] = self.sem()
            here = self.rows(at, count)

            def send(which=which, q=q, a=a, cols=cols, here=here, n=n):
                self.sends[a][here, cols] = self.sums[a][here, cols].astype(BF16)
                self.chunk_copy(which, q, a, cols, here, n, departure, arrival).start()

            pl.when(self.tm != q)(send)
        trading = exchange_small({"tm": self.tm + 1 - 2 * (self.tm % 2)})
        join_small(trading)
        trading = exchange_small({"tm": self.tm + 2 - 4 * (self.tm // 2)})
        join_small(trading)
        back = {0: self.sem(parts), 1: self.sem(parts)}
        outgoing = self.sem(2 * parts)
        for which, q, a, cols, at, n in chunks:
            here = self.rows(at, count)

            def settle(which=which, q=q, a=a, cols=cols, here=here, n=n):
                total = self.sums[a][here, cols]
                for other in range(parts):
                    if other != q:
                        pltpu.make_async_copy(
                            self.r_tm.at[which, other, :, pl.ds(0, n)], self.r_tm.at[which, other, :, pl.ds(0, n)],
                            self.recv_sems.at[arrival[which] + other],
                        ).wait()
                        total += self.r_tm[which, other, :, :n].astype(F32)
                self.own_chunk[0, which, :, :n] = total.astype(BF16)
                self.publish(which, q, a, cols, here, n, back, outgoing, "start")

            pl.when(self.tm == q)(settle)
        for which, q, a, cols, at, n in chunks:
            here = self.rows(at, count)

            def arrive(which=which, q=q, a=a, cols=cols, here=here, n=n):
                self.chunk_copy(which, q, a, cols, here, n, departure, arrival).wait_send()
                place = self.gathered.at[a, here, cols]
                pltpu.make_async_copy(place, place, self.recv_sems.at[back[which] + q]).wait()

            def left(which=which, q=q, a=a, cols=cols, here=here, n=n):
                self.publish(which, q, a, cols, here, n, back, outgoing, "wait")

            pl.when(self.tm != q)(arrive)
            pl.when(self.tm == q)(left)

        for level, which in ((2, 1), (1, 0)):
            count = halves[level]
            sent = []
            for i, (a, c, n, *ms) in enumerate(self.pieces):
                m = ms[which]
                cols = slice(c, c + n)
                place = self.gathered.at[a, self.rows(bases[i], count), cols]
                copy = self.copy(place, place, self.sem(), {"clip": self.across[m]})
                copy.start()
                sent.append((copy, self.gathered.at[a, self.rows(bases[i] + (1 - 2 * self.bit[m]) * count, count), cols]))
                bases[i] = bases[i] - self.bit[m] * count
            for copy, theirs in sent:
                copy.wait_send()
                copy.wait_recv()
        sent = []
        for a in range(3):
            place = self.gathered.at[a, self.rows(base, halves[0]), :]
            copy = self.copy(place, place, self.sem(), {"clip": self.across[1]})
            copy.start()
            sent.append(copy)
        for copy in sent:
            copy.wait()

    def chunk_copy(self, which, q, a, cols, here, n, departure, arrival):
        return pltpu.make_async_remote_copy(
            src_ref=self.sends[a].at[here, cols], dst_ref=self.r_tm.at[which, self.tm, :, pl.ds(0, n)],
            send_sem=self.send_sems.at[departure[which, q]], recv_sem=self.recv_sems.at[arrival[which] + self.tm],
            device_id={"tm": q}, device_id_type=MESH,
        )

    def publish(self, which, q, a, cols, here, n, back, outgoing, do):
        place = self.gathered.at[a, here, cols]
        chunk = self.own_chunk.at[0, which, :, pl.ds(0, n)]
        local = pltpu.make_async_copy(chunk, place, self.local_sems.at[which])
        local.start() if do == "start" else local.wait()
        for other in range(self.tm_count):
            if other != q:
                copy = pltpu.make_async_remote_copy(
                    src_ref=chunk, dst_ref=place, send_sem=self.send_sems.at[outgoing + which * self.tm_count + other],
                    recv_sem=self.recv_sems.at[back[which] + q], device_id={"tm": other}, device_id_type=MESH,
                )
                copy.start() if do == "start" else copy.wait_send()


def layer_kernel(
    lanes, spatial, features, hidden, tm_count, clip_count,
    low_ok_ref, up_ok_ref, full_ref, tok_hbm, tok_ref, cot_ref,
    pre_gain_ref, pre_bias_ref, wq_t_ref, w_project_ref, query_bias_ref, value_bias_ref,
    w_out_ref, out_bias_ref, mid_gain_ref, mid_bias_ref, w_up_ref, up_bias_ref, w_down_ref, down_bias_ref,
    out_ref, own_ref, above_ref, below_ref, gathered_ref, total_small_ref,
    a_w, a_up, a_down, a_small, a_upb, low_s, up_s, gl_s, gu_s, n1_s, k_s, v_s, kt_s, vt_s, qt_s, p_s, inv_s, att_s, attt_s, res_s, n2_s, act_s, gh_s,
    dao_s, dres_s, dq_s, dkv_s, dt_s,
    send_up, send_down, recv_low, recv_up, send_gl, send_gu, recv_above, recv_below,
    s_w, s_up, s_down, r_core, r_one, r_two, r_tm, own_chunk, r_small, ar_send, ar_recv, ar_local,
):
    f = features
    pad = n1_s.shape[1] // GROUP
    heads = f // HEAD_DIM
    tm = lax.axis_index("tm")
    last = tm_count - 1
    at_low, at_high = tm == 0, tm == last
    higher, lower = lax.rem(tm + 1, tm_count), lax.rem(tm + last, tm_count)
    step_up, step_down = (tm + 1) // tm_count, (tm_count - tm) // tm_count
    pre_gain, pre_bias = pre_gain_ref[...], pre_bias_ref[...]
    mid_gain, mid_bias = mid_gain_ref[...], mid_bias_ref[...]

    def has_low(l):
        return jnp.logical_or(tm > 0, lax.rem(l, WRAP) != 0)

    def has_up(l):
        return jnp.logical_or(tm < last, lax.rem(l, WRAP) != WRAP - 1)

    def copy(src, dst, send, recv, device):
        return pltpu.make_async_remote_copy(
            src_ref=src, dst_ref=dst, send_sem=send, recv_sem=recv, device_id={"tm": device}, device_id_type=MESH
        )

    def rising(l):
        return copy(tok_hbm.at[0, l], low_s.at[l + step_up], send_up.at[l], recv_low.at[l + step_up], higher)

    def falling(l):
        return copy(tok_hbm.at[0, l], up_s.at[l - step_down], send_down.at[l], recv_up.at[l - step_down], lower)

    def returning_low(l):
        return copy(gl_s.at[l], above_ref.at[0, l - step_down], send_gl.at[l], recv_above.at[l - step_down], lower)

    def returning_up(l):
        return copy(gu_s.at[l], below_ref.at[0, l + step_up], send_gu.at[l], recv_below.at[l + step_up], higher)

    clip = lax.axis_index("clip")
    masks = [1 << i for i in range((clip_count - 1).bit_length())]
    bit = {m: (clip // m) % 2 for m in masks}
    across = {m: clip + m * (1 - 2 * bit[m]) for m in masks}
    others = [lax.rem(tm + i, tm_count) for i in range(1, tm_count)]

    barrier = pltpu.get_barrier_semaphore()
    for device in others:
        pl.semaphore_signal(barrier, inc=1, device_id={"tm": device}, device_id_type=MESH)
    for m in masks:
        pl.semaphore_signal(barrier, inc=1, device_id={"clip": across[m]}, device_id_type=MESH)
    pl.semaphore_wait(barrier, len(others) + len(masks))

    def start_tokens(l, carry):
        pl.when(has_up(l))(lambda: rising(l).start())
        pl.when(has_low(l))(lambda: falling(l).start())
        return carry

    lax.fori_loop(0, lanes, start_tokens, 0)

    def fill(l, carry):
        @pl.when(jnp.logical_not(has_low(l)))
        def _():
            low_s[l] = jnp.zeros(low_s.shape[1:], BF16)

        @pl.when(jnp.logical_not(has_up(l)))
        def _():
            up_s[l] = jnp.zeros(up_s.shape[1:], BF16)

        return carry

    lax.fori_loop(0, lanes, fill, 0)

    for new in (a_w, a_up, a_down, a_small, a_upb):
        new[...] = jnp.zeros_like(new)

    def rows_of(j):
        return pl.ds(pl.multiple_of(j * pad, pad), spatial)

    for ref in (n1_s, att_s, dao_s, dq_s, dkv_s, res_s, dres_s):
        for j in range(GROUP):
            if len(ref.shape) == 3:
                ref[:, pl.ds(j * pad + pad - 16, 16), :] = jnp.zeros((ref.shape[0], 16, ref.shape[2]), ref.dtype)
            else:
                ref[pl.ds(j * pad + pad - 16, 16), :] = jnp.zeros((16, ref.shape[1]), ref.dtype)

    sums = Reduction(
        f, hidden, tm, tm_count, masks, bit, across, others, (a_w, a_up, a_down), (s_w, s_up, s_down),
        r_core, r_one, r_two, r_tm, own_chunk, gathered_ref, a_small, r_small, ar_send, ar_recv, ar_local,
    )

    def group(index, carry):
        base = index * GROUP

        def arrive(j, carry):
            l = base + j
            pl.when(has_low(l))(lambda: copy(tok_hbm.at[0, l], low_s.at[l], send_up.at[l], recv_low.at[l], lower).wait_recv())
            pl.when(has_up(l))(lambda: copy(tok_hbm.at[0, l], up_s.at[l], send_down.at[l], recv_up.at[l], higher).wait_recv())
            return carry

        lax.fori_loop(0, GROUP, arrive, 0)

        def forward(j, carry):
            below, above = low_s[base + j].astype(F32), up_s[base + j].astype(F32)
            for s, x in enumerate((below, tok_ref[0, base + j].astype(F32), above)):
                xhat, _ = normalise(x)
                n1 = (xhat * pre_gain + pre_bias).astype(BF16)
                n1_s[s, rows_of(j), :] = n1
                kv = dot(n1, w_project_ref[:, f:])
                k = kv[:, :f].astype(BF16)
                v = (kv[:, f:] + value_bias_ref[...]).astype(BF16)
                k_s[s, j] = k
                v_s[s, j] = v
                kt_s[s, j] = k.T
                vt_s[s, j] = v.T
                if s == 1:
                    qt = (dot(wq_t_ref[...], n1, NT) + query_bias_ref[...]).astype(BF16)
                    qt_s[j] = qt * jnp.asarray(HEAD_DIM ** (-0.5), BF16)
            low_ok, up_ok = low_ok_ref[base + j] > 0, up_ok_ref[base + j] > 0
            low_far, up_far = jnp.where(low_ok, 0.0, FAR), jnp.where(up_ok, 0.0, FAR)
            zero_half = jnp.zeros((HEAD_DIM, spatial), BF16)
            for h in range(heads):
                pair = slice(h // 2 * 2 * HEAD_DIM, (h // 2 + 1) * 2 * HEAD_DIM)
                mine = slice(h * HEAD_DIM, (h + 1) * HEAD_DIM)
                qh = qt_s[j, mine, :]
                qz = jnp.concatenate([qh, zero_half] if h % 2 == 0 else [zero_half, qh], 0)
                scores = [dot(k_s[s, j, :, pair], qz) for s in range(3)]
                tops = [jnp.max(x, 0, keepdims=True) for x in scores]
                top = jnp.maximum(jnp.maximum(tops[0] - low_far, tops[2] - up_far), tops[1])
                total, attended = None, None
                for s, shift in enumerate((top + low_far, top, top + up_far)):
                    prob = jnp.exp(scores[s] - shift)
                    part = column_sum(prob)
                    total = part if total is None else total + part
                    low_prob = prob.astype(BF16)
                    p_s[j, h, s] = low_prob
                    got = dot(vt_s[s, j, mine, :], low_prob)
                    attended = got if attended is None else attended + got
                inverse = 1.0 / total
                inv_s[j, h : h + 1, :] = inverse
                attt_s[j, mine, :] = (attended * inverse).astype(BF16)
            att_s[rows_of(j), :] = attt_s[j].T
            res_s[rows_of(j), :] = tok_ref[0, base + j].astype(F32)
            return carry

        lax.fori_loop(0, GROUP, forward, 0)

        residual = res_s[...] + dot(att_s[...], w_out_ref[...]) + out_bias_ref[...]
        res_s[...] = residual
        xhat2, rate2 = normalise(residual)
        n2_s[...] = (xhat2 * mid_gain + mid_bias).astype(BF16)
        for j in range(GROUP):
            full = full_ref[base + j] > 0
            g = cot_ref[0, base + j]
            dao_s[pl.ds(j * pad, spatial), :] = jnp.where(full, g.astype(F32), 0.0).astype(BF16)

        wide = 256

        def mlp(c, carry):
            cols = pl.ds(pl.multiple_of(c * wide, wide), wide)
            h = dot(n2_s[...], w_up_ref[:, cols]) + up_bias_ref[:, cols]
            act, slope = gelu_parts(h)
            act_s[:, cols] = act.astype(BF16)
            gh = (dot(dao_s[...], w_down_ref[cols, :], NT) * slope).astype(BF16)
            gh_s[:, cols] = gh
            a_upb[:, cols] += column_sum(gh.astype(F32))
            return carry

        lax.fori_loop(0, hidden // wide, mlp, 0)
        a_up[...] += dot(n2_s[...], gh_s[...], TN)
        a_down[...] += dot(dao_s[...], act_s[...], TN)
        pl.when(index == lanes // GROUP - 1)(lambda: sums.start_core((1, 2)))
        total_out = dot(act_s[...], w_down_ref[...]) + down_bias_ref[...] + res_s[...]
        grad_n2 = dot(gh_s[...], w_up_ref[...], NT)
        for j in range(GROUP):
            full = full_ref[base + j] > 0
            mine = total_out[j * pad : j * pad + spatial]
            out_ref[0, base + j] = jnp.where(full, mine, tok_ref[0, base + j].astype(F32)).astype(BF16)
        g = dao_s[...].astype(F32)
        xhat2, rate2 = normalise(res_s[...])
        dres = g + norm_back(grad_n2, xhat2, rate2, mid_gain)
        dres_s[...] = dres
        dao = dres.astype(BF16)
        dao_s[...] = dao
        a_small[3:4, :] += column_sum(dao.astype(F32))
        a_small[4:5, :] += column_sum(grad_n2 * xhat2)
        a_small[5:6, :] += column_sum(grad_n2)
        a_small[6:7, :] += column_sum(g)
        a_w[:, 3 * f :] += dot(att_s[...], dao, TN)

        def backward(j, carry):
            dot_rows = dao_s[rows_of(j), :]
            dt = dot(w_out_ref[...], dot_rows, NT).astype(BF16)
            zero_half = jnp.zeros((HEAD_DIM, spatial), BF16)
            for h in range(heads):
                pair = slice(h // 2 * 2 * HEAD_DIM, (h // 2 + 1) * 2 * HEAD_DIM)
                mine = slice(h * HEAD_DIM, (h + 1) * HEAD_DIM)
                dh = dt[mine, :].astype(F32) * inv_s[j, h : h + 1, :]
                delta = column_sum(dh * attt_s[j, mine, :].astype(F32))
                dh = dh.astype(BF16)
                dz = jnp.concatenate([dh, zero_half] if h % 2 == 0 else [zero_half, dh], 0)
                qh = qt_s[j, mine, :]
                grad_q = None
                for s in range(3):
                    prob = p_s[j, h, s]
                    grad_prob = dot(v_s[s, j, :, pair], dz)
                    grad_score = (prob.astype(F32) * (grad_prob - delta)).astype(BF16)
                    dt_s[1 + s, mine, :] = dot(qh, grad_score, NT).astype(BF16)
                    dt_s[4 + s, mine, :] = dot(dh, prob, NT).astype(BF16)
                    got = dot(kt_s[s, j, mine, :], grad_score)
                    grad_q = got if grad_q is None else grad_q + got
                dt_s[0, mine, :] = (grad_q * HEAD_DIM ** (-0.5)).astype(BF16)
            dq_s[rows_of(j), :] = dt_s[0].T
            for s in range(3):
                dkv_s[s, rows_of(j), :f] = dt_s[1 + s].T
                dkv_s[s, rows_of(j), f:] = dt_s[4 + s].T
            return carry

        lax.fori_loop(0, GROUP, backward, 0)

        dq = dq_s[...]
        a_w[:, :f] += dot(n1_s[1], dq, TN)
        a_small[2:3, :] += column_sum(dq.astype(F32))
        for s in range(3):
            dkv = dkv_s[s]
            a_w[:, f : 3 * f] += dot(n1_s[s], dkv, TN)
            a_small[7:8, :] += column_sum(dkv[:, f:].astype(F32))

        def finish(j, carry):
            below, above = low_s[base + j].astype(F32), up_s[base + j].astype(F32)
            for s, x in enumerate((below, tok_ref[0, base + j].astype(F32), above)):
                grad = dot(dkv_s[s, rows_of(j), :], w_project_ref[:, f:], NT)
                if s == 1:
                    grad += dot(dq_s[rows_of(j), :], w_project_ref[:, :f], NT)
                xhat, rate = normalise(x)
                a_small[0:1, :] += column_sum(grad * xhat)
                a_small[1:2, :] += column_sum(grad)
                back = norm_back(grad, xhat, rate, pre_gain)
                if s == 1:
                    straight = jnp.where(full_ref[base + j] > 0, 0.0, cot_ref[0, base + j].astype(F32))
                    own_ref[0, base + j] = (back + dres_s[rows_of(j), :] + straight).astype(BF16)
                else:
                    (gl_s if s == 0 else gu_s)[base + j] = back.astype(BF16)
            return carry

        lax.fori_loop(0, GROUP, finish, 0)

        def give_back(j, carry):
            l = base + j
            pl.when(has_low(l))(lambda: returning_low(l).start())
            pl.when(has_up(l))(lambda: returning_up(l).start())
            return carry

        lax.fori_loop(0, GROUP, give_back, 0)
        return carry

    lax.fori_loop(0, lanes // GROUP, group, 0)
    for i in range(hidden // f):
        a_small[8 + i : 9 + i, :] = a_upb[:, i * f : (i + 1) * f]
    sums.start_core((0,))
    sums.run()
    total_small_ref[...] = a_small[...]

    def settle(l, carry):
        @pl.when(has_up(l))
        def _():
            rising(l).wait_send()
            returning_up(l).wait_send()
            copy(gl_s.at[l], above_ref.at[0, l], send_gl.at[l], recv_above.at[l], higher).wait_recv()

        @pl.when(has_low(l))
        def _():
            falling(l).wait_send()
            returning_low(l).wait_send()
            copy(gu_s.at[l], below_ref.at[0, l], send_gu.at[l], recv_below.at[l], lower).wait_recv()

        return carry

    lax.fori_loop(0, lanes, settle, 0)


def finish_kernel(tm_ref, own_ref, above_ref, below_ref, out_ref):
    tm, last = tm_ref[0], tm_ref[1]
    for lane in range(WRAP):
        total = own_ref[0, lane].astype(F32)
        above, below = above_ref[0, lane].astype(F32), below_ref[0, lane].astype(F32)
        total += above if lane < WRAP - 1 else jnp.where(tm < last, above, 0.0)
        total += below if lane > 0 else jnp.where(tm > 0, below, 0.0)
        out_ref[0, lane] = total.astype(BF16)


def unpack_kernel(in_ref, project_ref, out_ref, up_ref, down_ref):
    f = out_ref.shape[1]
    project_ref[...] = in_ref[0, :, : 3 * f].astype(F32)
    out_ref[...] = in_ref[0, :, 3 * f :].astype(F32)
    up_ref[...] = in_ref[1].astype(F32)
    down_ref[...] = in_ref[2].astype(F32).T


def layer_call(lanes, spatial, f, hidden, tm_count, clip_count, scalars, tokens, cotangent, weights):
    pad = -(-spatial // 16) * 16
    rows = GROUP * pad
    smem = pl.BlockSpec(memory_space=pltpu.SMEM)
    vmem = pl.BlockSpec(memory_space=pltpu.VMEM)
    hbm = pl.BlockSpec(memory_space=pl.ANY)
    masks = (clip_count - 1).bit_length()
    extra = masks - 3
    sums = [pltpu.VMEM(s, F32) for s in [(f, hidden)] * 3 + [(16, f), (1, hidden)]]
    whole = jax.ShapeDtypeStruct((1, lanes, spatial, f), BF16)
    lane = lambda *s: pltpu.VMEM(s, BF16)
    dma = pltpu.SemaphoreType.DMA((lanes,))
    scratch = sums + [
        lane(lanes, spatial, f), lane(lanes, spatial, f), lane(lanes, spatial, f), lane(lanes, spatial, f),
        lane(3, rows, f), lane(3, GROUP, spatial, f), lane(3, GROUP, spatial, f),
        lane(3, GROUP, f, spatial), lane(3, GROUP, f, spatial), lane(GROUP, f, spatial),
        lane(GROUP, f // HEAD_DIM, 3, spatial, spatial), pltpu.VMEM((GROUP, 8, spatial), F32),
        lane(rows, f), lane(GROUP, f, spatial), pltpu.VMEM((rows, f), F32), lane(rows, f),
        lane(rows, hidden), lane(rows, hidden), lane(rows, f), pltpu.VMEM((rows, f), F32),
        lane(rows, f), lane(3, rows, 2 * f), lane(7, f, spatial),
    ] + [dma] * 8
    sems = pltpu.SemaphoreType.DMA((96,))
    scratch += [
        lane(f, hidden), lane(f, hidden), lane(f, hidden), lane(3, f // 2, hidden), lane(3, f // 4, hidden),
        lane(3, f // 8, hidden), lane(2, tm_count, f // 8, hidden // 2), lane(1 + extra, 3, f // 8, hidden),
        pltpu.VMEM((masks + 2, 16, f), F32), sems, sems, pltpu.SemaphoreType.DMA((2,)),
    ]
    return pl.pallas_call(
        functools.partial(layer_kernel, lanes, spatial, f, hidden, tm_count, clip_count),
        in_specs=[smem] * 3 + [hbm] + [vmem] * (2 + len(weights)),
        out_specs=[vmem, vmem, hbm, hbm, hbm, vmem],
        out_shape=[whole] * 4 + [jax.ShapeDtypeStruct((3, f, hidden), BF16), jax.ShapeDtypeStruct((16, f), F32)],
        scratch_shapes=scratch,
        name="layer",
        compiler_params=pltpu.CompilerParams(
            vmem_limit_bytes=63 * 1024 * 1024, collective_id=0, has_side_effects=True
        ),
        cost_estimate=pl.CostEstimate(flops=100 * 10**9, bytes_accessed=40 * 10**6, transcendentals=0),
    )(*scalars, tokens, tokens, cotangent, *weights)


def body(
    tokens, cotangent, lane_frames, pre_gain, pre_bias, w_project, query_bias, value_bias,
    w_out, out_bias, mid_gain, mid_bias, w_up, up_bias, w_down, down_bias,
):
    lanes, spatial, f = tokens.shape[1:]
    hidden = w_up.shape[1]
    tm_count = lax.axis_size("tm")
    tm_index = lax.axis_index("tm")
    lane_span = jnp.maximum(lane_frames // (2 * tm_count), 1)
    lane_offset = jnp.arange(lanes, dtype=jnp.int32) % lane_span
    occupied = lane_frames > 0
    low_ok = (occupied & ((tm_index > 0) | (lane_offset > 0))).astype(jnp.int32)
    up_ok = (occupied & ((tm_index < tm_count - 1) | (lane_offset < lane_span - 1))).astype(jnp.int32)
    full = occupied.astype(jnp.int32)
    row = lambda v: v.astype(F32).reshape(1, -1)
    weights = (
        row(pre_gain), row(pre_bias), w_project[:, :f].T, w_project,
        query_bias.astype(F32).reshape(-1, 1), row(value_bias), w_out, row(out_bias),
        row(mid_gain), row(mid_bias), w_up, row(up_bias), w_down, row(down_bias),
    )
    out, own, above, below, gathered, small = layer_call(
        lanes, spatial, f, hidden, tm_count, lax.axis_size("clip"), (low_ok, up_ok, full), tokens, cotangent, weights
    )
    block = pl.BlockSpec((1, WRAP, spatial, f), lambda i: (0, i, 0, 0))
    tm_arr = jnp.stack([tm_index, jnp.asarray(tm_count - 1, tm_index.dtype)]).astype(jnp.int32)
    input_grad = pl.pallas_call(
        finish_kernel,
        grid=(lanes // WRAP,),
        in_specs=[pl.BlockSpec(memory_space=pltpu.SMEM), block, block, block],
        out_specs=block,
        out_shape=jax.ShapeDtypeStruct(tokens.shape, BF16),
        name="finish",
    )(tm_arr, own, above, below)

    tall = 128
    wide_block = lambda n: pl.BlockSpec((tall, n), lambda i: (i, 0))
    g_project, g_out, g_up, g_down = pl.pallas_call(
        unpack_kernel,
        grid=(f // tall,),
        in_specs=[pl.BlockSpec((3, tall, hidden), lambda i: (0, i, 0))],
        out_specs=[wide_block(3 * f), wide_block(f), wide_block(hidden), pl.BlockSpec((hidden, tall), lambda i: (0, i))],
        out_shape=[jax.ShapeDtypeStruct(n, F32) for n in ((f, 3 * f), (f, f), (f, hidden), (hidden, f))],
        name="unpack",
    )(gathered)
    g_small, g_upb = small[:8], small[8 : 8 + hidden // f].reshape(hidden)
    return (
        out, input_grad, g_small[0], g_small[1], g_project, g_small[2], g_small[7], g_out, g_small[3],
        g_small[4], g_small[5], g_up, g_upb, g_down, g_small[6],
    )


def solution(mesh):
    spread = P("tm", "clip", None, None)
    return jax.shard_map(
        body,
        mesh=mesh,
        in_specs=(spread, spread, P("clip")) + (P(),) * 13,
        out_specs=(spread, spread) + (P(),) * 13,
        check_vma=False,
    )
```

```python
import functools

import jax
import jax.numpy as jnp
from jax import lax
from jax.experimental import pallas as pl
from jax.experimental.pallas import tpu as pltpu
from jax.sharding import PartitionSpec as P

HEAD_DIM = 64
GROUP = 2
WRAP = 4
MESH = pl.DeviceIdType.MESH
EPSILON = 1e-06
FAR = 1e30
F32 = jnp.float32
BF16 = jnp.bfloat16
NN = (((1,), (0,)), ((), ()))
NT = (((1,), (1,)), ((), ()))
TN = (((0,), (0,)), ((), ()))


def dot(a, b, dims=NN):
    return lax.dot_general(a, b, dims, preferred_element_type=F32)


def row_mean(value):
    return jnp.sum(value, -1, keepdims=True) * (1.0 / value.shape[-1])


def normalise(x):
    center = x - row_mean(x)
    rate = lax.rsqrt(row_mean(center * center) + EPSILON)
    return center * rate, rate


def norm_back(grad, xhat, rate, gain):
    e = grad * gain
    return rate * (e - row_mean(e) - xhat * row_mean(e * xhat))


def gelu_parts(h):
    bell = jnp.exp(-0.5 * (h * h))
    t = 1.0 / (1.0 + 0.23164190 * jnp.abs(h))
    poly = t * (0.127414796 + t * (-0.142248368 + t * (0.7107068705 + t * (-0.7265760135 + t * 0.5307027145))))
    tail = poly * bell
    phi = jnp.where(h >= 0.0, 1.0 - tail, tail)
    return h * phi, phi + h * (bell * 0.3989422804014327)


def column_sum(value):
    return jnp.sum(value, 0, keepdims=True)


class Reduction:
    def __init__(
        self, f, hidden, tm, tm_count, masks, bit, across, others, sums, sends,
        r_core, r_one, r_two, r_tm, own_chunk, gathered, small, r_small, send_sems, recv_sems, local_sems,
    ):
        self.f, self.hidden, self.tm, self.tm_count = f, hidden, tm, tm_count
        self.masks, self.bit, self.across, self.others = masks, bit, across, others
        self.sums, self.sends = sums, sends
        self.r_core, self.r_one, self.r_two, self.r_tm = r_core, r_one, r_two, r_tm
        self.own_chunk, self.gathered, self.small, self.r_small = own_chunk, gathered, small, r_small
        self.send_sems, self.recv_sems, self.local_sems = send_sems, recv_sems, local_sems
        self.used, self.trades = 0, 0
        half = (len(masks) - 1) // 2
        self.extra = masks[2 : 1 + half] + masks[2 + half :]
        one, two = masks[1], masks[1 + half]
        wide = hidden // 2
        self.pieces = [
            (1, 0, hidden, one, two), (2, 0, hidden, two, one), (0, 0, wide, one, two), (0, wide, wide, two, one),
        ]
        self.core = {a: None for a in range(3)}

    def sem(self, n=1):
        at = self.used
        self.used += n
        return at

    def copy(self, src, dst, at, device):
        return pltpu.make_async_remote_copy(
            src_ref=src, dst_ref=dst, send_sem=self.send_sems.at[at], recv_sem=self.recv_sems.at[at],
            device_id=device, device_id_type=MESH,
        )

    def rows(self, at, count):
        return pl.ds(pl.multiple_of(at, 16), count)

    def start_core(self, arrays):
        count = self.f // 2
        away = self.rows((1 - self.bit[1]) * count, count)
        for a in arrays:
            self.sends[a][away, :] = self.sums[a][away, :].astype(BF16)
            copy = self.copy(self.sends[a].at[away, :], self.r_core.at[a], a, {"clip": self.across[1]})
            copy.start()

    def run(self):
        f = self.f
        self.used = 3
        halves = [f // 2, f // 4, f // 8]
        flying = []

        def exchange_small(device):
            at = self.sem()
            slot = self.trades
            self.trades += 1
            copy = self.copy(self.small, self.r_small.at[slot], at, device)
            copy.start()
            return copy, slot

        def join_small(pair):
            copy, at = pair
            copy.wait()
            self.small[...] += self.r_small[at]

        trading = exchange_small({"clip": self.across[1]})
        base = self.bit[1] * halves[0]
        away = self.rows((1 - self.bit[1]) * halves[0], halves[0])
        for a in (1, 2, 0):
            self.copy(self.sends[a].at[away, :], self.r_core.at[a], a, {"clip": self.across[1]}).wait()
        join_small(trading)

        def add(a, cols, at, count, got):
            where = self.rows(at, count)
            self.sums[a][where, cols] += got.astype(F32)

        def half_step(level, bases, boxes, which):
            count = halves[level]
            sent, new = [], []
            for i, (a, c, n, *ms) in enumerate(self.pieces):
                m = ms[which]
                cols = slice(c, c + n)
                away = self.rows(bases[i] + (1 - self.bit[m]) * count, count)
                if level == 1:
                    got = self.r_core[a, pl.ds(pl.multiple_of((1 - self.bit[m]) * count, 16), count), cols]
                    add(a, cols, bases[i] + (1 - self.bit[m]) * count, count, got)
                self.sends[a][away, cols] = self.sums[a][away, cols].astype(BF16)
                copy = self.copy(
                    self.sends[a].at[away, cols], boxes.at[a, :, cols], self.sem(), {"clip": self.across[m]}
                )
                copy.start()
                sent.append(copy)
                new.append(bases[i] + self.bit[m] * count)
            for i, (a, c, n, *ms) in enumerate(self.pieces):
                cols = slice(c, c + n)
                if level == 1:
                    m = ms[which]
                    got = self.r_core[a, pl.ds(pl.multiple_of(self.bit[m] * count, 16), count), cols]
                    add(a, cols, new[i], count, got)
            for i, (a, c, n, *ms) in enumerate(self.pieces):
                sent[i].wait()
                cols = slice(c, c + n)
                add(a, cols, new[i], count, boxes[a, :, cols])
            return new

        trading = exchange_small({"clip": self.across[self.masks[1]]})
        bases = half_step(1, [base] * 4, self.r_one, 0)
        join_small(trading)
        trading = exchange_small({"clip": self.across[self.pieces[0][4]]})
        bases = half_step(2, bases, self.r_two, 1)
        join_small(trading)
        count = halves[2]
        for n_extra, m in enumerate(self.extra):
            trading = exchange_small({"clip": self.across[m]})
            sent = []
            for i, (a, c, n, *ms) in enumerate(self.pieces):
                cols = slice(c, c + n)
                here = self.rows(bases[i], count)
                box = self.own_chunk.at[1 + n_extra, a, :, cols]
                self.sends[a][here, cols] = self.sums[a][here, cols].astype(BF16)
                copy = self.copy(self.sends[a].at[here, cols], box, self.sem(), {"clip": self.across[m]})
                copy.start()
                sent.append((copy, box))
            for i, (a, c, n, *ms) in enumerate(self.pieces):
                copy, box = sent[i]
                copy.wait()
                cols = slice(c, c + n)
                here = self.rows(bases[i], count)
                self.sums[a][here, cols] = self.sends[a][here, cols].astype(F32) + box[...].astype(F32)
            join_small(trading)

        chunks = []
        for first in (0, 2):
            for q in range(4):
                a, c, n = self.pieces[first + q // 2][:3]
                cols = slice(c + (q % 2) * (n // 2), c + (q % 2) * (n // 2) + n // 2)
                chunks.append((first // 2, q, a, cols, bases[first + q // 2], n // 2))
        parts = self.tm_count
        arrival = {0: self.sem(parts), 1: self.sem(parts)}
        departure = {}
        for which, q, a, cols, at, n in chunks:
            departure[which, q] = self.sem()
            here = self.rows(at, count)

            def send(which=which, q=q, a=a, cols=cols, here=here, n=n):
                self.sends[a][here, cols] = self.sums[a][here, cols].astype(BF16)
                self.chunk_copy(which, q, a, cols, here, n, departure, arrival).start()

            pl.when(self.tm != q)(send)
        trading = exchange_small({"tm": self.tm + 1 - 2 * (self.tm % 2)})
        join_small(trading)
        trading = exchange_small({"tm": self.tm + 2 - 4 * (self.tm // 2)})
        join_small(trading)
        back = {0: self.sem(parts), 1: self.sem(parts)}
        outgoing = self.sem(2 * parts)
        for which, q, a, cols, at, n in chunks:
            here = self.rows(at, count)

            def settle(which=which, q=q, a=a, cols=cols, here=here, n=n):
                total = self.sums[a][here, cols]
                for other in range(parts):
                    if other != q:
                        pltpu.make_async_copy(
                            self.r_tm.at[which, other, :, pl.ds(0, n)], self.r_tm.at[which, other, :, pl.ds(0, n)],
                            self.recv_sems.at[arrival[which] + other],
                        ).wait()
                        total += self.r_tm[which, other, :, :n].astype(F32)
                self.own_chunk[0, which, :, :n] = total.astype(BF16)
                self.publish(which, q, a, cols, here, n, back, outgoing, "start")

            pl.when(self.tm == q)(settle)
        for which, q, a, cols, at, n in chunks:
            here = self.rows(at, count)

            def arrive(which=which, q=q, a=a, cols=cols, here=here, n=n):
                self.chunk_copy(which, q, a, cols, here, n, departure, arrival).wait_send()
                place = self.gathered.at[a, here, cols]
                pltpu.make_async_copy(place, place, self.recv_sems.at[back[which] + q]).wait()

            def left(which=which, q=q, a=a, cols=cols, here=here, n=n):
                self.publish(which, q, a, cols, here, n, back, outgoing, "wait")

            pl.when(self.tm != q)(arrive)
            pl.when(self.tm == q)(left)

        for level, which in ((2, 1), (1, 0)):
            count = halves[level]
            sent = []
            for i, (a, c, n, *ms) in enumerate(self.pieces):
                m = ms[which]
                cols = slice(c, c + n)
                place = self.gathered.at[a, self.rows(bases[i], count), cols]
                copy = self.copy(place, place, self.sem(), {"clip": self.across[m]})
                copy.start()
                sent.append((copy, self.gathered.at[a, self.rows(bases[i] + (1 - 2 * self.bit[m]) * count, count), cols]))
                bases[i] = bases[i] - self.bit[m] * count
            for copy, theirs in sent:
                copy.wait_send()
                copy.wait_recv()
        sent = []
        for a in range(3):
            place = self.gathered.at[a, self.rows(base, halves[0]), :]
            copy = self.copy(place, place, self.sem(), {"clip": self.across[1]})
            copy.start()
            sent.append(copy)
        for copy in sent:
            copy.wait()

    def chunk_copy(self, which, q, a, cols, here, n, departure, arrival):
        return pltpu.make_async_remote_copy(
            src_ref=self.sends[a].at[here, cols], dst_ref=self.r_tm.at[which, self.tm, :, pl.ds(0, n)],
            send_sem=self.send_sems.at[departure[which, q]], recv_sem=self.recv_sems.at[arrival[which] + self.tm],
            device_id={"tm": q}, device_id_type=MESH,
        )

    def publish(self, which, q, a, cols, here, n, back, outgoing, do):
        place = self.gathered.at[a, here, cols]
        chunk = self.own_chunk.at[0, which, :, pl.ds(0, n)]
        local = pltpu.make_async_copy(chunk, place, self.local_sems.at[which])
        local.start() if do == "start" else local.wait()
        for other in range(self.tm_count):
            if other != q:
                copy = pltpu.make_async_remote_copy(
                    src_ref=chunk, dst_ref=place, send_sem=self.send_sems.at[outgoing + which * self.tm_count + other],
                    recv_sem=self.recv_sems.at[back[which] + q], device_id={"tm": other}, device_id_type=MESH,
                )
                copy.start() if do == "start" else copy.wait_send()


def layer_kernel(
    lanes, spatial, features, hidden, tm_count, clip_count,
    frames_ref, tok_hbm, tok_ref, cot_ref,
    pre_gain_ref, pre_bias_ref, w_project_ref, query_bias_ref, value_bias_ref,
    w_out_ref, out_bias_ref, mid_gain_ref, mid_bias_ref, w_up_ref, up_bias_ref, w_down_ref, down_bias_ref,
    out_ref, own_ref, above_ref, below_ref, gathered_ref, total_small_ref,
    a_w, a_up, a_down, a_small, a_upb, low_s, up_s, gl_s, gu_s, n1_s, k_s, v_s, kt_s, vt_s, qt_s, p_s, inv_s, att_s, attt_s, res_s, n2_s, act_s, gh_s,
    dao_s, dres_s, dq_s, dkv_s, dt_s,
    send_up, send_down, recv_low, recv_up, send_gl, send_gu, recv_above, recv_below,
    s_w, s_up, s_down, r_core, r_one, r_two, r_tm, own_chunk, r_small, ar_send, ar_recv, ar_local,
):
    f = features
    pad = n1_s.shape[1] // GROUP
    heads = f // HEAD_DIM
    tm = lax.axis_index("tm")
    last = tm_count - 1
    at_low, at_high = tm == 0, tm == last
    higher, lower = lax.rem(tm + 1, tm_count), lax.rem(tm + last, tm_count)
    step_up, step_down = (tm + 1) // tm_count, (tm_count - tm) // tm_count

    def row(ref):
        return ref[...].astype(F32).reshape(1, -1)

    pre_gain, pre_bias, mid_gain, mid_bias = row(pre_gain_ref), row(pre_bias_ref), row(mid_gain_ref), row(mid_bias_ref)
    out_bias, down_bias, up_bias = row(out_bias_ref), row(down_bias_ref), row(up_bias_ref)
    query_bias, value_bias = row(query_bias_ref), row(value_bias_ref)

    def full_lane(l):
        return frames_ref[l] > 0

    def joined(l):
        frames = frames_ref[l]
        inner_low = ((frames == 4 * tm_count) & (l % 2 > 0)) | ((frames == 8 * tm_count) & (l % 4 > 0))
        inner_up = ((frames == 4 * tm_count) & (l % 2 < 1)) | ((frames == 8 * tm_count) & (l % 4 < 3))
        return (frames > 0) & (inner_low | (tm > 0)), (frames > 0) & (inner_up | (tm < last))

    def has_low(l):
        return jnp.logical_or(tm > 0, lax.rem(l, WRAP) != 0)

    def has_up(l):
        return jnp.logical_or(tm < last, lax.rem(l, WRAP) != WRAP - 1)

    def copy(src, dst, send, recv, device):
        return pltpu.make_async_remote_copy(
            src_ref=src, dst_ref=dst, send_sem=send, recv_sem=recv, device_id={"tm": device}, device_id_type=MESH
        )

    def rising(l):
        return copy(tok_hbm.at[0, l], low_s.at[l + step_up], send_up.at[l], recv_low.at[l + step_up], higher)

    def falling(l):
        return copy(tok_hbm.at[0, l], up_s.at[l - step_down], send_down.at[l], recv_up.at[l - step_down], lower)

    def returning_low(l):
        return copy(gl_s.at[l], above_ref.at[0, l - step_down], send_gl.at[l], recv_above.at[l - step_down], lower)

    def returning_up(l):
        return copy(gu_s.at[l], below_ref.at[0, l + step_up], send_gu.at[l], recv_below.at[l + step_up], higher)

    clip = lax.axis_index("clip")
    masks = [1 << i for i in range((clip_count - 1).bit_length())]
    bit = {m: (clip // m) % 2 for m in masks}
    across = {m: clip + m * (1 - 2 * bit[m]) for m in masks}
    others = [lax.rem(tm + i, tm_count) for i in range(1, tm_count)]

    barrier = pltpu.get_barrier_semaphore()
    for device in others:
        pl.semaphore_signal(barrier, inc=1, device_id={"tm": device}, device_id_type=MESH)
    for m in masks:
        pl.semaphore_signal(barrier, inc=1, device_id={"clip": across[m]}, device_id_type=MESH)
    pl.semaphore_wait(barrier, len(others) + len(masks))

    def start_tokens(l, carry):
        pl.when(has_up(l))(lambda: rising(l).start())
        pl.when(has_low(l))(lambda: falling(l).start())
        return carry

    lax.fori_loop(0, lanes, start_tokens, 0)

    def fill(l, carry):
        @pl.when(jnp.logical_not(has_low(l)))
        def _():
            low_s[l] = jnp.zeros(low_s.shape[1:], BF16)

        @pl.when(jnp.logical_not(has_up(l)))
        def _():
            up_s[l] = jnp.zeros(up_s.shape[1:], BF16)

        return carry

    lax.fori_loop(0, lanes, fill, 0)

    for new in (a_w, a_up, a_down, a_small, a_upb):
        new[...] = jnp.zeros_like(new)

    def rows_of(j):
        return pl.ds(pl.multiple_of(j * pad, pad), spatial)

    for ref in (n1_s, att_s, dao_s, dq_s, dkv_s, res_s, dres_s):
        for j in range(GROUP):
            if len(ref.shape) == 3:
                ref[:, pl.ds(j * pad + pad - 16, 16), :] = jnp.zeros((ref.shape[0], 16, ref.shape[2]), ref.dtype)
            else:
                ref[pl.ds(j * pad + pad - 16, 16), :] = jnp.zeros((16, ref.shape[1]), ref.dtype)

    sums = Reduction(
        f, hidden, tm, tm_count, masks, bit, across, others, (a_w, a_up, a_down), (s_w, s_up, s_down),
        r_core, r_one, r_two, r_tm, own_chunk, gathered_ref, a_small, r_small, ar_send, ar_recv, ar_local,
    )

    def group(index, carry):
        base = index * GROUP

        def arrive(j, carry):
            l = base + j
            pl.when(has_low(l))(lambda: copy(tok_hbm.at[0, l], low_s.at[l], send_up.at[l], recv_low.at[l], lower).wait_recv())
            pl.when(has_up(l))(lambda: copy(tok_hbm.at[0, l], up_s.at[l], send_down.at[l], recv_up.at[l], higher).wait_recv())
            return carry

        lax.fori_loop(0, GROUP, arrive, 0)

        def forward(j, carry):
            below, above = low_s[base + j].astype(F32), up_s[base + j].astype(F32)
            for s, x in enumerate((below, tok_ref[0, base + j].astype(F32), above)):
                xhat, _ = normalise(x)
                n1 = (xhat * pre_gain + pre_bias).astype(BF16)
                n1_s[s, rows_of(j), :] = n1
                kv = dot(n1, w_project_ref[:, f:])
                k = kv[:, :f].astype(BF16)
                v = (kv[:, f:] + value_bias).astype(BF16)
                k_s[s, j] = k
                v_s[s, j] = v
                kt_s[s, j] = k.T
                vt_s[s, j] = v.T
                if s == 1:
                    q = (dot(n1, w_project_ref[:, :f]) + query_bias).astype(BF16)
                    qt_s[j] = (q * jnp.asarray(HEAD_DIM ** (-0.5), BF16)).T
            low_ok, up_ok = joined(base + j)
            low_far, up_far = jnp.where(low_ok, 0.0, FAR), jnp.where(up_ok, 0.0, FAR)
            zero_half = jnp.zeros((HEAD_DIM, spatial), BF16)
            def get_scores(h):
                pair = slice(h // 2 * 2 * HEAD_DIM, (h // 2 + 1) * 2 * HEAD_DIM)
                qh = qt_s[j, h * HEAD_DIM : (h + 1) * HEAD_DIM, :]
                qz = jnp.concatenate([qh, zero_half] if h % 2 == 0 else [zero_half, qh], 0)
                return [dot(k_s[s, j, :, pair], qz) for s in range(3)]

            later = get_scores(0)
            for h in range(heads):
                mine = slice(h * HEAD_DIM, (h + 1) * HEAD_DIM)
                scores = later
                if h + 1 < heads:
                    later = get_scores(h + 1)
                tops = [jnp.max(x, 0, keepdims=True) for x in scores]
                top = jnp.maximum(jnp.maximum(tops[0] - low_far, tops[2] - up_far), tops[1])
                total, attended = None, None
                for s, shift in enumerate((top + low_far, top, top + up_far)):
                    prob = jnp.exp(scores[s] - shift)
                    part = column_sum(prob)
                    total = part if total is None else total + part
                    low_prob = prob.astype(BF16)
                    p_s[j, h, s] = low_prob
                    got = dot(vt_s[s, j, mine, :], low_prob)
                    attended = got if attended is None else attended + got
                inverse = 1.0 / total
                inv_s[j, h : h + 1, :] = inverse
                attt_s[j, mine, :] = (attended * inverse).astype(BF16)
            att_s[rows_of(j), :] = attt_s[j].T
            res_s[rows_of(j), :] = tok_ref[0, base + j].astype(F32)
            return carry

        for j in range(GROUP):
            forward(j, 0)

        residual = res_s[...] + dot(att_s[...], w_out_ref[...]) + out_bias
        res_s[...] = residual
        xhat2, rate2 = normalise(residual)
        n2_s[...] = (xhat2 * mid_gain + mid_bias).astype(BF16)
        for j in range(GROUP):
            full = full_lane(base + j)
            g = cot_ref[0, base + j]
            dao_s[pl.ds(j * pad, spatial), :] = jnp.where(full, g.astype(F32), 0.0).astype(BF16)

        wide = 256

        def mlp(c, carry):
            cols = pl.ds(pl.multiple_of(c * wide, wide), wide)
            h = dot(n2_s[...], w_up_ref[:, cols]) + up_bias[:, c * wide : (c + 1) * wide]
            act, slope = gelu_parts(h)
            act_s[:, cols] = act.astype(BF16)
            gh = (dot(dao_s[...], w_down_ref[cols, :], NT) * slope).astype(BF16)
            gh_s[:, cols] = gh
            a_upb[:, cols] += column_sum(gh.astype(F32))
            return carry

        for c in range(hidden // wide):
            mlp(c, 0)
        a_up[...] += dot(n2_s[...], gh_s[...], TN)
        a_down[...] += dot(dao_s[...], act_s[...], TN)
        pl.when(index == lanes // GROUP - 1)(lambda: sums.start_core((1, 2)))
        total_out = dot(act_s[...], w_down_ref[...]) + down_bias + res_s[...]
        grad_n2 = dot(gh_s[...], w_up_ref[...], NT)
        for j in range(GROUP):
            full = full_lane(base + j)
            mine = total_out[j * pad : j * pad + spatial]
            out_ref[0, base + j] = jnp.where(full, mine, tok_ref[0, base + j].astype(F32)).astype(BF16)
        g = dao_s[...].astype(F32)
        xhat2, rate2 = normalise(res_s[...])
        dres = g + norm_back(grad_n2, xhat2, rate2, mid_gain)
        dres_s[...] = dres
        dao = dres.astype(BF16)
        dao_s[...] = dao
        a_small[3:4, :] += column_sum(dao.astype(F32))
        a_small[4:5, :] += column_sum(grad_n2 * xhat2)
        a_small[5:6, :] += column_sum(grad_n2)
        a_small[6:7, :] += column_sum(g)
        a_w[:, 3 * f :] += dot(att_s[...], dao, TN)

        def backward(j, carry):
            dot_rows = dao_s[rows_of(j), :]
            dt = dot(w_out_ref[...], dot_rows, NT).astype(BF16)
            zero_half = jnp.zeros((HEAD_DIM, spatial), BF16)
            def prepare(h):
                pair = slice(h // 2 * 2 * HEAD_DIM, (h // 2 + 1) * 2 * HEAD_DIM)
                mine = slice(h * HEAD_DIM, (h + 1) * HEAD_DIM)
                dh = dt[mine, :].astype(F32) * inv_s[j, h : h + 1, :]
                delta = column_sum(dh * attt_s[j, mine, :].astype(F32))
                dh = dh.astype(BF16)
                dz = jnp.concatenate([dh, zero_half] if h % 2 == 0 else [zero_half, dh], 0)
                return dh, delta, [dot(v_s[s, j, :, pair], dz) for s in range(3)]

            later = prepare(0)
            for h in range(heads):
                mine = slice(h * HEAD_DIM, (h + 1) * HEAD_DIM)
                dh, delta, grad_probs = later
                if h + 1 < heads:
                    later = prepare(h + 1)
                qh = qt_s[j, mine, :]
                probs = [p_s[j, h, s] for s in range(3)]
                for s in range(3):
                    dt_s[4 + s, mine, :] = dot(dh, probs[s], NT).astype(BF16)
                ds = [(probs[s].astype(F32) * (grad_probs[s] - delta)).astype(BF16) for s in range(3)]
                for s in range(3):
                    dt_s[1 + s, mine, :] = dot(qh, ds[s], NT).astype(BF16)
                grad_q = None
                for s in range(3):
                    got = dot(kt_s[s, j, mine, :], ds[s])
                    grad_q = got if grad_q is None else grad_q + got
                dt_s[0, mine, :] = (grad_q * HEAD_DIM ** (-0.5)).astype(BF16)
            dq_s[rows_of(j), :] = dt_s[0].T
            for s in range(3):
                dkv_s[s, rows_of(j), :f] = dt_s[1 + s].T
                dkv_s[s, rows_of(j), f:] = dt_s[4 + s].T
            return carry

        for j in range(GROUP):
            backward(j, 0)

        dq = dq_s[...]
        a_w[:, :f] += dot(n1_s[1], dq, TN)
        a_small[2:3, :] += column_sum(dq.astype(F32))
        for s in range(3):
            dkv = dkv_s[s]
            a_w[:, f : 3 * f] += dot(n1_s[s], dkv, TN)
            a_small[7:8, :] += column_sum(dkv[:, f:].astype(F32))

        def finish(j, carry):
            below, above = low_s[base + j].astype(F32), up_s[base + j].astype(F32)
            for s, x in enumerate((below, tok_ref[0, base + j].astype(F32), above)):
                grad = dot(dkv_s[s, rows_of(j), :], w_project_ref[:, f:], NT)
                if s == 1:
                    grad += dot(dq_s[rows_of(j), :], w_project_ref[:, :f], NT)
                xhat, rate = normalise(x)
                a_small[0:1, :] += column_sum(grad * xhat)
                a_small[1:2, :] += column_sum(grad)
                back = norm_back(grad, xhat, rate, pre_gain)
                if s == 1:
                    straight = jnp.where(full_lane(base + j), 0.0, cot_ref[0, base + j].astype(F32))
                    own_ref[0, base + j] = (back + dres_s[rows_of(j), :] + straight).astype(BF16)
                else:
                    (gl_s if s == 0 else gu_s)[base + j] = back.astype(BF16)
            return carry

        for j in range(GROUP):
            finish(j, 0)

        def give_back(j, carry):
            l = base + j
            pl.when(has_low(l))(lambda: returning_low(l).start())
            pl.when(has_up(l))(lambda: returning_up(l).start())
            return carry

        lax.fori_loop(0, GROUP, give_back, 0)
        return carry

    lax.fori_loop(0, lanes // GROUP, group, 0)
    for i in range(hidden // f):
        a_small[8 + i : 9 + i, :] = a_upb[:, i * f : (i + 1) * f]
    sums.start_core((0,))
    sums.run()
    total_small_ref[...] = a_small[...]

    def settle(l, carry):
        @pl.when(has_up(l))
        def _():
            rising(l).wait_send()
            returning_up(l).wait_send()
            copy(gl_s.at[l], above_ref.at[0, l], send_gl.at[l], recv_above.at[l], higher).wait_recv()

        @pl.when(has_low(l))
        def _():
            falling(l).wait_send()
            returning_low(l).wait_send()
            copy(gu_s.at[l], below_ref.at[0, l], send_gu.at[l], recv_below.at[l], lower).wait_recv()

        return carry

    lax.fori_loop(0, lanes, settle, 0)


def finish_kernel(tm_ref, own_ref, above_ref, below_ref, out_ref):
    tm, last = tm_ref[0], tm_ref[1]
    for lane in range(WRAP):
        total = own_ref[0, lane].astype(F32)
        above, below = above_ref[0, lane].astype(F32), below_ref[0, lane].astype(F32)
        total += above if lane < WRAP - 1 else jnp.where(tm < last, above, 0.0)
        total += below if lane > 0 else jnp.where(tm > 0, below, 0.0)
        out_ref[0, lane] = total.astype(BF16)


def unpack_kernel(in_ref, project_ref, out_ref, up_ref, down_ref):
    f = out_ref.shape[1]
    project_ref[...] = in_ref[0, :, : 3 * f].astype(F32)
    out_ref[...] = in_ref[0, :, 3 * f :].astype(F32)
    up_ref[...] = in_ref[1].astype(F32)
    down_ref[...] = in_ref[2].astype(F32).T


def layer_call(lanes, spatial, f, hidden, tm_count, clip_count, frames, tokens, cotangent, weights):
    pad = -(-spatial // 16) * 16
    rows = GROUP * pad
    smem = pl.BlockSpec(memory_space=pltpu.SMEM)
    vmem = pl.BlockSpec(memory_space=pltpu.VMEM)
    hbm = pl.BlockSpec(memory_space=pl.ANY)
    masks = (clip_count - 1).bit_length()
    extra = masks - 3
    sums = [pltpu.VMEM(s, F32) for s in [(f, hidden)] * 3 + [(16, f), (1, hidden)]]
    whole = jax.ShapeDtypeStruct((1, lanes, spatial, f), BF16)
    lane = lambda *s: pltpu.VMEM(s, BF16)
    dma = pltpu.SemaphoreType.DMA((lanes,))
    scratch = sums + [
        lane(lanes, spatial, f), lane(lanes, spatial, f), lane(lanes, spatial, f), lane(lanes, spatial, f),
        lane(3, rows, f), lane(3, GROUP, spatial, f), lane(3, GROUP, spatial, f),
        lane(3, GROUP, f, spatial), lane(3, GROUP, f, spatial), lane(GROUP, f, spatial),
        lane(GROUP, f // HEAD_DIM, 3, spatial, spatial), pltpu.VMEM((GROUP, 8, spatial), F32),
        lane(rows, f), lane(GROUP, f, spatial), pltpu.VMEM((rows, f), F32), lane(rows, f),
        lane(rows, hidden), lane(rows, hidden), lane(rows, f), pltpu.VMEM((rows, f), F32),
        lane(rows, f), lane(3, rows, 2 * f), lane(7, f, spatial),
    ] + [dma] * 8
    sems = pltpu.SemaphoreType.DMA((96,))
    scratch += [
        lane(f, hidden), lane(f, hidden), lane(f, hidden), lane(3, f // 2, hidden), lane(3, f // 4, hidden),
        lane(3, f // 8, hidden), lane(2, tm_count, f // 8, hidden // 2), lane(1 + extra, 3, f // 8, hidden),
        pltpu.VMEM((masks + 2, 16, f), F32), sems, sems, pltpu.SemaphoreType.DMA((2,)),
    ]
    return pl.pallas_call(
        functools.partial(layer_kernel, lanes, spatial, f, hidden, tm_count, clip_count),
        in_specs=[smem, hbm] + [vmem] * (2 + len(weights)),
        out_specs=[vmem, vmem, hbm, hbm, hbm, vmem],
        out_shape=[whole] * 4 + [jax.ShapeDtypeStruct((3, f, hidden), BF16), jax.ShapeDtypeStruct((16, f), F32)],
        scratch_shapes=scratch,
        name="layer",
        compiler_params=pltpu.CompilerParams(
            vmem_limit_bytes=63 * 1024 * 1024, collective_id=0, has_side_effects=True
        ),
        cost_estimate=pl.CostEstimate(flops=100 * 10**9, bytes_accessed=40 * 10**6, transcendentals=0),
    )(frames, tokens, tokens, cotangent, *weights)


def body(
    tokens, cotangent, lane_frames, pre_gain, pre_bias, w_project, query_bias, value_bias,
    w_out, out_bias, mid_gain, mid_bias, w_up, up_bias, w_down, down_bias,
):
    lanes, spatial, f = tokens.shape[1:]
    hidden = w_up.shape[1]
    tm_count = lax.axis_size("tm")
    tm_index = lax.axis_index("tm")
    weights = (
        pre_gain, pre_bias, w_project, query_bias, value_bias, w_out, out_bias,
        mid_gain, mid_bias, w_up, up_bias, w_down, down_bias,
    )
    out, own, above, below, gathered, small = layer_call(
        lanes, spatial, f, hidden, tm_count, lax.axis_size("clip"), lane_frames, tokens, cotangent, weights
    )
    block = pl.BlockSpec((1, WRAP, spatial, f), lambda i: (0, i, 0, 0))
    tm_arr = jnp.stack([tm_index, jnp.asarray(tm_count - 1, tm_index.dtype)]).astype(jnp.int32)
    input_grad = pl.pallas_call(
        finish_kernel,
        grid=(lanes // WRAP,),
        in_specs=[pl.BlockSpec(memory_space=pltpu.SMEM), block, block, block],
        out_specs=block,
        out_shape=jax.ShapeDtypeStruct(tokens.shape, BF16),
        name="finish",
    )(tm_arr, own, above, below)

    tall = 128
    wide_block = lambda n: pl.BlockSpec((tall, n), lambda i: (i, 0))
    g_project, g_out, g_up, g_down = pl.pallas_call(
        unpack_kernel,
        grid=(f // tall,),
        in_specs=[pl.BlockSpec((3, tall, hidden), lambda i: (0, i, 0))],
        out_specs=[wide_block(3 * f), wide_block(f), wide_block(hidden), pl.BlockSpec((hidden, tall), lambda i: (0, i))],
        out_shape=[jax.ShapeDtypeStruct(n, F32) for n in ((f, 3 * f), (f, f), (f, hidden), (hidden, f))],
        name="unpack",
    )(gathered)
    g_small, g_upb = small[:8], small[8 : 8 + hidden // f].reshape(hidden)
    return (
        out, input_grad, g_small[0], g_small[1], g_project, g_small[2], g_small[7], g_out, g_small[3],
        g_small[4], g_small[5], g_up, g_upb, g_down, g_small[6],
    )


def solution(mesh):
    spread = P("tm", "clip", None, None)
    return jax.shard_map(
        body,
        mesh=mesh,
        in_specs=(spread, spread, P("clip")) + (P(),) * 13,
        out_specs=(spread, spread) + (P(),) * 13,
        check_vma=False,
    )
```

```python
import functools

import jax
import jax.numpy as jnp
from jax import lax
from jax.experimental import pallas as pl
from jax.experimental.pallas import tpu as pltpu
from jax.sharding import PartitionSpec as P

HEAD_DIM = 64
GROUP = 2
WRAP = 4
MESH = pl.DeviceIdType.MESH
EPSILON = 1e-06
FAR = 1e30
F32 = jnp.float32
BF16 = jnp.bfloat16
NN = (((1,), (0,)), ((), ()))
NT = (((1,), (1,)), ((), ()))
TN = (((0,), (0,)), ((), ()))


def dot(a, b, dims=NN):
    return lax.dot_general(a, b, dims, preferred_element_type=F32)


def row_mean(value):
    return jnp.sum(value, -1, keepdims=True) * (1.0 / value.shape[-1])


def normalise(x):
    center = x - row_mean(x)
    rate = lax.rsqrt(row_mean(center * center) + EPSILON)
    return center * rate, rate


def norm_back(grad, xhat, rate, gain):
    e = grad * gain
    return rate * (e - row_mean(e) - xhat * row_mean(e * xhat))


def gelu_parts(h):
    bell = jnp.exp(-0.5 * (h * h))
    t = 1.0 / (1.0 + 0.23164190 * jnp.abs(h))
    poly = t * (0.127414796 + t * (-0.142248368 + t * (0.7107068705 + t * (-0.7265760135 + t * 0.5307027145))))
    tail = poly * bell
    phi = jnp.where(h >= 0.0, 1.0 - tail, tail)
    return h * phi, phi + h * (bell * 0.3989422804014327)


def column_sum(value):
    return jnp.sum(value, 0, keepdims=True)


class Reduction:
    def __init__(
        self, f, hidden, tm, tm_count, masks, bit, across, others, sums, sends,
        r_core, r_one, r_two, r_tm, own_chunk, gathered, small, r_small, send_sems, recv_sems, local_sems,
    ):
        self.f, self.hidden, self.tm, self.tm_count = f, hidden, tm, tm_count
        self.masks, self.bit, self.across, self.others = masks, bit, across, others
        self.sums, self.sends = sums, sends
        self.r_core, self.r_one, self.r_two, self.r_tm = r_core, r_one, r_two, r_tm
        self.own_chunk, self.gathered, self.small, self.r_small = own_chunk, gathered, small, r_small
        self.send_sems, self.recv_sems, self.local_sems = send_sems, recv_sems, local_sems
        self.used, self.trades = 0, 0
        half = (len(masks) - 1) // 2
        self.extra = masks[2 : 1 + half] + masks[2 + half :]
        one, two = masks[1], masks[1 + half]
        wide = hidden // 2
        self.pieces = [
            (1, 0, hidden, one, two), (2, 0, hidden, two, one), (0, 0, wide, one, two), (0, wide, wide, two, one),
        ]
        self.core = {a: None for a in range(3)}

    def sem(self, n=1):
        at = self.used
        self.used += n
        return at

    def copy(self, src, dst, at, device):
        return pltpu.make_async_remote_copy(
            src_ref=src, dst_ref=dst, send_sem=self.send_sems.at[at], recv_sem=self.recv_sems.at[at],
            device_id=device, device_id_type=MESH,
        )

    def rows(self, at, count):
        return pl.ds(pl.multiple_of(at, 16), count)

    def start_core(self, arrays):
        count = self.f // 2
        away = self.rows((1 - self.bit[1]) * count, count)
        for a in arrays:
            self.sends[a][away, :] = self.sums[a][away, :].astype(BF16)
            copy = self.copy(self.sends[a].at[away, :], self.r_core.at[a], a, {"clip": self.across[1]})
            copy.start()

    def run(self, between):
        f = self.f
        self.used = 3
        halves = [f // 2, f // 4, f // 8]
        parts = self.tm_count
        groups = ((0, 1), (2, 3))

        def exchange_small(device):
            at = self.sem()
            slot = self.trades
            self.trades += 1
            copy = self.copy(self.small, self.r_small.at[slot], at, device)
            copy.start()
            return copy, slot

        def join_small(pair):
            copy, slot = pair
            copy.wait()
            self.small[...] += self.r_small[slot]

        def add(a, cols, at, count, got):
            where = self.rows(at, count)
            self.sums[a][where, cols] += got.astype(F32)

        base = self.bit[1] * halves[0]
        away = self.rows((1 - self.bit[1]) * halves[0], halves[0])
        bases = [base] * 4
        flying = {}

        def wait_core(arrays):
            for a in arrays:
                self.copy(self.sends[a].at[away, :], self.r_core.at[a], a, {"clip": self.across[1]}).wait()

        def start_half(level, members, boxes, which):
            count = halves[level]
            for i in members:
                a, c, n, *ms = self.pieces[i]
                m = ms[which]
                cols = slice(c, c + n)
                off = (1 - self.bit[m]) * count
                away = self.rows(bases[i] + off, count)
                if level == 1:
                    add(a, cols, bases[i] + off, count, self.r_core[a, self.rows(off, count), cols])
                self.sends[a][away, cols] = self.sums[a][away, cols].astype(BF16)
                copy = self.copy(
                    self.sends[a].at[away, cols], boxes.at[a, :, cols], self.sem(), {"clip": self.across[m]}
                )
                copy.start()
                flying[level, i] = copy
            for i in members:
                a, c, n, *ms = self.pieces[i]
                m = ms[which]
                cols = slice(c, c + n)
                off = self.bit[m] * count
                bases[i] = bases[i] + off
                if level == 1:
                    add(a, cols, bases[i], count, self.r_core[a, self.rows(off, count), cols])

        def end_half(level, members, boxes):
            for i in members:
                a, c, n, *ms = self.pieces[i]
                cols = slice(c, c + n)
                flying[level, i].wait()
                add(a, cols, bases[i], halves[level], boxes[a, :, cols])

        trading = exchange_small({"clip": self.across[1]})
        wait_core((1, 2))
        start_half(1, groups[0], self.r_one, 0)
        wait_core((0,))
        start_half(1, groups[1], self.r_one, 0)
        join_small(trading)
        trading = exchange_small({"clip": self.across[self.masks[1]]})
        between(0)
        end_half(1, groups[0], self.r_one)
        start_half(2, groups[0], self.r_two, 1)
        end_half(1, groups[1], self.r_one)
        start_half(2, groups[1], self.r_two, 1)
        join_small(trading)
        trading = exchange_small({"clip": self.across[self.pieces[0][4]]})
        between(1)
        end_half(2, groups[0], self.r_two)
        if not self.extra:
            self.start_quarters(0, bases)
        end_half(2, groups[1], self.r_two)
        if not self.extra:
            self.start_quarters(1, bases)
        join_small(trading)
        count = halves[2]
        for n_extra, m in enumerate(self.extra):
            trading = exchange_small({"clip": self.across[m]})
            sent = []
            for i, (a, c, n, *ms) in enumerate(self.pieces):
                cols = slice(c, c + n)
                here = self.rows(bases[i], count)
                box = self.own_chunk.at[1 + n_extra, a, :, cols]
                self.sends[a][here, cols] = self.sums[a][here, cols].astype(BF16)
                copy = self.copy(self.sends[a].at[here, cols], box, self.sem(), {"clip": self.across[m]})
                copy.start()
                sent.append((copy, box))
            for i, (a, c, n, *ms) in enumerate(self.pieces):
                copy, box = sent[i]
                copy.wait()
                cols = slice(c, c + n)
                here = self.rows(bases[i], count)
                self.sums[a][here, cols] = self.sends[a][here, cols].astype(F32) + box[...].astype(F32)
            join_small(trading)
        if self.extra:
            self.start_quarters(0, bases)
            self.start_quarters(1, bases)
        trading = exchange_small({"tm": self.tm + 1 - 2 * (self.tm % 2)})
        between(2)
        join_small(trading)
        trading = exchange_small({"tm": self.tm + 2 - 4 * (self.tm // 2)})
        self.settle_quarters(0)
        self.settle_quarters(1)
        join_small(trading)
        between(3)

        def start_back(level, members, which):
            count = halves[level]
            for i in members:
                a, c, n, *ms = self.pieces[i]
                m = ms[which]
                place = self.gathered.at[a, self.rows(bases[i], count), slice(c, c + n)]
                copy = self.copy(place, place, self.sem(), {"clip": self.across[m]})
                copy.start()
                flying[level, i] = copy
                bases[i] = bases[i] - self.bit[m] * count

        def end_back(level, members):
            for i in members:
                flying[level, i].wait()

        def start_core_back(arrays):
            for a in arrays:
                place = self.gathered.at[a, self.rows(base, halves[0]), :]
                copy = self.copy(place, place, self.sem(), {"clip": self.across[1]})
                copy.start()
                flying[0, a] = copy

        self.end_quarters(0)
        start_back(2, groups[0], 1)
        self.end_quarters(1)
        start_back(2, groups[1], 1)
        between(4)
        end_back(2, groups[0])
        start_back(1, groups[0], 0)
        end_back(2, groups[1])
        start_back(1, groups[1], 0)
        between(5)
        end_back(1, groups[0])
        start_core_back((1, 2))
        end_back(1, groups[1])
        start_core_back((0,))
        between(6)
        for a in range(3):
            flying[0, a].wait()

    def start_quarters(self, which, bases):
        if which == 0:
            self.chunks, self.departure = {}, {}
            parts = self.tm_count
            self.arrival = [self.sem(parts), self.sem(parts)]
            self.back = [self.sem(parts), self.sem(parts)]
            self.outgoing = [self.sem(parts), self.sem(parts)]
        for q in range(4):
            i = 2 * which + q // 2
            a, c, n = self.pieces[i][:3]
            n = n // 2
            cols = slice(c + (q % 2) * n, c + (q % 2) * n + n)
            here = self.rows(bases[i], self.f // 8)
            self.chunks[which, q] = (a, cols, here, n)
            self.departure[which, q] = self.sem()

            def send(which=which, q=q, a=a, cols=cols, here=here, n=n):
                self.sends[a][here, cols] = self.sums[a][here, cols].astype(BF16)
                self.chunk_copy(which, q, a, cols, here, n).start()

            pl.when(self.tm != q)(send)

    def settle_quarters(self, which):
        for q in range(4):
            a, cols, here, n = self.chunks[which, q]

            def settle(q=q, a=a, cols=cols, here=here, n=n):
                total = self.sums[a][here, cols]
                for other in range(self.tm_count):
                    if other != q:
                        box = self.r_tm.at[which, other, :, pl.ds(0, n)]
                        pltpu.make_async_copy(box, box, self.recv_sems.at[self.arrival[which] + other]).wait()
                        total += box[...].astype(F32)
                self.own_chunk[0, which, :, :n] = total.astype(BF16)
                self.publish(which, q, a, cols, here, n, "start")

            pl.when(self.tm == q)(settle)

    def end_quarters(self, which):
        for q in range(4):
            a, cols, here, n = self.chunks[which, q]

            def arrive(q=q, a=a, cols=cols, here=here, n=n):
                self.chunk_copy(which, q, a, cols, here, n).wait_send()
                place = self.gathered.at[a, here, cols]
                pltpu.make_async_copy(place, place, self.recv_sems.at[self.back[which] + q]).wait()

            def left(q=q, a=a, cols=cols, here=here, n=n):
                self.publish(which, q, a, cols, here, n, "wait")

            pl.when(self.tm != q)(arrive)
            pl.when(self.tm == q)(left)

    def chunk_copy(self, which, q, a, cols, here, n):
        return pltpu.make_async_remote_copy(
            src_ref=self.sends[a].at[here, cols], dst_ref=self.r_tm.at[which, self.tm, :, pl.ds(0, n)],
            send_sem=self.send_sems.at[self.departure[which, q]], recv_sem=self.recv_sems.at[self.arrival[which] + self.tm],
            device_id={"tm": q}, device_id_type=MESH,
        )

    def publish(self, which, q, a, cols, here, n, do):
        place = self.gathered.at[a, here, cols]
        chunk = self.own_chunk.at[0, which, :, pl.ds(0, n)]
        local = pltpu.make_async_copy(chunk, place, self.local_sems.at[which])
        local.start() if do == "start" else local.wait()
        for other in range(self.tm_count):
            if other != q:
                copy = pltpu.make_async_remote_copy(
                    src_ref=chunk, dst_ref=place, send_sem=self.send_sems.at[self.outgoing[which] + other],
                    recv_sem=self.recv_sems.at[self.back[which] + q], device_id={"tm": other}, device_id_type=MESH,
                )
                copy.start() if do == "start" else copy.wait_send()


def layer_kernel(
    lanes, spatial, features, hidden, tm_count, clip_count,
    frames_ref, tok_ref, cot_ref,
    pre_gain_ref, pre_bias_ref, w_project_ref, query_bias_ref, value_bias_ref,
    w_out_ref, out_bias_ref, mid_gain_ref, mid_bias_ref, w_up_ref, up_bias_ref, w_down_ref, down_bias_ref,
    out_ref, own_ref, gathered_ref, total_small_ref,
    a_w, a_up, a_down, a_small, a_upb, low_s, up_s, gl_s, gu_s, above_s, below_s, n1_s, k_s, v_s, kt_s, vt_s, qt_s, p_s, inv_s, att_s, attt_s, res_s, n2_s, act_s, gh_s,
    dao_s, dres_s, dq_s, dkv_s, dt_s,
    send_up, send_down, recv_low, recv_up, send_gl, send_gu, recv_above, recv_below,
    s_w, r_core, r_one, r_two, r_tm, own_chunk, r_small, ar_send, ar_recv, ar_local,
):
    f = features
    pad = n1_s.shape[1] // GROUP
    heads = f // HEAD_DIM
    tm = lax.axis_index("tm")
    last = tm_count - 1
    at_low, at_high = tm == 0, tm == last
    higher, lower = lax.rem(tm + 1, tm_count), lax.rem(tm + last, tm_count)
    step_up, step_down = (tm + 1) // tm_count, (tm_count - tm) // tm_count

    def row(ref):
        return ref[...].astype(F32).reshape(1, -1)

    pre_gain, pre_bias, mid_gain, mid_bias = row(pre_gain_ref), row(pre_bias_ref), row(mid_gain_ref), row(mid_bias_ref)
    out_bias, down_bias, up_bias = row(out_bias_ref), row(down_bias_ref), row(up_bias_ref)
    query_bias, value_bias = row(query_bias_ref), row(value_bias_ref)

    def full_lane(l):
        return frames_ref[l] > 0

    def joined(l):
        frames = frames_ref[l]
        inner_low = ((frames == 4 * tm_count) & (l % 2 > 0)) | ((frames == 8 * tm_count) & (l % 4 > 0))
        inner_up = ((frames == 4 * tm_count) & (l % 2 < 1)) | ((frames == 8 * tm_count) & (l % 4 < 3))
        return (frames > 0) & (inner_low | (tm > 0)), (frames > 0) & (inner_up | (tm < last))

    def has_low(l):
        return jnp.logical_or(tm > 0, lax.rem(l, WRAP) != 0)

    def has_up(l):
        return jnp.logical_or(tm < last, lax.rem(l, WRAP) != WRAP - 1)

    def copy(src, dst, send, recv, device):
        return pltpu.make_async_remote_copy(
            src_ref=src, dst_ref=dst, send_sem=send, recv_sem=recv, device_id={"tm": device}, device_id_type=MESH
        )

    def rising(l):
        return copy(gl_s.at[l], low_s.at[l + step_up], send_up.at[l], recv_low.at[l + step_up], higher)

    def falling(l):
        return copy(gl_s.at[l], up_s.at[l - step_down], send_down.at[l], recv_up.at[l - step_down], lower)

    def returning_low(l):
        return copy(gl_s.at[l], above_s.at[l - step_down], send_gl.at[l], recv_above.at[l - step_down], lower)

    def returning_up(l):
        return copy(gu_s.at[l], below_s.at[l + step_up], send_gu.at[l], recv_below.at[l + step_up], higher)

    clip = lax.axis_index("clip")
    masks = [1 << i for i in range((clip_count - 1).bit_length())]
    bit = {m: (clip // m) % 2 for m in masks}
    across = {m: clip + m * (1 - 2 * bit[m]) for m in masks}
    others = [lax.rem(tm + i, tm_count) for i in range(1, tm_count)]

    barrier = pltpu.get_barrier_semaphore()
    for device in others:
        pl.semaphore_signal(barrier, inc=1, device_id={"tm": device}, device_id_type=MESH)
    for m in masks:
        pl.semaphore_signal(barrier, inc=1, device_id={"clip": across[m]}, device_id_type=MESH)
    pl.semaphore_wait(barrier, len(others) + len(masks))

    def start_tokens(l, carry):
        xhat, _ = normalise(tok_ref[0, l].astype(F32))
        gl_s[l] = (xhat * pre_gain + pre_bias).astype(BF16)
        pl.when(has_up(l))(lambda: rising(l).start())
        pl.when(has_low(l))(lambda: falling(l).start())
        return carry

    lax.fori_loop(0, lanes, start_tokens, 0)

    def fill(l, carry):
        @pl.when(jnp.logical_not(has_low(l)))
        def _():
            low_s[l] = jnp.zeros(low_s.shape[1:], BF16)
            below_s[l] = jnp.zeros(low_s.shape[1:], BF16)

        @pl.when(jnp.logical_not(has_up(l)))
        def _():
            up_s[l] = jnp.zeros(up_s.shape[1:], BF16)
            above_s[l] = jnp.zeros(up_s.shape[1:], BF16)

        return carry

    lax.fori_loop(0, lanes, fill, 0)

    for new in (a_w, a_up, a_down, a_small, a_upb):
        new[...] = jnp.zeros_like(new)

    def rows_of(j):
        return pl.ds(pl.multiple_of(j * pad, pad), spatial)

    for ref in (n1_s, att_s, dao_s, dq_s, dkv_s, res_s, dres_s):
        for j in range(GROUP):
            if len(ref.shape) == 3:
                ref[:, pl.ds(j * pad + pad - 16, 16), :] = jnp.zeros((ref.shape[0], 16, ref.shape[2]), ref.dtype)
            else:
                ref[pl.ds(j * pad + pad - 16, 16), :] = jnp.zeros((16, ref.shape[1]), ref.dtype)

    sums = Reduction(
        f, hidden, tm, tm_count, masks, bit, across, others, (a_w, a_up, a_down), (s_w, act_s.at[pl.ds(0, f), :], gh_s.at[pl.ds(0, f), :]),
        r_core, r_one, r_two, r_tm, own_chunk, gathered_ref, a_small, r_small, ar_send, ar_recv, ar_local,
    )

    def group(index, carry):
        base = index * GROUP

        def arrive(j, carry):
            l = base + j
            pl.when(has_low(l))(lambda: copy(gl_s.at[l], low_s.at[l], send_up.at[l], recv_low.at[l], lower).wait_recv())
            pl.when(has_up(l))(lambda: copy(gl_s.at[l], up_s.at[l], send_down.at[l], recv_up.at[l], higher).wait_recv())
            return carry

        lax.fori_loop(0, GROUP, arrive, 0)

        def forward(j, carry):
            for s, n1 in enumerate((low_s[base + j], gl_s[base + j], up_s[base + j])):
                n1_s[s, rows_of(j), :] = n1
                kv = dot(n1, w_project_ref[:, f:])
                k = kv[:, :f].astype(BF16)
                v = (kv[:, f:] + value_bias).astype(BF16)
                k_s[s, j] = k
                v_s[s, j] = v
                kt_s[s, j] = k.T
                vt_s[s, j] = v.T
                if s == 1:
                    q = (dot(n1, w_project_ref[:, :f]) + query_bias).astype(BF16)
                    qt_s[j] = (q * jnp.asarray(HEAD_DIM ** (-0.5), BF16)).T
            low_ok, up_ok = joined(base + j)
            low_far, up_far = jnp.where(low_ok, 0.0, FAR), jnp.where(up_ok, 0.0, FAR)
            zero_half = jnp.zeros((HEAD_DIM, spatial), BF16)
            def get_scores(h):
                pair = slice(h // 2 * 2 * HEAD_DIM, (h // 2 + 1) * 2 * HEAD_DIM)
                qh = qt_s[j, h * HEAD_DIM : (h + 1) * HEAD_DIM, :]
                qz = jnp.concatenate([qh, zero_half] if h % 2 == 0 else [zero_half, qh], 0)
                return [dot(k_s[s, j, :, pair], qz) for s in range(3)]

            later = get_scores(0)
            for h in range(heads):
                mine = slice(h * HEAD_DIM, (h + 1) * HEAD_DIM)
                scores = later
                if h + 1 < heads:
                    later = get_scores(h + 1)
                tops = [jnp.max(x, 0, keepdims=True) for x in scores]
                top = jnp.maximum(jnp.maximum(tops[0] - low_far, tops[2] - up_far), tops[1])
                total, attended = None, None
                for s, shift in enumerate((top + low_far, top, top + up_far)):
                    prob = jnp.exp(scores[s] - shift)
                    part = column_sum(prob)
                    total = part if total is None else total + part
                    low_prob = prob.astype(BF16)
                    p_s[j, h, s] = low_prob
                    got = dot(vt_s[s, j, mine, :], low_prob)
                    attended = got if attended is None else attended + got
                inverse = 1.0 / total
                inv_s[j, h : h + 1, :] = inverse
                attt_s[j, mine, :] = (attended * inverse).astype(BF16)
            att_s[rows_of(j), :] = attt_s[j].T
            res_s[rows_of(j), :] = tok_ref[0, base + j].astype(F32)
            return carry

        for j in range(GROUP):
            forward(j, 0)

        residual = res_s[...] + dot(att_s[...], w_out_ref[...]) + out_bias
        res_s[...] = residual
        xhat2, rate2 = normalise(residual)
        n2_s[...] = (xhat2 * mid_gain + mid_bias).astype(BF16)
        for j in range(GROUP):
            full = full_lane(base + j)
            g = cot_ref[0, base + j]
            dao_s[pl.ds(j * pad, spatial), :] = jnp.where(full, g.astype(F32), 0.0).astype(BF16)

        wide = 256

        def mlp(c, carry):
            cols = pl.ds(pl.multiple_of(c * wide, wide), wide)
            h = dot(n2_s[...], w_up_ref[:, cols]) + up_bias[:, c * wide : (c + 1) * wide]
            act, slope = gelu_parts(h)
            act_s[:, cols] = act.astype(BF16)
            gh = (dot(dao_s[...], w_down_ref[cols, :], NT) * slope).astype(BF16)
            gh_s[:, cols] = gh
            a_upb[:, cols] += column_sum(gh.astype(F32))
            return carry

        for c in range(hidden // wide):
            mlp(c, 0)
        a_up[...] += dot(n2_s[...], gh_s[...], TN)
        a_down[...] += dot(dao_s[...], act_s[...], TN)
        total_out = dot(act_s[...], w_down_ref[...]) + down_bias + res_s[...]
        grad_n2 = dot(gh_s[...], w_up_ref[...], NT)
        pl.when(index == lanes // GROUP - 1)(lambda: sums.start_core((1, 2)))
        for j in range(GROUP):
            full = full_lane(base + j)
            mine = total_out[j * pad : j * pad + spatial]
            out_ref[0, base + j] = jnp.where(full, mine, tok_ref[0, base + j].astype(F32)).astype(BF16)
        g = dao_s[...].astype(F32)
        xhat2, rate2 = normalise(res_s[...])
        dres = g + norm_back(grad_n2, xhat2, rate2, mid_gain)
        dres_s[...] = dres
        dao = dres.astype(BF16)
        dao_s[...] = dao
        a_small[3:4, :] += column_sum(dao.astype(F32))
        a_small[4:5, :] += column_sum(grad_n2 * xhat2)
        a_small[5:6, :] += column_sum(grad_n2)
        a_small[6:7, :] += column_sum(g)
        a_w[:, 3 * f :] += dot(att_s[...], dao, TN)

        def backward(j, carry):
            dot_rows = dao_s[rows_of(j), :]
            dt = dot(w_out_ref[...], dot_rows, NT).astype(BF16)
            zero_half = jnp.zeros((HEAD_DIM, spatial), BF16)
            def prepare(h):
                pair = slice(h // 2 * 2 * HEAD_DIM, (h // 2 + 1) * 2 * HEAD_DIM)
                mine = slice(h * HEAD_DIM, (h + 1) * HEAD_DIM)
                dh = dt[mine, :].astype(F32) * inv_s[j, h : h + 1, :]
                delta = column_sum(dh * attt_s[j, mine, :].astype(F32))
                dh = dh.astype(BF16)
                dz = jnp.concatenate([dh, zero_half] if h % 2 == 0 else [zero_half, dh], 0)
                return dh, delta, [dot(v_s[s, j, :, pair], dz) for s in range(3)]

            later = prepare(0)
            for h in range(heads):
                mine = slice(h * HEAD_DIM, (h + 1) * HEAD_DIM)
                dh, delta, grad_probs = later
                if h + 1 < heads:
                    later = prepare(h + 1)
                qh = qt_s[j, mine, :]
                probs = [p_s[j, h, s] for s in range(3)]
                for s in range(3):
                    dt_s[4 + s, mine, :] = dot(dh, probs[s], NT).astype(BF16)
                ds = [(probs[s].astype(F32) * (grad_probs[s] - delta)).astype(BF16) for s in range(3)]
                for s in range(3):
                    dt_s[1 + s, mine, :] = dot(qh, ds[s], NT).astype(BF16)
                grad_q = None
                for s in range(3):
                    got = dot(kt_s[s, j, mine, :], ds[s])
                    grad_q = got if grad_q is None else grad_q + got
                dt_s[0, mine, :] = (grad_q * HEAD_DIM ** (-0.5)).astype(BF16)
            dq_s[rows_of(j), :] = dt_s[0].T
            for s in range(3):
                dkv_s[s, rows_of(j), :f] = dt_s[1 + s].T
                dkv_s[s, rows_of(j), f:] = dt_s[4 + s].T
            return carry

        for j in range(GROUP):
            backward(j, 0)

        dq = dq_s[...]
        a_w[:, :f] += dot(n1_s[1], dq, TN)
        a_small[2:3, :] += column_sum(dq.astype(F32))
        dkv = dkv_s[...].reshape(3 * GROUP * pad, 2 * f)
        a_w[:, f : 3 * f] += dot(n1_s[...].reshape(3 * GROUP * pad, f), dkv, TN)
        a_small[7:8, :] += column_sum(dkv[:, f:].astype(F32))

        def finish(j, carry):
            l = base + j
            pl.when(has_up(l))(lambda: rising(l).wait_send())
            pl.when(has_low(l))(lambda: falling(l).wait_send())
            for s, box in enumerate((gl_s, low_s, gu_s)):
                grad = dot(dkv_s[s, rows_of(j), :], w_project_ref[:, f:], NT)
                if s == 1:
                    grad += dot(dq_s[rows_of(j), :], w_project_ref[:, :f], NT)
                a_small[0:1, :] += column_sum(grad * n1_s[s, rows_of(j), :].astype(F32))
                a_small[1:2, :] += column_sum(grad)
                box[l] = grad.astype(BF16)
            straight = jnp.where(full_lane(l), 0.0, cot_ref[0, l].astype(F32))
            own_ref[0, l] = (dres_s[rows_of(j), :] + straight).astype(BF16)
            return carry

        for j in range(GROUP):
            finish(j, 0)

        def give_back(j, carry):
            l = base + j
            pl.when(has_low(l))(lambda: returning_low(l).start())
            pl.when(has_up(l))(lambda: returning_up(l).start())
            return carry

        lax.fori_loop(0, GROUP, give_back, 0)
        return carry

    lax.fori_loop(0, lanes // GROUP, group, 0)
    def conclude(l, carry):
        @pl.when(has_up(l))
        def _():
            returning_up(l).wait_send()
            copy(gl_s.at[l], above_s.at[l], send_gl.at[l], recv_above.at[l], higher).wait_recv()

        @pl.when(has_low(l))
        def _():
            returning_low(l).wait_send()
            copy(gu_s.at[l], below_s.at[l], send_gu.at[l], recv_below.at[l], lower).wait_recv()

        grad = low_s[l].astype(F32) + above_s[l].astype(F32) + below_s[l].astype(F32)
        xhat, rate = normalise(tok_ref[0, l].astype(F32))
        own_ref[0, l] = (norm_back(grad, xhat, rate, pre_gain) + own_ref[0, l].astype(F32)).astype(BF16)
        return carry

    bounds = [0] + [lanes * k // 16 for k in (4, 6, 8, 10, 12, 13, 14)] + [lanes]

    def between(step):
        lax.fori_loop(bounds[step], bounds[step + 1], conclude, 0)

    for i in range(hidden // f):
        a_small[8 + i : 9 + i, :] = a_upb[:, i * f : (i + 1) * f]
    sums.start_core((0,))
    sums.run(between)
    between(7)
    total_small_ref[...] = a_small[...]
    total_small_ref[0:1, :] = (a_small[0:1, :] - pre_bias * a_small[1:2, :]) / pre_gain


def unpack_kernel(in_ref, project_ref, out_ref, up_ref, down_ref):
    f = out_ref.shape[1]
    project_ref[...] = in_ref[0, :, : 3 * f].astype(F32)
    out_ref[...] = in_ref[0, :, 3 * f :].astype(F32)
    up_ref[...] = in_ref[1].astype(F32)
    down_ref[...] = in_ref[2].astype(F32).T


def layer_call(lanes, spatial, f, hidden, tm_count, clip_count, frames, tokens, cotangent, weights):
    pad = -(-spatial // 16) * 16
    rows = GROUP * pad
    smem = pl.BlockSpec(memory_space=pltpu.SMEM)
    vmem = pl.BlockSpec(memory_space=pltpu.VMEM)
    hbm = pl.BlockSpec(memory_space=pl.ANY)
    masks = (clip_count - 1).bit_length()
    extra = masks - 3
    sums = [pltpu.VMEM(s, F32) for s in [(f, hidden)] * 3 + [(16, f), (1, hidden)]]
    whole = jax.ShapeDtypeStruct((1, lanes, spatial, f), BF16)
    lane = lambda *s: pltpu.VMEM(s, BF16)
    dma = pltpu.SemaphoreType.DMA((lanes,))
    scratch = sums + [
        lane(lanes, spatial, f), lane(lanes, spatial, f), lane(lanes, spatial, f), lane(lanes, spatial, f),
        lane(lanes, spatial, f), lane(lanes, spatial, f),
        lane(3, rows, f), lane(3, GROUP, spatial, f), lane(3, GROUP, spatial, f),
        lane(3, GROUP, f, spatial), lane(3, GROUP, f, spatial), lane(GROUP, f, spatial),
        lane(GROUP, f // HEAD_DIM, 3, spatial, spatial), pltpu.VMEM((GROUP, 8, spatial), F32),
        lane(rows, f), lane(GROUP, f, spatial), pltpu.VMEM((rows, f), F32), lane(rows, f),
        lane(rows, hidden), lane(rows, hidden), lane(rows, f), pltpu.VMEM((rows, f), F32),
        lane(rows, f), lane(3, rows, 2 * f), lane(7, f, spatial),
    ] + [dma] * 8
    sems = pltpu.SemaphoreType.DMA((96,))
    scratch += [
        lane(f, hidden), lane(3, f // 2, hidden), lane(3, f // 4, hidden),
        lane(3, f // 8, hidden), lane(2, tm_count, f // 8, hidden // 2), lane(1 + extra, 3, f // 8, hidden),
        pltpu.VMEM((masks + 2, 16, f), F32), sems, sems, pltpu.SemaphoreType.DMA((2,)),
    ]
    return pl.pallas_call(
        functools.partial(layer_kernel, lanes, spatial, f, hidden, tm_count, clip_count),
        in_specs=[smem] + [vmem] * (2 + len(weights)),
        out_specs=[vmem, vmem, hbm, vmem],
        out_shape=[whole] * 2 + [jax.ShapeDtypeStruct((3, f, hidden), BF16), jax.ShapeDtypeStruct((16, f), F32)],
        scratch_shapes=scratch,
        name="layer",
        compiler_params=pltpu.CompilerParams(
            vmem_limit_bytes=63 * 1024 * 1024, collective_id=0, has_side_effects=True
        ),
        cost_estimate=pl.CostEstimate(flops=100 * 10**9, bytes_accessed=40 * 10**6, transcendentals=0),
    )(frames, tokens, cotangent, *weights)


def body(
    tokens, cotangent, lane_frames, pre_gain, pre_bias, w_project, query_bias, value_bias,
    w_out, out_bias, mid_gain, mid_bias, w_up, up_bias, w_down, down_bias,
):
    lanes, spatial, f = tokens.shape[1:]
    hidden = w_up.shape[1]
    tm_count = lax.axis_size("tm")
    weights = (
        pre_gain, pre_bias, w_project, query_bias, value_bias, w_out, out_bias,
        mid_gain, mid_bias, w_up, up_bias, w_down, down_bias,
    )
    out, input_grad, gathered, small = layer_call(
        lanes, spatial, f, hidden, tm_count, lax.axis_size("clip"), lane_frames, tokens, cotangent, weights
    )
    tall = 128
    wide_block = lambda n: pl.BlockSpec((tall, n), lambda i: (i, 0))
    g_project, g_out, g_up, g_down = pl.pallas_call(
        unpack_kernel,
        grid=(f // tall,),
        in_specs=[pl.BlockSpec((3, tall, hidden), lambda i: (0, i, 0))],
        out_specs=[wide_block(3 * f), wide_block(f), wide_block(hidden), pl.BlockSpec((hidden, tall), lambda i: (0, i))],
        out_shape=[jax.ShapeDtypeStruct(n, F32) for n in ((f, 3 * f), (f, f), (f, hidden), (hidden, f))],
        name="unpack",
    )(gathered)
    g_small, g_upb = small[:8], small[8 : 8 + hidden // f].reshape(hidden)
    return (
        out, input_grad, g_small[0], g_small[1], g_project, g_small[2], g_small[7], g_out, g_small[3],
        g_small[4], g_small[5], g_up, g_upb, g_down, g_small[6],
    )


def solution(mesh):
    spread = P("tm", "clip", None, None)
    return jax.shard_map(
        body,
        mesh=mesh,
        in_specs=(spread, spread, P("clip")) + (P(),) * 13,
        out_specs=(spread, spread) + (P(),) * 13,
        check_vma=False,
    )
```

```python
import functools

import jax
import jax.numpy as jnp
from jax import lax
from jax.experimental import pallas as pl
from jax.experimental.pallas import tpu as pltpu
from jax.sharding import PartitionSpec as P

HEAD_DIM = 64
GROUP = 2
WRAP = 4
MESH = pl.DeviceIdType.MESH
EPSILON = 1e-06
FAR = 1e30
F32 = jnp.float32
BF16 = jnp.bfloat16
NN = (((1,), (0,)), ((), ()))
NT = (((1,), (1,)), ((), ()))
TN = (((0,), (0,)), ((), ()))


def dot(a, b, dims=NN):
    return lax.dot_general(a, b, dims, preferred_element_type=F32)


def row_mean(value):
    return jnp.sum(value, -1, keepdims=True) * (1.0 / value.shape[-1])


def normalise(x):
    center = x - row_mean(x)
    rate = lax.rsqrt(row_mean(center * center) + EPSILON)
    return center * rate, rate


def norm_back(grad, xhat, rate, gain):
    e = grad * gain
    return rate * (e - row_mean(e) - xhat * row_mean(e * xhat))


def gelu_parts(h):
    size = jnp.abs(h)
    bell = jnp.exp(-0.5 * (h * h))
    whole = 1.0 + 0.23164190 * size
    t = pl.reciprocal(whole, approx=True)
    t = t * (2.0 - whole * t)
    poly = t * (0.127414796 + t * (-0.142248368 + t * (0.7107068705 + t * (-0.7265760135 + t * 0.5307027145))))
    tail = poly * bell
    phi = jnp.where(h >= 0.0, 1.0 - tail, tail)
    return jnp.maximum(h, 0.0) - size * tail, phi + h * (bell * 0.3989422804014327)


def column_sum(value):
    return jnp.sum(value, 0, keepdims=True)


UP, DOWN, W = 1, 2, 0
LATE = 1
TALL = 128
TAIL = [(W, 0), ("trade", 0), ("lanes", 2), (UP, 3), (DOWN, 3), ("give",), (W, 1), ("trade", 1), ("lanes", 3), (W, 2), ("trade", 2), (UP, 4), (DOWN, 4), (W, 3), ("trade", 3), (UP, 5), (DOWN, 5), (W, 4), ("trade", 4), ("lanes", 4), (UP, 6), (DOWN, 6), ("trade", 5), (W, 5), (UP, 7), (DOWN, 7), (W, 6), (W, 7), ("lanes", 6), (UP, 8), (DOWN, 8), (W, 8)]


class Reduction:
    def __init__(
        self, f, hidden, tm, tm_count, masks, bit, across, sums, sends,
        r_core, r_one, r_two, r_more, r_tm, own_chunk, gathered, small, r_small, send_sems, recv_sems, local_sems,
    ):
        self.f, self.hidden, self.tm, self.tm_count = f, hidden, tm, tm_count
        self.masks, self.bit, self.across = masks, bit, across
        self.sums, self.sends = sums, sends
        self.r_core, self.r_one, self.r_two, self.r_more, self.r_tm = r_core, r_one, r_two, r_more, r_tm
        self.own_chunk, self.gathered, self.small, self.r_small = own_chunk, gathered, small, r_small
        self.send_sems, self.recv_sems, self.local_sems = send_sems, recv_sems, local_sems
        half = (len(masks) - 1) // 2
        self.more = masks[2 : 1 + half] + masks[2 + half :]
        one, two = masks[1], masks[1 + half]
        wide = hidden // 2
        self.pieces = [(slice(0, wide), one, two), (slice(wide, hidden), two, one)]
        self.core = bit[1] * (f // 2)
        self.level_one = [self.core + bit[m] * (f // 4) for _, m, _ in self.pieces]
        self.level_two = [at + bit[m] * (f // 8) for at, (_, _, m) in zip(self.level_one, self.pieces)]
        self.used, self.known, self.flying = 0, {}, {}

    def sem(self, name, n=1):
        if name not in self.known:
            self.known[name] = self.used
            self.used += n
        return self.known[name]

    def copy(self, name, src, dst, device):
        at = self.sem(name)
        return pltpu.make_async_remote_copy(
            src_ref=src, dst_ref=dst, send_sem=self.send_sems.at[at], recv_sem=self.recv_sems.at[at],
            device_id=device, device_id_type=MESH,
        )

    def rows(self, at, count):
        return pl.ds(pl.multiple_of(at, 16), count)

    def add(self, a, cols, at, count, got):
        where = self.rows(at, count)
        self.sums[a][where, cols] += got.astype(F32)

    def core_copy(self, a):
        count = self.f // 2
        away = self.rows((1 - self.bit[1]) * count, count)
        return self.copy(("core", a), self.sends[a].at[away, :], self.r_core.at[a], {"clip": self.across[1]})

    def half_copy(self, level, a, i):
        cols, *ms = self.pieces[i]
        count = self.f // (4 * level)
        m = ms[level - 1]
        start = self.core if level == 1 else self.level_one[i]
        away = self.rows(start + (1 - self.bit[m]) * count, count)
        box = (self.r_one, self.r_two)[level - 1]
        return self.copy(
            ("half", level, a, i), self.sends[a].at[away, cols], box.at[a, :, cols], {"clip": self.across[m]}
        )

    def start_half(self, level, a):
        count = self.f // (4 * level)
        for i, (cols, *ms) in enumerate(self.pieces):
            m = ms[level - 1]
            off = (1 - self.bit[m]) * count
            start = self.core if level == 1 else self.level_one[i]
            if level == 1:
                self.add(a, cols, start + off, count, self.r_core[a, self.rows(off, count), cols])
            away = self.rows(start + off, count)
            self.sends[a][away, cols] = self.sums[a][away, cols].astype(BF16)
            self.half_copy(level, a, i).start()
        if level == 1:
            for i, (cols, m, _) in enumerate(self.pieces):
                off = self.bit[m] * count
                self.add(a, cols, self.core + off, count, self.r_core[a, self.rows(off, count), cols])

    def end_half(self, level, a):
        count = self.f // (4 * level)
        for i, (cols, *_) in enumerate(self.pieces):
            self.half_copy(level, a, i).wait()
            at = (self.level_one, self.level_two)[level - 1][i]
            self.add(a, cols, at, count, (self.r_one, self.r_two)[level - 1][a, :, cols])

    def chunk(self, q):
        n = self.hidden // 4
        return slice(q * n, (q + 1) * n), self.rows(self.level_two[q // 2], self.f // 8)

    def chunk_copy(self, a, q):
        cols, here = self.chunk(q)
        return pltpu.make_async_remote_copy(
            src_ref=self.sends[a].at[here, cols], dst_ref=self.r_tm.at[a, self.tm],
            send_sem=self.send_sems.at[self.sem(("leave", a, q))],
            recv_sem=self.recv_sems.at[self.sem(("meet", a), self.tm_count) + self.tm],
            device_id={"tm": q}, device_id_type=MESH,
        )

    def publish(self, a, q, do):
        cols, here = self.chunk(q)
        place, mine = self.gathered.at[a, here, cols], self.own_chunk.at[a]
        local = pltpu.make_async_copy(mine, place, self.local_sems.at[a])
        local.start() if do == "start" else local.wait()
        for other in range(self.tm_count):
            if other != q:
                copy = pltpu.make_async_remote_copy(
                    src_ref=mine, dst_ref=place, send_sem=self.send_sems.at[self.sem(("out", a), self.tm_count) + other],
                    recv_sem=self.recv_sems.at[self.sem(("back", a), self.tm_count) + q],
                    device_id={"tm": other}, device_id_type=MESH,
                )
                copy.start() if do == "start" else copy.wait_send()

    def back_copy(self, level, a, i):
        cols, *ms = self.pieces[i]
        at, count = (self.level_two, self.level_one)[2 - level][i], self.f // (4 * level)
        place = self.gathered.at[a, self.rows(at, count), cols]
        return self.copy(("return", level, a, i), place, place, {"clip": self.across[ms[level - 1]]})

    def core_back(self, a):
        place = self.gathered.at[a, self.rows(self.core, self.f // 2), :]
        return self.copy(("core back", a), place, place, {"clip": self.across[1]})

    def step(self, a, n):
        if n == 0:
            count = self.f // 2
            away = self.rows((1 - self.bit[1]) * count, count)
            self.sends[a][away, :] = self.sums[a][away, :].astype(BF16)
            self.core_copy(a).start()
        elif n == 1:
            self.core_copy(a).wait()
            self.start_half(1, a)
        elif n == 2:
            self.end_half(1, a)
            self.start_half(2, a)
        elif n == 3:
            self.end_half(2, a)
            count = self.f // 8
            for k, m in enumerate(self.more):
                for i, (cols, *_) in enumerate(self.pieces):
                    here = self.rows(self.level_two[i], count)
                    box = self.r_more.at[k, a, :, cols]
                    self.sends[a][here, cols] = self.sums[a][here, cols].astype(BF16)
                    copy = self.copy(("more", k, a, i), self.sends[a].at[here, cols], box, {"clip": self.across[m]})
                    copy.start()
                    copy.wait()
                    self.sums[a][here, cols] = self.sends[a][here, cols].astype(F32) + box[...].astype(F32)
            for q in range(4):

                def send(q=q):
                    cols, here = self.chunk(q)
                    self.sends[a][here, cols] = self.sums[a][here, cols].astype(BF16)
                    self.chunk_copy(a, q).start()

                pl.when(self.tm != q)(send)
        elif n == 4:
            for q in range(4):

                def settle(q=q):
                    cols, here = self.chunk(q)
                    total = self.sums[a][here, cols]
                    for other in range(self.tm_count):
                        if other != q:
                            box = self.r_tm.at[a, other]
                            at = self.sem(("meet", a), self.tm_count) + other
                            pltpu.make_async_copy(box, box, self.recv_sems.at[at]).wait()
                            total += box[...].astype(F32)
                    self.own_chunk[a] = total.astype(BF16)
                    self.publish(a, q, "start")

                pl.when(self.tm == q)(settle)
        elif n == 5:
            for q in range(4):

                def arrive(q=q):
                    self.chunk_copy(a, q).wait_send()
                    cols, here = self.chunk(q)
                    place = self.gathered.at[a, here, cols]
                    at = self.sem(("back", a), self.tm_count) + q
                    pltpu.make_async_copy(place, place, self.recv_sems.at[at]).wait()

                pl.when(self.tm != q)(arrive)
                pl.when(self.tm == q)(functools.partial(self.publish, a, q, "wait"))
            for i in range(2):
                self.back_copy(2, a, i).start()
        elif n == 6:
            for i in range(2):
                self.back_copy(2, a, i).wait()
            for i in range(2):
                self.back_copy(1, a, i).start()
        elif n == 7:
            for i in range(2):
                self.back_copy(1, a, i).wait()
            self.core_back(a).start()
        else:
            self.core_back(a).wait()

    def trade(self, k, do):
        if k < len(self.masks):
            device = {"clip": self.across[self.masks[k]]}
        else:
            m = 1 << (k - len(self.masks))
            device = {"tm": self.tm + m - 2 * m * ((self.tm // m) % 2)}
        copy = self.copy(("small", k), self.small, self.r_small.at[k], device)
        if do == "start":
            copy.start()
        else:
            copy.wait()
            self.small[...] += self.r_small[k]

    def trades(self):
        return len(self.masks) + (self.tm_count - 1).bit_length()


def layer_kernel(
    lanes, spatial, features, hidden, tm_count, clip_count,
    frames_ref, tok_hbm, cot_hbm,
    pre_gain_ref, pre_bias_ref, w_project_hbm, query_bias_ref, value_bias_ref,
    w_out_hbm, out_bias_ref, mid_gain_ref, mid_bias_ref, w_up_hbm, up_bias_ref, w_down_hbm, down_bias_ref,
    out_hbm, own_ref, gathered_ref, total_small_ref,
    a_w, a_up, a_down, a_small, a_upb, low_s, up_s, gl_s, above_s, below_s, raw_s, tok_s, cot_s, out_s,
    w_project_ref, w_out_ref, w_up_ref, w_down_ref, n1_s, k_s, v_s, kt_s, vt_s, qt_s, p_s, inv_s, att_s, attt_s, res_s, n2_s, act_s, gh_s,
    dao_s, dq_s, dkv_s, dt_s,
    send_up, send_down, recv_low, recv_up, send_gl, send_gu, recv_above, recv_below,
    raw_sems, weight_sems, out_sems, s_w, r_core, r_one, r_two, r_more, r_tm, own_chunk, r_small, ar_send, ar_recv, ar_local,
):
    f = features
    pad = n1_s.shape[2] // GROUP
    heads = f // HEAD_DIM
    tm = lax.axis_index("tm")
    last = tm_count - 1
    at_low, at_high = tm == 0, tm == last
    higher, lower = lax.rem(tm + 1, tm_count), lax.rem(tm + last, tm_count)
    step_up, step_down = (tm + 1) // tm_count, (tm_count - tm) // tm_count

    def row(ref):
        return ref[...].astype(F32).reshape(1, -1)

    pre_gain, pre_bias, mid_gain, mid_bias = row(pre_gain_ref), row(pre_bias_ref), row(mid_gain_ref), row(mid_bias_ref)
    out_bias, down_bias, up_bias = row(out_bias_ref), row(down_bias_ref), row(up_bias_ref)
    query_bias, value_bias = row(query_bias_ref), row(value_bias_ref)

    def full_lane(l):
        return frames_ref[l] > 0

    def joined(l):
        frames = frames_ref[l]
        inner_low = ((frames == 4 * tm_count) & (l % 2 > 0)) | ((frames == 8 * tm_count) & (l % 4 > 0))
        inner_up = ((frames == 4 * tm_count) & (l % 2 < 1)) | ((frames == 8 * tm_count) & (l % 4 < 3))
        return (frames > 0) & (inner_low | (tm > 0)), (frames > 0) & (inner_up | (tm < last))

    def has_low(l):
        return jnp.logical_or(tm > 0, lax.rem(l, WRAP) != 0)

    def has_up(l):
        return jnp.logical_or(tm < last, lax.rem(l, WRAP) != WRAP - 1)

    def copy(src, dst, send, recv, device):
        return pltpu.make_async_remote_copy(
            src_ref=src, dst_ref=dst, send_sem=send, recv_sem=recv, device_id={"tm": device}, device_id_type=MESH
        )

    def rising(l):
        return copy(gl_s.at[l], low_s.at[l + step_up], send_up.at[l], recv_low.at[l + step_up], higher)

    def falling(l):
        return copy(gl_s.at[l], up_s.at[l - step_down], send_down.at[l], recv_up.at[l - step_down], lower)

    def returning_low(l):
        return copy(gl_s.at[l], above_s.at[l - step_down], send_gl.at[l], recv_above.at[l - step_down], lower)

    def returning_up(l):
        return copy(up_s.at[l], below_s.at[l + step_up], send_gu.at[l], recv_below.at[l + step_up], higher)

    clip = lax.axis_index("clip")
    masks = [1 << i for i in range((clip_count - 1).bit_length())]
    bit = {m: (clip // m) % 2 for m in masks}
    across = {m: clip + m * (1 - 2 * bit[m]) for m in masks}
    others = [lax.rem(tm + i, tm_count) for i in range(1, tm_count)]

    third = spatial // 3 // 16 * 16
    cuts = [(0, third), (third, third), (2 * third, spatial - 2 * third)]

    def raw_copy(hbm, start, count):
        place = pl.ds(start, count)
        return pltpu.make_async_copy(hbm.at[0, place], raw_s.at[place], raw_sems.at[start // third])

    moved = ((w_project_hbm, w_project_ref), (w_out_hbm, w_out_ref), (w_up_hbm, w_up_ref), (w_down_hbm, w_down_ref))
    for start, count in cuts:
        raw_copy(tok_hbm, start, count).start()
    for i, (hbm, ref) in enumerate(moved):
        pltpu.make_async_copy(hbm, ref, weight_sems.at[i]).start()

    barrier = pltpu.get_barrier_semaphore()
    for device in others:
        pl.semaphore_signal(barrier, inc=1, device_id={"tm": device}, device_id_type=MESH)
    for m in masks:
        pl.semaphore_signal(barrier, inc=1, device_id={"clip": across[m]}, device_id_type=MESH)
    pl.semaphore_wait(barrier, len(others) + len(masks))

    def store(g):
        return pltpu.make_async_copy(out_s.at[g % 2], out_hbm.at[0, pl.ds(g * GROUP, GROUP)], out_sems.at[g % 2])

    for start, count in cuts:
        raw_copy(tok_hbm, start, count).wait()
        tok_s[:, start : start + count, :] = jnp.transpose(raw_s[start : start + count], (1, 0, 2))
    for start, count in cuts:
        raw_copy(cot_hbm, start, count).start()

    def start_tokens(pair, carry):
        for l in (2 * pair, 2 * pair + 1):
            xhat, _ = normalise(tok_s[l].astype(F32))
            gl_s[l] = (xhat * pre_gain + pre_bias).astype(BF16)
        for l in (2 * pair, 2 * pair + 1):
            pl.when(has_up(l))(lambda: rising(l).start())
            pl.when(has_low(l))(lambda: falling(l).start())
        return carry

    lax.fori_loop(0, lanes // 2, start_tokens, 0)
    for start, count in cuts:
        raw_copy(cot_hbm, start, count).wait()
        cot_s[:, start : start + count, :] = jnp.transpose(raw_s[start : start + count], (1, 0, 2))
    for i, (hbm, ref) in enumerate(moved):
        pltpu.make_async_copy(hbm, ref, weight_sems.at[i]).wait()

    def fill(l, carry):
        @pl.when(jnp.logical_not(has_low(l)))
        def _():
            low_s[l] = jnp.zeros(low_s.shape[1:], BF16)
            below_s[l] = jnp.zeros(low_s.shape[1:], BF16)

        @pl.when(jnp.logical_not(has_up(l)))
        def _():
            up_s[l] = jnp.zeros(up_s.shape[1:], BF16)
            above_s[l] = jnp.zeros(up_s.shape[1:], BF16)

        return carry

    lax.fori_loop(0, lanes, fill, 0)

    for new in (a_w, a_up, a_down, a_small, a_upb):
        new[...] = jnp.zeros_like(new)

    vt_s[:, :, :, HEAD_DIM:, :] = jnp.ones((3, GROUP, heads, 16, spatial), BF16)

    def rows_of(j):
        return pl.ds(pl.multiple_of(j * pad, pad), spatial)

    for ref in (n1_s, dq_s, dkv_s):
        ref[...] = jnp.zeros_like(ref)
    for ref in (att_s, dao_s, res_s):
        for j in range(GROUP):
            ref[pl.ds(j * pad + pad - 16, 16), :] = jnp.zeros((16, ref.shape[1]), ref.dtype)

    sums = Reduction(
        f, hidden, tm, tm_count, masks, bit, across, (a_w, a_up, a_down),
        (s_w, act_s.at[pl.ds(0, f), :], gh_s.at[pl.ds(0, f), :]),
        r_core, r_one, r_two, r_more, r_tm, own_chunk, gathered_ref, a_small, r_small, ar_send, ar_recv, ar_local,
    )

    groups = lanes // GROUP

    def in_last(index, *steps):
        @pl.when(index == lanes // GROUP - 1)
        def _():
            for a, n in steps:
                sums.step(a, n)

    def group(index, carry):
        base = index * GROUP
        slot = index % 2
        pl.when(index >= 2)(lambda: store(index - 2).wait())

        def arrive(j, carry):
            l = base + j
            pl.when(has_low(l))(lambda: copy(gl_s.at[l], low_s.at[l], send_up.at[l], recv_low.at[l], lower).wait_recv())
            pl.when(has_up(l))(lambda: copy(gl_s.at[l], up_s.at[l], send_down.at[l], recv_up.at[l], higher).wait_recv())
            return carry

        lax.fori_loop(0, GROUP, arrive, 0)

        zero_half = jnp.zeros((HEAD_DIM, spatial), BF16)

        def pair_of(h):
            return slice(h // 2 * 2 * HEAD_DIM, (h // 2 + 1) * 2 * HEAD_DIM)

        def mine_of(h):
            return slice(h * HEAD_DIM, (h + 1) * HEAD_DIM)

        def in_pair(h, value):
            return jnp.concatenate([value, zero_half] if h % 2 == 0 else [zero_half, value], 0)

        def project(j, s):
            n1 = (low_s, gl_s, up_s)[s][base + j]
            n1_s[slot, s, rows_of(j), :] = n1
            kv = dot(n1, w_project_ref[:, f:])
            k = kv[:, :f].astype(BF16)
            v = (kv[:, f:] + value_bias).astype(BF16)
            k_s[s, j] = k
            v_s[s, j] = v
            kt_s[s, j] = k.T
            vt_s[s, j, :, :HEAD_DIM, :] = v.T.reshape(heads, HEAD_DIM, spatial)
            if s == 1:
                q = (dot(n1, w_project_ref[:, :f]) + query_bias).astype(BF16)
                qt_s[j] = (q * jnp.asarray(HEAD_DIM ** (-0.5), BF16)).T

        def get_scores(j, h):
            qz = in_pair(h, qt_s[j, mine_of(h), :])
            return [dot(k_s[s, j, :, pair_of(h)], qz) for s in range(3)]

        def attend(j, h, scores):
            low_ok, up_ok = joined(base + j)
            low_far, up_far = jnp.where(low_ok, 0.0, FAR), jnp.where(up_ok, 0.0, FAR)
            tops = [jnp.max(x, 0, keepdims=True) for x in scores]
            top = jnp.maximum(jnp.maximum(tops[0] - low_far, tops[2] - up_far), tops[1])
            attended = None
            for s, shift in enumerate((top + low_far, top, top + up_far)):
                low_prob = jnp.exp(scores[s] - shift).astype(BF16)
                p_s[j, h, s] = low_prob
                got = dot(vt_s[s, j, h], low_prob)
                attended = got if attended is None else attended + got
            inverse = 1.0 / attended[HEAD_DIM : HEAD_DIM + 1, :]
            inv_s[j, h : h + 1, :] = inverse
            attt_s[j, mine_of(h), :] = (attended[:HEAD_DIM, :] * inverse).astype(BF16)

        for s in (1, 0, 2):
            project(0, s)
        steps = [(j, h) for j in range(GROUP) for h in range(heads)]
        beside = {(j, h): [] for j, h in steps}
        for j in range(1, GROUP):
            for s, h in ((1, 0), (0, 2), (2, 4)):
                beside[j - 1, h].append(functools.partial(project, j, s))
        later = get_scores(0, 0)
        for i, (j, h) in enumerate(steps):
            scores = later
            for work in beside[j, h]:
                work()
            if i + 1 < len(steps):
                later = get_scores(*steps[i + 1])
            attend(j, h, scores)
            if h == heads - 1:
                att_s[rows_of(j), :] = attt_s[j].T
                res_s[rows_of(j), :] = tok_s[base + j].astype(F32)

        def sent(j, carry):
            l = base + j
            pl.when(has_up(l))(lambda: rising(l).wait_send())
            pl.when(has_low(l))(lambda: falling(l).wait_send())
            return carry

        lax.fori_loop(0, GROUP, sent, 0)

        residual = res_s[...] + dot(att_s[...], w_out_ref[...]) + out_bias
        res_s[...] = residual
        xhat2, rate2 = normalise(residual)
        n2_s[...] = (xhat2 * mid_gain + mid_bias).astype(BF16)
        for j in range(GROUP):
            full = full_lane(base + j)
            g = cot_s[base + j]
            dao_s[pl.ds(j * pad, spatial), :] = jnp.where(full, g.astype(F32), 0.0).astype(BF16)

        wide = 256

        def mlp(c, carry):
            cols = pl.ds(pl.multiple_of(c * wide, wide), wide)
            h = dot(n2_s[...], w_up_ref[:, cols]) + up_bias[:, c * wide : (c + 1) * wide]
            act, slope = gelu_parts(h)
            act_s[:, cols] = act.astype(BF16)
            gh = dot(dao_s[...], w_down_ref[cols, :], NT) * slope
            gh_s[:, cols] = gh.astype(BF16)
            a_upb[:, cols] += column_sum(gh)
            return carry

        before = project_back(1 - slot, jnp.maximum(base - GROUP, 0))
        chunks = hidden // wide
        for c in range(chunks):
            mlp(c, 0)
            for work in before[len(before) * c // chunks : len(before) * (c + 1) // chunks]:
                work()
        a_up[...] += dot(n2_s[...], gh_s[...], TN)
        a_down[...] += dot(dao_s[...], act_s[...], TN)
        total_out = dot(act_s[...], w_down_ref[...]) + down_bias + res_s[...]
        grad_n2 = dot(gh_s[...], w_up_ref[...], NT)
        in_last(index, (1, 0), (2, 0))
        for j in range(GROUP):
            full = full_lane(base + j)
            mine = total_out[j * pad : j * pad + spatial]
            out_s[slot, j] = jnp.where(full, mine, tok_s[base + j].astype(F32)).astype(BF16)
        store(index).start()
        g = dao_s[...].astype(F32)
        xhat2, rate2 = normalise(res_s[...])
        dres = g + norm_back(grad_n2, xhat2, rate2, mid_gain)
        for j in range(GROUP):
            straight = jnp.where(full_lane(base + j), 0.0, cot_s[base + j].astype(F32))
            own_ref[0, base + j] = (dres[j * pad : j * pad + spatial] + straight).astype(BF16)
        dao = dres.astype(BF16)
        dao_s[...] = dao
        a_small[3:4, :] += column_sum(dao.astype(F32))
        a_small[4:5, :] += column_sum(grad_n2 * xhat2)
        a_small[5:6, :] += column_sum(grad_n2)
        a_small[6:7, :] += column_sum(g)
        a_w[:, 3 * f :] += dot(att_s[...], dao, TN)

        def start_back(j):
            return dot(w_out_ref[...], dao_s[rows_of(j), :], NT).astype(BF16)

        def prepare(j, h, dt):
            dh = dt[mine_of(h), :].astype(F32) * inv_s[j, h : h + 1, :]
            delta = column_sum(dh * attt_s[j, mine_of(h), :].astype(F32))
            dh = dh.astype(BF16)
            dz = in_pair(h, dh)
            return dh, delta, [dot(v_s[s, j, :, pair_of(h)], dz) for s in range(3)]

        def attend_back(j, h, dh, delta, grad_probs):
            mine = mine_of(h)
            qh = qt_s[j, mine, :]
            probs = [p_s[j, h, s] for s in range(3)]
            for s in range(3):
                dt_s[4 + s, mine, :] = dot(dh, probs[s], NT).astype(BF16)
            ds = [(probs[s].astype(F32) * (grad_probs[s] - delta)).astype(BF16) for s in range(3)]
            for s in range(3):
                dt_s[1 + s, mine, :] = dot(qh, ds[s], NT).astype(BF16)
            grad_q = None
            for s in range(3):
                got = dot(kt_s[s, j, mine, :], ds[s])
                grad_q = got if grad_q is None else grad_q + got
            dt_s[0, mine, :] = (grad_q * HEAD_DIM ** (-0.5)).astype(BF16)

        dts = [start_back(j) for j in range(GROUP)]
        later = prepare(0, 0, dts[0])
        for i, (j, h) in enumerate(steps):
            now = later
            if i + 1 < len(steps):
                later = prepare(*steps[i + 1], dts[steps[i + 1][0]])
            attend_back(j, h, *now)
            if (j, h) == steps[len(steps) // 2 - 1]:
                in_last(index, (1, 1), (2, 1))
            if h == heads - 1:
                dq_s[slot, rows_of(j), :] = dt_s[0].T
                for s in range(3):
                    dkv_s[slot, s, rows_of(j), :f] = dt_s[1 + s].T
                    dkv_s[slot, s, rows_of(j), f:] = dt_s[4 + s].T

        in_last(index, (1, 2), (2, 2))
        pl.when(jnp.logical_and(index > 0, index < groups - LATE + 1))(lambda: give_back(base - GROUP))
        return carry

    def project_back(side, base):
        def weights_q():
            dq = dq_s[side]
            a_w[:, :f] += dot(n1_s[side, 1], dq, TN)
            a_small[2:3, :] += column_sum(dq.astype(F32))

        def weights_kv():
            dkv = dkv_s[side].reshape(3 * GROUP * pad, 2 * f)
            a_w[:, f : 3 * f] += dot(n1_s[side].reshape(3 * GROUP * pad, f), dkv, TN)
            a_small[7:8, :] += column_sum(dkv[:, f:].astype(F32))

        def rows_back(j, s):
            grad = dot(dkv_s[side, s, rows_of(j), :], w_project_ref[:, f:], NT)
            if s == 1:
                grad += dot(dq_s[side, rows_of(j), :], w_project_ref[:, :f], NT)
            a_small[0:1, :] += column_sum(grad * n1_s[side, s, rows_of(j), :].astype(F32))
            a_small[1:2, :] += column_sum(grad)
            (gl_s, low_s, up_s)[s][base + j] = grad.astype(BF16)

        rows_work = [functools.partial(rows_back, j, s) for j in range(GROUP) for s in range(3)]
        return [weights_q] + rows_work[:3] + [weights_kv] + rows_work[3:]

    def give_back(base):
        def one(j, carry):
            l = base + j
            pl.when(has_low(l))(lambda: returning_low(l).start())
            pl.when(has_up(l))(lambda: returning_up(l).start())
            return carry

        lax.fori_loop(0, GROUP, one, 0)

    lax.fori_loop(0, lanes // GROUP, group, 0)
    for work in project_back((lanes // GROUP - 1) % 2, lanes - GROUP):
        work()

    def conclude(pair, carry):
        for l in (2 * pair, 2 * pair + 1):

            @pl.when(has_up(l))
            def _(l=l):
                returning_up(l).wait_send()
                copy(gl_s.at[l], above_s.at[l], send_gl.at[l], recv_above.at[l], higher).wait_recv()

            @pl.when(has_low(l))
            def _(l=l):
                returning_low(l).wait_send()
                copy(up_s.at[l], below_s.at[l], send_gu.at[l], recv_below.at[l], lower).wait_recv()

        for l in (2 * pair, 2 * pair + 1):
            grad = low_s[l].astype(F32) + above_s[l].astype(F32) + below_s[l].astype(F32)
            xhat, rate = normalise(tok_s[l].astype(F32))
            own_ref[0, l] = (norm_back(grad, xhat, rate, pre_gain) + own_ref[0, l].astype(F32)).astype(BF16)
        return carry

    for i in range(hidden // f):
        a_small[8 + i : 9 + i, :] = a_upb[:, i * f : (i + 1) * f]
    for g in range(max(lanes // GROUP - 2, 0), lanes // GROUP):
        store(g).wait()
    done = 0
    for what in TAIL:
        if what[0] == "lanes":
            until = lanes // 2 * what[1] // 8
            lax.fori_loop(done, until, conclude, 0)
            done = until
        elif what[0] == "give":
            for i in range(LATE, 0, -1):
                give_back(lanes - i * GROUP)
        elif what[0] == "trade":
            k = what[1]
            if k > 0:
                sums.trade(k - 1, "join")
            if k < 5:
                sums.trade(k, "start")
        else:
            sums.step(*what)
    lax.fori_loop(done, lanes // 2, conclude, 0)
    for k in range(5, sums.trades()):
        sums.trade(k, "start")
        sums.trade(k, "join")
    total_small_ref[...] = a_small[...]
    total_small_ref[0:1, :] = (a_small[0:1, :] - pre_bias * a_small[1:2, :]) / pre_gain


def finish_kernel(
    out_in, grad_in, sums_ref, small_ref,
    out_ref, grad_ref, project_ref, w_out_ref, up_ref, down_ref,
    pre_gain_ref, pre_bias_ref, query_bias_ref, value_bias_ref, out_bias_ref, mid_gain_ref, mid_bias_ref, up_bias_ref,
    down_bias_ref,
):
    f = w_out_ref.shape[1]
    step = pl.program_id(0)
    out_ref[0] = jnp.transpose(out_in[0], (1, 0, 2))
    grad_ref[0] = jnp.transpose(grad_in[0], (1, 0, 2))

    @pl.when(jnp.logical_and(step % 2 == 0, step < 2 * f // TALL))
    def _():
        project_ref[...] = sums_ref[0, :, : 3 * f].astype(F32)
        w_out_ref[...] = sums_ref[0, :, 3 * f :].astype(F32)
        up_ref[...] = sums_ref[1].astype(F32)
        down_ref[...] = sums_ref[2].astype(F32).T

    @pl.when(step == 0)
    def _():
        vectors = (
            pre_gain_ref, pre_bias_ref, query_bias_ref, out_bias_ref, mid_gain_ref, mid_bias_ref, down_bias_ref,
            value_bias_ref,
        )
        for i, ref in enumerate(vectors):
            ref[...] = small_ref[i]
        for i in range(up_bias_ref.shape[0] // f):
            up_bias_ref[pl.ds(i * f, f)] = small_ref[8 + i]


def layer_call(lanes, spatial, f, hidden, tm_count, clip_count, frames, tokens, cotangent, weights):
    pad = -(-spatial // 16) * 16
    rows = GROUP * pad
    smem = pl.BlockSpec(memory_space=pltpu.SMEM)
    vmem = pl.BlockSpec(memory_space=pltpu.VMEM)
    hbm = pl.BlockSpec(memory_space=pl.ANY)
    masks = (clip_count - 1).bit_length()
    sums = [pltpu.VMEM(s, F32) for s in [(f, hidden)] * 3 + [(16, f), (1, hidden)]]
    whole = jax.ShapeDtypeStruct((1, lanes, spatial, f), BF16)
    lane = lambda *s: pltpu.VMEM(s, BF16)
    dma = pltpu.SemaphoreType.DMA((lanes,))
    scratch = sums + [
        lane(lanes, spatial, f), lane(lanes, spatial, f), lane(lanes, spatial, f), lane(lanes, spatial, f),
        lane(lanes, spatial, f),
        lane(spatial, lanes, f), lane(lanes, spatial, f), lane(lanes, spatial, f), lane(2, GROUP, spatial, f),
        lane(f, 3 * f), lane(f, f), lane(f, hidden), lane(hidden, f),
        lane(2, 3, rows, f), lane(3, GROUP, spatial, f), lane(3, GROUP, spatial, f),
        lane(3, GROUP, f, spatial), lane(3, GROUP, f // HEAD_DIM, HEAD_DIM + 16, spatial), lane(GROUP, f, spatial),
        lane(GROUP, f // HEAD_DIM, 3, spatial, spatial), pltpu.VMEM((GROUP, 8, spatial), F32),
        lane(rows, f), lane(GROUP, f, spatial), pltpu.VMEM((rows, f), F32), lane(rows, f),
        lane(rows, hidden), lane(rows, hidden), lane(rows, f),
        lane(2, rows, f), lane(2, 3, rows, 2 * f), lane(7, f, spatial),
    ] + [dma] * 8 + [pltpu.SemaphoreType.DMA((n,)) for n in (3, 4, 2)]
    sems = pltpu.SemaphoreType.DMA((96,))
    scratch += [
        lane(f, hidden), lane(3, f // 2, hidden), lane(3, f // 4, hidden),
        lane(3, f // 8, hidden), lane(max(masks - 3, 1), 3, f // 8, hidden), lane(3, tm_count, f // 8, hidden // 4),
        lane(3, f // 8, hidden // 4), pltpu.VMEM((masks + 2, 16, f), F32), sems, sems, pltpu.SemaphoreType.DMA((3,)),
    ]
    return pl.pallas_call(
        functools.partial(layer_kernel, lanes, spatial, f, hidden, tm_count, clip_count),
        in_specs=[smem, hbm, hbm] + [hbm if w.ndim == 2 else vmem for w in weights],
        out_specs=[hbm, vmem, hbm, vmem],
        out_shape=[whole] * 2 + [jax.ShapeDtypeStruct((3, f, hidden), BF16), jax.ShapeDtypeStruct((16, f), F32)],
        scratch_shapes=scratch,
        name="layer",
        compiler_params=pltpu.CompilerParams(
            vmem_limit_bytes=63 * 1024 * 1024, collective_id=0, has_side_effects=True
        ),
        cost_estimate=pl.CostEstimate(flops=100 * 10**9, bytes_accessed=40 * 10**6, transcendentals=0),
    )(frames, tokens, cotangent, *weights)


def body(
    tokens, cotangent, lane_frames, pre_gain, pre_bias, w_project, query_bias, value_bias,
    w_out, out_bias, mid_gain, mid_bias, w_up, up_bias, w_down, down_bias,
):
    lanes, spatial, f = tokens.shape[1:]
    hidden = w_up.shape[1]
    tm_count = lax.axis_size("tm")
    weights = (
        pre_gain, pre_bias, w_project, query_bias, value_bias, w_out, out_bias,
        mid_gain, mid_bias, w_up, up_bias, w_down, down_bias,
    )
    out, input_grad, gathered, small = layer_call(
        lanes, spatial, f, hidden, tm_count, lax.axis_size("clip"), lane_frames,
        tokens.transpose(0, 2, 1, 3), cotangent.transpose(0, 2, 1, 3), weights,
    )
    part = 32
    steps = max(-(-spatial // part), 2 * f // TALL)
    turn = lambda i: jnp.minimum(i, -(-spatial // part) - 1)
    tall = lambda i: jnp.minimum(i // 2, f // TALL - 1)
    lane_block = pl.BlockSpec((1, lanes, part, f), lambda i: (0, 0, turn(i), 0))
    token_block = pl.BlockSpec((1, part, lanes, f), lambda i: (0, turn(i), 0, 0))
    row_block = lambda n: pl.BlockSpec((TALL, n), lambda i: (tall(i), 0))
    vector = lambda n: pl.BlockSpec((n,), lambda i: (0,))
    sizes = [f] * 7 + [hidden, f]
    got = pl.pallas_call(
        finish_kernel,
        grid=(steps,),
        in_specs=[
            lane_block, lane_block, pl.BlockSpec((3, TALL, hidden), lambda i: (0, tall(i), 0)),
            pl.BlockSpec((16, f), lambda i: (0, 0)),
        ],
        out_specs=[
            token_block, token_block, row_block(3 * f), row_block(f), row_block(hidden),
            pl.BlockSpec((hidden, TALL), lambda i: (0, tall(i))),
        ] + [vector(n) for n in sizes],
        out_shape=[jax.ShapeDtypeStruct((1, spatial, lanes, f), BF16)] * 2
        + [jax.ShapeDtypeStruct(n, F32) for n in ((f, 3 * f), (f, f), (f, hidden), (hidden, f))]
        + [jax.ShapeDtypeStruct((n,), F32) for n in sizes],
        name="finish",
    )(out, input_grad, gathered, small)
    out, input_grad = (v.transpose(0, 2, 1, 3) for v in got[:2])
    g_project, g_out, g_up, g_down = got[2:6]
    pre_gain, pre_bias, query_bias, value_bias, out_bias, mid_gain, mid_bias, up_bias, down_bias = got[6:]
    return (
        out, input_grad, pre_gain, pre_bias, g_project, query_bias, value_bias, g_out, out_bias,
        mid_gain, mid_bias, g_up, up_bias, g_down, down_bias,
    )


def solution(mesh):
    spread = P("tm", "clip", None, None)
    return jax.shard_map(
        body,
        mesh=mesh,
        in_specs=(spread, spread, P("clip")) + (P(),) * 13,
        out_specs=(spread, spread) + (P(),) * 13,
        check_vma=False,
    )
```

```python
import functools

import jax
import jax.numpy as jnp
from jax import lax
from jax.experimental import pallas as pl
from jax.experimental.pallas import tpu as pltpu
from jax.sharding import PartitionSpec as P

HEAD_DIM = 64
GROUP = 2
WRAP = 4
MESH = pl.DeviceIdType.MESH
EPSILON = 1e-06
FAR = 1e30
F32 = jnp.float32
BF16 = jnp.bfloat16
NN = (((1,), (0,)), ((), ()))
NT = (((1,), (1,)), ((), ()))
TN = (((0,), (0,)), ((), ()))


def dot(a, b, dims=NN):
    return lax.dot_general(a, b, dims, preferred_element_type=F32)


def row_mean(value):
    return jnp.sum(value, -1, keepdims=True) * (1.0 / value.shape[-1])


def normalise(x):
    center = x - row_mean(x)
    rate = lax.rsqrt(row_mean(center * center) + EPSILON)
    return center * rate, rate


def norm_back(grad, xhat, rate, gain):
    e = grad * gain
    return rate * (e - row_mean(e) - xhat * row_mean(e * xhat))


def gelu_parts(h):
    size = jnp.abs(h)
    bell = jnp.exp(-0.5 * (h * h))
    whole = 1.0 + 0.23164190 * size
    t = pl.reciprocal(whole, approx=True)
    t = t * (2.0 - whole * t)
    poly = t * (0.127414796 + t * (-0.142248368 + t * (0.7107068705 + t * (-0.7265760135 + t * 0.5307027145))))
    tail = poly * bell
    phi = jnp.where(h >= 0.0, 1.0 - tail, tail)
    return jnp.maximum(h, 0.0) - size * tail, phi + h * (bell * 0.3989422804014327)


def column_sum(value):
    return jnp.sum(value, 0, keepdims=True)


UP, DOWN, W = 1, 2, 0
LATE = 1
TAIL = [
    (W, 0), ("rows", 0, 6), (UP, 3), (DOWN, 3), ("trade", 0, "start"), ("lanes", 2), ("trade", 0, "join"), ("trade", 1, "start"), (W, 1), ("trade", 1, "join"), ("trade", 2, "start"), (W, 2),
    ("lanes", 3), ("trade", 2, "join"), ("trade", 3, "start"), (W, 3), (UP, 4), (DOWN, 4), ("trade", 3, "join"), ("trade", 4, "start"), (W, 4), ("give",), (UP, 5), (DOWN, 5),
    (W, 5), (UP, 6), (DOWN, 6), (W, 6), (UP, 7), (DOWN, 7), (W, 7), ("trade", 4, "join"), ("lanes", 4), ("lanes", 5), (UP, 8), (DOWN, 8),
    (W, 8),
]


class Reduction:
    def __init__(
        self, f, hidden, tm, tm_count, masks, bit, across, sums, sends,
        r_core, r_one, r_two, r_more, r_tm, own_chunk, gathered, small, r_small, send_sems, recv_sems, local_sems,
    ):
        self.f, self.hidden, self.tm, self.tm_count = f, hidden, tm, tm_count
        self.masks, self.bit, self.across = masks, bit, across
        self.sums, self.sends = sums, sends
        self.r_core, self.r_one, self.r_two, self.r_more, self.r_tm = r_core, r_one, r_two, r_more, r_tm
        self.own_chunk, self.gathered, self.small, self.r_small = own_chunk, gathered, small, r_small
        self.send_sems, self.recv_sems, self.local_sems = send_sems, recv_sems, local_sems
        half = (len(masks) - 1) // 2
        self.more = masks[2 : 1 + half] + masks[2 + half :]
        one, two = masks[1], masks[1 + half]
        wide = hidden // 2
        self.pieces = [(slice(0, wide), one, two), (slice(wide, hidden), two, one)]
        self.core = bit[1] * (f // 2)
        self.level_one = [self.core + bit[m] * (f // 4) for _, m, _ in self.pieces]
        self.level_two = [at + bit[m] * (f // 8) for at, (_, _, m) in zip(self.level_one, self.pieces)]
        self.used, self.known, self.flying = 0, {}, {}

    def sem(self, name, n=1):
        if name not in self.known:
            self.known[name] = self.used
            self.used += n
        return self.known[name]

    def copy(self, name, src, dst, device):
        at = self.sem(name)
        return pltpu.make_async_remote_copy(
            src_ref=src, dst_ref=dst, send_sem=self.send_sems.at[at], recv_sem=self.recv_sems.at[at],
            device_id=device, device_id_type=MESH,
        )

    def rows(self, at, count):
        return pl.ds(pl.multiple_of(at, 16), count)

    def add(self, a, cols, at, count, got):
        where = self.rows(at, count)
        self.sums[a][where, cols] += got.astype(F32)

    def core_copy(self, a):
        count = self.f // 2
        away = self.rows((1 - self.bit[1]) * count, count)
        return self.copy(("core", a), self.sends[a].at[away, :], self.r_core.at[a], {"clip": self.across[1]})

    def half_copy(self, level, a, i):
        cols, *ms = self.pieces[i]
        count = self.f // (4 * level)
        m = ms[level - 1]
        start = self.core if level == 1 else self.level_one[i]
        away = self.rows(start + (1 - self.bit[m]) * count, count)
        box = (self.r_one, self.r_two)[level - 1]
        return self.copy(
            ("half", level, a, i), self.sends[a].at[away, cols], box.at[a, :, cols], {"clip": self.across[m]}
        )

    def start_half(self, level, a):
        count = self.f // (4 * level)
        for i, (cols, *ms) in enumerate(self.pieces):
            m = ms[level - 1]
            off = (1 - self.bit[m]) * count
            start = self.core if level == 1 else self.level_one[i]
            if level == 1:
                self.add(a, cols, start + off, count, self.r_core[a, self.rows(off, count), cols])
            away = self.rows(start + off, count)
            self.sends[a][away, cols] = self.sums[a][away, cols].astype(BF16)
            self.half_copy(level, a, i).start()
        if level == 1:
            for i, (cols, m, _) in enumerate(self.pieces):
                off = self.bit[m] * count
                self.add(a, cols, self.core + off, count, self.r_core[a, self.rows(off, count), cols])

    def end_half(self, level, a):
        count = self.f // (4 * level)
        for i, (cols, *_) in enumerate(self.pieces):
            self.half_copy(level, a, i).wait()
            at = (self.level_one, self.level_two)[level - 1][i]
            self.add(a, cols, at, count, (self.r_one, self.r_two)[level - 1][a, :, cols])

    def chunk(self, q):
        n = self.hidden // 4
        return slice(q * n, (q + 1) * n), self.rows(self.level_two[q // 2], self.f // 8)

    def chunk_copy(self, a, q):
        cols, here = self.chunk(q)
        return pltpu.make_async_remote_copy(
            src_ref=self.sends[a].at[here, cols], dst_ref=self.r_tm.at[a, self.tm],
            send_sem=self.send_sems.at[self.sem(("leave", a, q))],
            recv_sem=self.recv_sems.at[self.sem(("meet", a), self.tm_count) + self.tm],
            device_id={"tm": q}, device_id_type=MESH,
        )

    def publish(self, a, q, do):
        cols, here = self.chunk(q)
        place, mine = self.gathered.at[a, here, cols], self.own_chunk.at[a]
        local = pltpu.make_async_copy(mine, place, self.local_sems.at[a])
        local.start() if do == "start" else local.wait()
        for other in range(self.tm_count):
            if other != q:
                copy = pltpu.make_async_remote_copy(
                    src_ref=mine, dst_ref=place, send_sem=self.send_sems.at[self.sem(("out", a), self.tm_count) + other],
                    recv_sem=self.recv_sems.at[self.sem(("back", a), self.tm_count) + q],
                    device_id={"tm": other}, device_id_type=MESH,
                )
                copy.start() if do == "start" else copy.wait_send()

    def back_copy(self, level, a, i):
        cols, *ms = self.pieces[i]
        at, count = (self.level_two, self.level_one)[2 - level][i], self.f // (4 * level)
        place = self.gathered.at[a, self.rows(at, count), cols]
        return self.copy(("return", level, a, i), place, place, {"clip": self.across[ms[level - 1]]})

    def core_back(self, a):
        place = self.gathered.at[a, self.rows(self.core, self.f // 2), :]
        return self.copy(("core back", a), place, place, {"clip": self.across[1]})

    def step(self, a, n):
        if n == 0:
            count = self.f // 2
            away = self.rows((1 - self.bit[1]) * count, count)
            self.sends[a][away, :] = self.sums[a][away, :].astype(BF16)
            self.core_copy(a).start()
        elif n == 1:
            self.core_copy(a).wait()
            self.start_half(1, a)
        elif n == 2:
            self.end_half(1, a)
            self.start_half(2, a)
        elif n == 3:
            self.end_half(2, a)
            count = self.f // 8
            for k, m in enumerate(self.more):
                for i, (cols, *_) in enumerate(self.pieces):
                    here = self.rows(self.level_two[i], count)
                    box = self.r_more.at[k, a, :, cols]
                    self.sends[a][here, cols] = self.sums[a][here, cols].astype(BF16)
                    copy = self.copy(("more", k, a, i), self.sends[a].at[here, cols], box, {"clip": self.across[m]})
                    copy.start()
                    copy.wait()
                    self.sums[a][here, cols] = self.sends[a][here, cols].astype(F32) + box[...].astype(F32)
            for q in range(4):

                def send(q=q):
                    cols, here = self.chunk(q)
                    self.sends[a][here, cols] = self.sums[a][here, cols].astype(BF16)
                    self.chunk_copy(a, q).start()

                pl.when(self.tm != q)(send)
        elif n == 4:
            for q in range(4):

                def settle(q=q):
                    cols, here = self.chunk(q)
                    total = self.sums[a][here, cols]
                    for other in range(self.tm_count):
                        if other != q:
                            box = self.r_tm.at[a, other]
                            at = self.sem(("meet", a), self.tm_count) + other
                            pltpu.make_async_copy(box, box, self.recv_sems.at[at]).wait()
                            total += box[...].astype(F32)
                    self.own_chunk[a] = total.astype(BF16)
                    self.publish(a, q, "start")

                pl.when(self.tm == q)(settle)
        elif n == 5:
            for q in range(4):

                def arrive(q=q):
                    self.chunk_copy(a, q).wait_send()
                    cols, here = self.chunk(q)
                    place = self.gathered.at[a, here, cols]
                    at = self.sem(("back", a), self.tm_count) + q
                    pltpu.make_async_copy(place, place, self.recv_sems.at[at]).wait()

                pl.when(self.tm != q)(arrive)
                pl.when(self.tm == q)(functools.partial(self.publish, a, q, "wait"))
            for i in range(2):
                self.back_copy(2, a, i).start()
        elif n == 6:
            for i in range(2):
                self.back_copy(2, a, i).wait()
            for i in range(2):
                self.back_copy(1, a, i).start()
        elif n == 7:
            for i in range(2):
                self.back_copy(1, a, i).wait()
            self.core_back(a).start()
        else:
            self.core_back(a).wait()

    def trade(self, k, do):
        if k < len(self.masks):
            device = {"clip": self.across[self.masks[k]]}
        else:
            m = 1 << (k - len(self.masks))
            device = {"tm": self.tm + m - 2 * m * ((self.tm // m) % 2)}
        copy = self.copy(("small", k), self.small, self.r_small.at[k], device)
        if do == "start":
            copy.start()
        else:
            copy.wait()
            self.small[...] += self.r_small[k]

    def trades(self):
        return len(self.masks) + (self.tm_count - 1).bit_length()


def layer_kernel(
    lanes, spatial, features, hidden, tm_count, clip_count,
    frames_ref, tok_hbm, cot_hbm,
    pre_gain_ref, pre_bias_ref, w_project_hbm, query_bias_ref, value_bias_ref,
    w_out_hbm, out_bias_ref, mid_gain_ref, mid_bias_ref, w_up_hbm, up_bias_ref, w_down_hbm, down_bias_ref,
    out_hbm, grad_hbm, gathered_ref, total_small_ref,
    a_w, a_up, a_down, a_small, a_upb, low_s, up_s, gl_s, above_s, below_s, own_s, raw_s, tok_s, cot_s, out_s,
    w_project_ref, w_out_ref, w_up_ref, w_down_ref, n1_s, k_s, v_s, kt_s, vt_s, qt_s, p_s, inv_s, att_s, attt_s, res_s, n2_s, act_s, gh_s,
    dao_s, dq_s, dkv_s, dt_s,
    send_up, send_down, recv_low, recv_up, send_gl, send_gu, recv_above, recv_below,
    raw_sems, weight_sems, out_sems, own_sems, s_w, r_core, r_one, r_two, r_more, r_tm, own_chunk, r_small, ar_send, ar_recv, ar_local,
):
    f = features
    pad = n1_s.shape[2] // GROUP
    heads = f // HEAD_DIM
    tm = lax.axis_index("tm")
    last = tm_count - 1
    at_low, at_high = tm == 0, tm == last
    higher, lower = lax.rem(tm + 1, tm_count), lax.rem(tm + last, tm_count)
    step_up, step_down = (tm + 1) // tm_count, (tm_count - tm) // tm_count

    def row(ref):
        return ref[...].astype(F32).reshape(1, -1)

    pre_gain, pre_bias, mid_gain, mid_bias = row(pre_gain_ref), row(pre_bias_ref), row(mid_gain_ref), row(mid_bias_ref)
    out_bias, down_bias, up_bias = row(out_bias_ref), row(down_bias_ref), row(up_bias_ref)
    query_bias, value_bias = row(query_bias_ref), row(value_bias_ref)

    def full_lane(l):
        return frames_ref[l] > 0

    def joined(l):
        frames = frames_ref[l]
        inner_low = ((frames == 4 * tm_count) & (l % 2 > 0)) | ((frames == 8 * tm_count) & (l % 4 > 0))
        inner_up = ((frames == 4 * tm_count) & (l % 2 < 1)) | ((frames == 8 * tm_count) & (l % 4 < 3))
        return (frames > 0) & (inner_low | (tm > 0)), (frames > 0) & (inner_up | (tm < last))

    def has_low(l):
        return jnp.logical_or(tm > 0, lax.rem(l, WRAP) != 0)

    def has_up(l):
        return jnp.logical_or(tm < last, lax.rem(l, WRAP) != WRAP - 1)

    def copy(src, dst, send, recv, device):
        return pltpu.make_async_remote_copy(
            src_ref=src, dst_ref=dst, send_sem=send, recv_sem=recv, device_id={"tm": device}, device_id_type=MESH
        )

    def rising(l):
        return copy(gl_s.at[l], low_s.at[l + step_up], send_up.at[l], recv_low.at[l + step_up], higher)

    def falling(l):
        return copy(gl_s.at[l], up_s.at[l - step_down], send_down.at[l], recv_up.at[l - step_down], lower)

    def returning_low(l):
        return copy(gl_s.at[l], above_s.at[l - step_down], send_gl.at[l], recv_above.at[l - step_down], lower)

    def returning_up(l):
        return copy(up_s.at[l], below_s.at[l + step_up], send_gu.at[l], recv_below.at[l + step_up], higher)

    clip = lax.axis_index("clip")
    masks = [1 << i for i in range((clip_count - 1).bit_length())]
    bit = {m: (clip // m) % 2 for m in masks}
    across = {m: clip + m * (1 - 2 * bit[m]) for m in masks}
    others = [lax.rem(tm + i, tm_count) for i in range(1, tm_count)]

    third = spatial // 3 // 16 * 16
    cuts = [(0, third), (third, third), (2 * third, spatial - 2 * third)]

    def raw_copy(hbm, start, count):
        place = pl.ds(start, count)
        return pltpu.make_async_copy(hbm.at[0, place], raw_s.at[place], raw_sems.at[start // third])

    moved = ((w_project_hbm, w_project_ref), (w_out_hbm, w_out_ref), (w_up_hbm, w_up_ref), (w_down_hbm, w_down_ref))
    for start, count in cuts:
        raw_copy(tok_hbm, start, count).start()
    for i, (hbm, ref) in enumerate(moved):
        pltpu.make_async_copy(hbm, ref, weight_sems.at[i]).start()

    barrier = pltpu.get_barrier_semaphore()
    for device in others:
        pl.semaphore_signal(barrier, inc=1, device_id={"tm": device}, device_id_type=MESH)
    for m in masks:
        pl.semaphore_signal(barrier, inc=1, device_id={"clip": across[m]}, device_id_type=MESH)

    def store(g):
        return pltpu.make_async_copy(out_s.at[g % 2], out_hbm.at[0, pl.ds(g * GROUP, GROUP)], out_sems.at[g % 2])

    for start, count in cuts:
        raw_copy(tok_hbm, start, count).wait()
        tok_s[:, start : start + count, :] = jnp.transpose(raw_s[start : start + count], (1, 0, 2))
    for start, count in cuts:
        raw_copy(cot_hbm, start, count).start()
    pl.semaphore_wait(barrier, len(others) + len(masks))

    def start_tokens(pair, carry):
        for l in (2 * pair, 2 * pair + 1):
            xhat, _ = normalise(tok_s[l].astype(F32))
            gl_s[l] = (xhat * pre_gain + pre_bias).astype(BF16)
        for l in (2 * pair, 2 * pair + 1):
            pl.when(has_up(l))(lambda: rising(l).start())
            pl.when(has_low(l))(lambda: falling(l).start())
        return carry

    lax.fori_loop(0, lanes // 2, start_tokens, 0)
    for start, count in cuts:
        raw_copy(cot_hbm, start, count).wait()
        cot_s[:, start : start + count, :] = jnp.transpose(raw_s[start : start + count], (1, 0, 2))
    for i, (hbm, ref) in enumerate(moved):
        pltpu.make_async_copy(hbm, ref, weight_sems.at[i]).wait()

    def fill(l, carry):
        @pl.when(jnp.logical_not(has_low(l)))
        def _():
            low_s[l] = jnp.zeros(low_s.shape[1:], BF16)
            below_s[l] = jnp.zeros(low_s.shape[1:], BF16)

        @pl.when(jnp.logical_not(has_up(l)))
        def _():
            up_s[l] = jnp.zeros(up_s.shape[1:], BF16)
            above_s[l] = jnp.zeros(up_s.shape[1:], BF16)

        return carry

    lax.fori_loop(0, lanes, fill, 0)

    for new in (a_w, a_up, a_down, a_small, a_upb):
        new[...] = jnp.zeros_like(new)

    vt_s[:, :, :, HEAD_DIM:, :] = jnp.ones((3, GROUP, heads, 16, spatial), BF16)

    def rows_of(j):
        return pl.ds(pl.multiple_of(j * pad, pad), spatial)

    for ref in (n1_s, dq_s, dkv_s):
        ref[...] = jnp.zeros_like(ref)
    for ref in (att_s, dao_s, res_s):
        for j in range(GROUP):
            ref[pl.ds(j * pad + pad - 16, 16), :] = jnp.zeros((16, ref.shape[1]), ref.dtype)

    sums = Reduction(
        f, hidden, tm, tm_count, masks, bit, across, (a_w, a_up, a_down),
        (s_w, act_s.at[pl.ds(0, f), :], gh_s.at[pl.ds(0, f), :]),
        r_core, r_one, r_two, r_more, r_tm, own_chunk, gathered_ref, a_small, r_small, ar_send, ar_recv, ar_local,
    )

    groups = lanes // GROUP

    def in_last(index, *steps):
        @pl.when(index == lanes // GROUP - 1)
        def _():
            for a, n in steps:
                sums.step(a, n)

    def group(index, carry):
        base = index * GROUP
        slot = index % 2
        pl.when(index >= 2)(lambda: store(index - 2).wait())

        def arrive(j, carry):
            l = base + j
            pl.when(has_low(l))(lambda: copy(gl_s.at[l], low_s.at[l], send_up.at[l], recv_low.at[l], lower).wait_recv())
            pl.when(has_up(l))(lambda: copy(gl_s.at[l], up_s.at[l], send_down.at[l], recv_up.at[l], higher).wait_recv())
            return carry

        lax.fori_loop(0, GROUP, arrive, 0)

        zero_half = jnp.zeros((HEAD_DIM, spatial), BF16)

        def pair_of(h):
            return slice(h // 2 * 2 * HEAD_DIM, (h // 2 + 1) * 2 * HEAD_DIM)

        def mine_of(h):
            return slice(h * HEAD_DIM, (h + 1) * HEAD_DIM)

        def in_pair(h, value):
            return jnp.concatenate([value, zero_half] if h % 2 == 0 else [zero_half, value], 0)

        def project(j, s):
            n1 = (low_s, gl_s, up_s)[s][base + j]
            n1_s[slot, s, rows_of(j), :] = n1
            kv = dot(n1, w_project_ref[:, f:])
            k = kv[:, :f].astype(BF16)
            v = (kv[:, f:] + value_bias).astype(BF16)
            k_s[s, j] = k
            v_s[s, j] = v
            kt_s[s, j] = k.T
            vt_s[s, j, :, :HEAD_DIM, :] = v.T.reshape(heads, HEAD_DIM, spatial)
            if s == 1:
                q = (dot(n1, w_project_ref[:, :f]) + query_bias).astype(BF16)
                qt_s[j] = (q * jnp.asarray(HEAD_DIM ** (-0.5), BF16)).T

        def get_scores(j, h):
            qz = in_pair(h, qt_s[j, mine_of(h), :])
            return [dot(k_s[s, j, :, pair_of(h)], qz) for s in range(3)]

        def attend(j, h, scores):
            low_ok, up_ok = joined(base + j)
            low_far, up_far = jnp.where(low_ok, 0.0, FAR), jnp.where(up_ok, 0.0, FAR)
            tops = [jnp.max(x, 0, keepdims=True) for x in scores]
            top = jnp.maximum(jnp.maximum(tops[0] - low_far, tops[2] - up_far), tops[1])
            attended = None
            for s, shift in enumerate((top + low_far, top, top + up_far)):
                low_prob = jnp.exp(scores[s] - shift).astype(BF16)
                p_s[j, h, s] = low_prob
                got = dot(vt_s[s, j, h], low_prob)
                attended = got if attended is None else attended + got
            inverse = 1.0 / attended[HEAD_DIM : HEAD_DIM + 1, :]
            inv_s[j, h : h + 1, :] = inverse
            attt_s[j, mine_of(h), :] = (attended[:HEAD_DIM, :] * inverse).astype(BF16)

        for s in (1, 0, 2):
            project(0, s)
        steps = [(j, h) for j in range(GROUP) for h in range(heads)]
        beside = {(j, h): [] for j, h in steps}
        for j in range(1, GROUP):
            for s, h in ((1, 0), (0, 2), (2, 4)):
                beside[j - 1, h].append(functools.partial(project, j, s))
        later = get_scores(0, 0)
        for i, (j, h) in enumerate(steps):
            scores = later
            for work in beside[j, h]:
                work()
            if i + 1 < len(steps):
                later = get_scores(*steps[i + 1])
            attend(j, h, scores)
            if h == heads - 1:
                att_s[rows_of(j), :] = attt_s[j].T
                res_s[rows_of(j), :] = tok_s[base + j].astype(F32)

        def sent(j, carry):
            l = base + j
            pl.when(has_up(l))(lambda: rising(l).wait_send())
            pl.when(has_low(l))(lambda: falling(l).wait_send())
            return carry

        lax.fori_loop(0, GROUP, sent, 0)

        residual = res_s[...] + dot(att_s[...], w_out_ref[...]) + out_bias
        res_s[...] = residual
        xhat2, rate2 = normalise(residual)
        n2_s[...] = (xhat2 * mid_gain + mid_bias).astype(BF16)
        for j in range(GROUP):
            full = full_lane(base + j)
            g = cot_s[base + j]
            dao_s[pl.ds(j * pad, spatial), :] = jnp.where(full, g.astype(F32), 0.0).astype(BF16)

        wide = 256

        def mlp(c, carry):
            cols = pl.ds(pl.multiple_of(c * wide, wide), wide)
            h = dot(n2_s[...], w_up_ref[:, cols]) + up_bias[:, c * wide : (c + 1) * wide]
            act, slope = gelu_parts(h)
            act_s[:, cols] = act.astype(BF16)
            gh = dot(dao_s[...], w_down_ref[cols, :], NT) * slope
            gh_s[:, cols] = gh.astype(BF16)
            a_upb[:, cols] += column_sum(gh)
            return carry

        before, _, _ = project_back(1 - slot, jnp.maximum(base - GROUP, 0))
        chunks = hidden // wide
        for c in range(chunks):
            mlp(c, 0)
            for work in before[len(before) * c // chunks : len(before) * (c + 1) // chunks]:
                work()
        a_up[...] += dot(n2_s[...], gh_s[...], TN)
        a_down[...] += dot(dao_s[...], act_s[...], TN)
        total_out = dot(act_s[...], w_down_ref[...]) + down_bias + res_s[...]
        grad_n2 = dot(gh_s[...], w_up_ref[...], NT)
        in_last(index, (1, 0), (2, 0))
        for j in range(GROUP):
            full = full_lane(base + j)
            mine = total_out[j * pad : j * pad + spatial]
            out_s[slot, j] = jnp.where(full, mine, tok_s[base + j].astype(F32)).astype(BF16)
        store(index).start()
        g = dao_s[...].astype(F32)
        xhat2, rate2 = normalise(res_s[...])
        dres = g + norm_back(grad_n2, xhat2, rate2, mid_gain)
        for j in range(GROUP):
            straight = jnp.where(full_lane(base + j), 0.0, cot_s[base + j].astype(F32))
            own_s[base + j] = (dres[j * pad : j * pad + spatial] + straight).astype(BF16)
        dao = dres.astype(BF16)
        dao_s[...] = dao
        a_small[3:4, :] += column_sum(dao.astype(F32))
        a_small[4:5, :] += column_sum(grad_n2 * xhat2)
        a_small[5:6, :] += column_sum(grad_n2)
        a_small[6:7, :] += column_sum(g)
        a_w[:, 3 * f :] += dot(att_s[...], dao, TN)

        def start_back(j):
            return dot(w_out_ref[...], dao_s[rows_of(j), :], NT).astype(BF16)

        def prepare(j, h, dt):
            dh = dt[mine_of(h), :].astype(F32) * inv_s[j, h : h + 1, :]
            delta = column_sum(dh * attt_s[j, mine_of(h), :].astype(F32))
            dh = dh.astype(BF16)
            dz = in_pair(h, dh)
            return dh, delta, [dot(v_s[s, j, :, pair_of(h)], dz) for s in range(3)]

        def attend_back(j, h, dh, delta, grad_probs):
            mine = mine_of(h)
            qh = qt_s[j, mine, :]
            probs = [p_s[j, h, s] for s in range(3)]
            for s in range(3):
                dt_s[4 + s, mine, :] = dot(dh, probs[s], NT).astype(BF16)
            ds = [(probs[s].astype(F32) * (grad_probs[s] - delta)).astype(BF16) for s in range(3)]
            for s in range(3):
                dt_s[1 + s, mine, :] = dot(qh, ds[s], NT).astype(BF16)
            grad_q = None
            for s in range(3):
                got = dot(kt_s[s, j, mine, :], ds[s])
                grad_q = got if grad_q is None else grad_q + got
            dt_s[0, mine, :] = (grad_q * HEAD_DIM ** (-0.5)).astype(BF16)

        dts = [start_back(j) for j in range(GROUP)]
        later = prepare(0, 0, dts[0])
        for i, (j, h) in enumerate(steps):
            now = later
            if i + 1 < len(steps):
                later = prepare(*steps[i + 1], dts[steps[i + 1][0]])
            attend_back(j, h, *now)
            if (j, h) == steps[len(steps) // 2 - 1]:
                in_last(index, (1, 1), (2, 1))
            if h == heads - 1:
                dq_s[slot, rows_of(j), :] = dt_s[0].T
                for s in range(3):
                    dkv_s[slot, s, rows_of(j), :f] = dt_s[1 + s].T
                    dkv_s[slot, s, rows_of(j), f:] = dt_s[4 + s].T

        in_last(index, (1, 2), (2, 2))
        pl.when(jnp.logical_and(index > 0, index < groups - LATE + 1))(lambda: give_back(base - GROUP))
        return carry

    def project_back(side, base):
        def weights_q():
            dq = dq_s[side]
            a_w[:, :f] += dot(n1_s[side, 1], dq, TN)
            a_small[2:3, :] += column_sum(dq.astype(F32))

        def weights_kv():
            dkv = dkv_s[side].reshape(3 * GROUP * pad, 2 * f)
            a_w[:, f : 3 * f] += dot(n1_s[side].reshape(3 * GROUP * pad, f), dkv, TN)
            a_small[7:8, :] += column_sum(dkv[:, f:].astype(F32))

        def rows_back(j, s):
            grad = dot(dkv_s[side, s, rows_of(j), :], w_project_ref[:, f:], NT)
            if s == 1:
                grad += dot(dq_s[side, rows_of(j), :], w_project_ref[:, :f], NT)
            a_small[0:1, :] += column_sum(grad * n1_s[side, s, rows_of(j), :].astype(F32))
            a_small[1:2, :] += column_sum(grad)
            (gl_s, low_s, up_s)[s][base + j] = grad.astype(BF16)

        rows_work = [functools.partial(rows_back, j, s) for j in range(GROUP) for s in range(3)]
        return [weights_q] + rows_work[:3] + [weights_kv] + rows_work[3:], [weights_q, weights_kv], rows_work

    def give_back(base):
        def one(j, carry):
            l = base + j
            pl.when(has_low(l))(lambda: returning_low(l).start())
            pl.when(has_up(l))(lambda: returning_up(l).start())
            return carry

        lax.fori_loop(0, GROUP, one, 0)

    lax.fori_loop(0, lanes // GROUP, group, 0)
    _, final_weights, final_rows = project_back((lanes // GROUP - 1) % 2, lanes - GROUP)
    for work in final_weights:
        work()

    def hand_over(pair):
        place = pl.ds(2 * pair, 2)
        return pltpu.make_async_copy(own_s.at[place], grad_hbm.at[0, place], own_sems.at[pair])

    def handed_over(pair, carry):
        hand_over(pair).wait()
        return carry

    def conclude(pair, carry):
        for l in (2 * pair, 2 * pair + 1):

            @pl.when(has_up(l))
            def _(l=l):
                returning_up(l).wait_send()
                copy(gl_s.at[l], above_s.at[l], send_gl.at[l], recv_above.at[l], higher).wait_recv()

            @pl.when(has_low(l))
            def _(l=l):
                returning_low(l).wait_send()
                copy(up_s.at[l], below_s.at[l], send_gu.at[l], recv_below.at[l], lower).wait_recv()

        for l in (2 * pair, 2 * pair + 1):
            grad = low_s[l].astype(F32) + above_s[l].astype(F32) + below_s[l].astype(F32)
            xhat, rate = normalise(tok_s[l].astype(F32))
            own_s[l] = (norm_back(grad, xhat, rate, pre_gain) + own_s[l].astype(F32)).astype(BF16)
        hand_over(pair).start()
        return carry

    for i in range(hidden // f):
        a_small[8 + i : 9 + i, :] = a_upb[:, i * f : (i + 1) * f]
    for g in range(max(lanes // GROUP - 2, 0), lanes // GROUP):
        store(g).wait()
    done = 0
    for what in TAIL:
        if what[0] == "lanes":
            until = lanes // 2 * what[1] // 8
            lax.fori_loop(done, until, conclude, 0)
            done = until
        elif what[0] == "rows":
            for work in final_rows[what[1] : what[2]]:
                work()
        elif what[0] == "give":
            for i in range(LATE, 0, -1):
                give_back(lanes - i * GROUP)
        elif what[0] == "trade":
            sums.trade(what[1], what[2])
        else:
            sums.step(*what)
    lax.fori_loop(done, lanes // 2, conclude, 0)
    for k in range(5, sums.trades()):
        sums.trade(k, "start")
        sums.trade(k, "join")
    lax.fori_loop(0, lanes // 2, handed_over, 0)
    total_small_ref[...] = a_small[...]
    total_small_ref[0:1, :] = (a_small[0:1, :] - pre_bias * a_small[1:2, :]) / pre_gain


def finish_kernel(
    out_hbm, grad_hbm, sums_hbm, small_ref,
    out_to, grad_to, project_to, w_out_to, up_to, down_to,
    pre_gain_ref, pre_bias_ref, query_bias_ref, value_bias_ref, out_bias_ref, mid_gain_ref, mid_bias_ref, up_bias_ref,
    down_bias_ref,
    lane_s, turned_s, sums_s, project_s, w_out_s, up_s, down_s, in_sems, sum_sems, out_sems, wide_sems,
):
    f, spatial = w_out_s.shape[1], lane_s.shape[2]
    third = spatial // 3 // 16 * 16
    cuts = [(0, third), (third, third), (2 * third, spatial - 2 * third)]
    sides = ((out_hbm, out_to), (grad_hbm, grad_to))

    def load(i, k):
        start, count = cuts[k]
        place = pl.ds(start, count)
        return pltpu.make_async_copy(sides[i][0].at[0, :, place], lane_s.at[i, :, place], in_sems.at[i, k])

    def store(i, k):
        start, count = cuts[k]
        place = pl.ds(start, count)
        return pltpu.make_async_copy(turned_s.at[i, place], sides[i][1].at[0, place], out_sems.at[i, k])

    def load_sums(a):
        return pltpu.make_async_copy(sums_hbm.at[a], sums_s.at[a], sum_sems.at[a])

    wide = ((up_s, up_to), (down_s, down_to), (project_s, project_to), (w_out_s, w_out_to))

    def store_wide(i):
        return pltpu.make_async_copy(*wide[i], wide_sems.at[i])

    def turn(i, k):
        load(i, k).wait()
        start, count = cuts[k]
        turned_s[i, start : start + count] = jnp.transpose(lane_s[i, :, start : start + count], (1, 0, 2))
        store(i, k).start()

    load_sums(1).start()
    for k in range(3):
        load(0, k).start()
    load_sums(2).start()
    for k in range(3):
        load(1, k).start()
    load_sums(0).start()
    load_sums(1).wait()
    up_s[...] = sums_s[1].astype(F32)
    store_wide(0).start()
    for k in range(3):
        turn(0, k)
    load_sums(2).wait()
    down_s[...] = sums_s[2].T.astype(F32)
    store_wide(1).start()
    for k in range(3):
        turn(1, k)
    load_sums(0).wait()
    project_s[...] = sums_s[0, :, : 3 * f].astype(F32)
    w_out_s[...] = sums_s[0, :, 3 * f :].astype(F32)
    store_wide(2).start()
    store_wide(3).start()
    vectors = (
        pre_gain_ref, pre_bias_ref, query_bias_ref, out_bias_ref, mid_gain_ref, mid_bias_ref, down_bias_ref,
        value_bias_ref,
    )
    for i, ref in enumerate(vectors):
        ref[...] = small_ref[i]
    for i in range(up_bias_ref.shape[0] // f):
        up_bias_ref[pl.ds(i * f, f)] = small_ref[8 + i]
    for i in range(2):
        for k in range(3):
            store(i, k).wait()
    for i in range(4):
        store_wide(i).wait()


def layer_call(lanes, spatial, f, hidden, tm_count, clip_count, frames, tokens, cotangent, weights):
    pad = -(-spatial // 16) * 16
    rows = GROUP * pad
    smem = pl.BlockSpec(memory_space=pltpu.SMEM)
    vmem = pl.BlockSpec(memory_space=pltpu.VMEM)
    hbm = pl.BlockSpec(memory_space=pl.ANY)
    masks = (clip_count - 1).bit_length()
    sums = [pltpu.VMEM(s, F32) for s in [(f, hidden)] * 3 + [(16, f), (1, hidden)]]
    whole = jax.ShapeDtypeStruct((1, lanes, spatial, f), BF16)
    lane = lambda *s: pltpu.VMEM(s, BF16)
    dma = pltpu.SemaphoreType.DMA((lanes,))
    scratch = sums + [
        lane(lanes, spatial, f), lane(lanes, spatial, f), lane(lanes, spatial, f), lane(lanes, spatial, f),
        lane(lanes, spatial, f),
        lane(lanes, spatial, f), lane(spatial, lanes, f), lane(lanes, spatial, f), lane(lanes, spatial, f), lane(2, GROUP, spatial, f),
        lane(f, 3 * f), lane(f, f), lane(f, hidden), lane(hidden, f),
        lane(2, 3, rows, f), lane(3, GROUP, spatial, f), lane(3, GROUP, spatial, f),
        lane(3, GROUP, f, spatial), lane(3, GROUP, f // HEAD_DIM, HEAD_DIM + 16, spatial), lane(GROUP, f, spatial),
        lane(GROUP, f // HEAD_DIM, 3, spatial, spatial), pltpu.VMEM((GROUP, 8, spatial), F32),
        lane(rows, f), lane(GROUP, f, spatial), pltpu.VMEM((rows, f), F32), lane(rows, f),
        lane(rows, hidden), lane(rows, hidden), lane(rows, f),
        lane(2, rows, f), lane(2, 3, rows, 2 * f), lane(7, f, spatial),
    ] + [dma] * 8 + [pltpu.SemaphoreType.DMA((n,)) for n in (3, 4, 2, lanes // 2)]
    sems = pltpu.SemaphoreType.DMA((96,))
    scratch += [
        lane(f, hidden), lane(3, f // 2, hidden), lane(3, f // 4, hidden),
        lane(3, f // 8, hidden), lane(max(masks - 3, 1), 3, f // 8, hidden), lane(3, tm_count, f // 8, hidden // 4),
        lane(3, f // 8, hidden // 4), pltpu.VMEM((masks + 2, 16, f), F32), sems, sems, pltpu.SemaphoreType.DMA((3,)),
    ]
    return pl.pallas_call(
        functools.partial(layer_kernel, lanes, spatial, f, hidden, tm_count, clip_count),
        in_specs=[smem, hbm, hbm] + [hbm if w.ndim == 2 else vmem for w in weights],
        out_specs=[hbm, hbm, hbm, vmem],
        out_shape=[whole] * 2 + [jax.ShapeDtypeStruct((3, f, hidden), BF16), jax.ShapeDtypeStruct((16, f), F32)],
        scratch_shapes=scratch,
        name="layer",
        compiler_params=pltpu.CompilerParams(
            vmem_limit_bytes=63 * 1024 * 1024, collective_id=0, has_side_effects=True
        ),
        cost_estimate=pl.CostEstimate(flops=100 * 10**9, bytes_accessed=40 * 10**6, transcendentals=0),
    )(frames, tokens, cotangent, *weights)


def body(
    tokens, cotangent, lane_frames, pre_gain, pre_bias, w_project, query_bias, value_bias,
    w_out, out_bias, mid_gain, mid_bias, w_up, up_bias, w_down, down_bias,
):
    lanes, spatial, f = tokens.shape[1:]
    hidden = w_up.shape[1]
    tm_count = lax.axis_size("tm")
    weights = (
        pre_gain, pre_bias, w_project, query_bias, value_bias, w_out, out_bias,
        mid_gain, mid_bias, w_up, up_bias, w_down, down_bias,
    )
    out, input_grad, gathered, small = layer_call(
        lanes, spatial, f, hidden, tm_count, lax.axis_size("clip"), lane_frames,
        tokens.transpose(0, 2, 1, 3), cotangent.transpose(0, 2, 1, 3), weights,
    )
    vmem, hbm = pl.BlockSpec(memory_space=pltpu.VMEM), pl.BlockSpec(memory_space=pl.ANY)
    sizes = [f] * 7 + [hidden, f]
    wide = ((f, 3 * f), (f, f), (f, hidden), (hidden, f))
    dma = lambda *n: pltpu.SemaphoreType.DMA(n)
    got = pl.pallas_call(
        finish_kernel,
        in_specs=[hbm] * 3 + [vmem],
        out_specs=[hbm] * 6 + [vmem] * len(sizes),
        out_shape=[jax.ShapeDtypeStruct((1, spatial, lanes, f), BF16)] * 2
        + [jax.ShapeDtypeStruct(n, F32) for n in wide]
        + [jax.ShapeDtypeStruct((n,), F32) for n in sizes],
        scratch_shapes=[
            pltpu.VMEM((2, lanes, spatial, f), BF16), pltpu.VMEM((2, spatial, lanes, f), BF16),
            pltpu.VMEM((3, f, hidden), BF16),
        ] + [pltpu.VMEM(n, F32) for n in wide] + [dma(2, 3), dma(3), dma(2, 3), dma(4)],
        name="finish",
        compiler_params=pltpu.CompilerParams(vmem_limit_bytes=63 * 1024 * 1024),
    )(out, input_grad, gathered, small)
    out, input_grad = (v.transpose(0, 2, 1, 3) for v in got[:2])
    g_project, g_out, g_up, g_down = got[2:6]
    pre_gain, pre_bias, query_bias, value_bias, out_bias, mid_gain, mid_bias, up_bias, down_bias = got[6:]
    return (
        out, input_grad, pre_gain, pre_bias, g_project, query_bias, value_bias, g_out, out_bias,
        mid_gain, mid_bias, g_up, up_bias, g_down, down_bias,
    )


def solution(mesh):
    spread = P("tm", "clip", None, None)
    return jax.shard_map(
        body,
        mesh=mesh,
        in_specs=(spread, spread, P("clip")) + (P(),) * 13,
        out_specs=(spread, spread) + (P(),) * 13,
        check_vma=False,
    )
```

```python
import functools

import jax
import jax.numpy as jnp
from jax import lax
from jax.experimental import pallas as pl
from jax.experimental.pallas import tpu as pltpu
from jax.sharding import PartitionSpec as P

HEAD_DIM = 64
GROUP = 2
WRAP = 4
MESH = pl.DeviceIdType.MESH
EPSILON = 1e-06
FAR = 1e30
F32 = jnp.float32
BF16 = jnp.bfloat16
NN = (((1,), (0,)), ((), ()))
NT = (((1,), (1,)), ((), ()))
TN = (((0,), (0,)), ((), ()))


def dot(a, b, dims=NN):
    return lax.dot_general(a, b, dims, preferred_element_type=F32)


def row_mean(value):
    return jnp.sum(value, -1, keepdims=True) * (1.0 / value.shape[-1])


def normalise(x):
    center = x - row_mean(x)
    rate = lax.rsqrt(row_mean(center * center) + EPSILON)
    return center * rate, rate


def norm_back(grad, xhat, rate, gain):
    e = grad * gain
    return rate * (e - row_mean(e) - xhat * row_mean(e * xhat))


def gelu_parts(h):
    size = jnp.abs(h)
    bell = jnp.exp(-0.5 * (h * h))
    whole = 1.0 + 0.23164190 * size
    t = pl.reciprocal(whole, approx=True)
    t = t * (2.0 - whole * t)
    poly = t * (0.127414796 + t * (-0.142248368 + t * (0.7107068705 + t * (-0.7265760135 + t * 0.5307027145))))
    tail = poly * bell
    phi = jnp.where(h >= 0.0, 1.0 - tail, tail)
    return jnp.maximum(h, 0.0) - size * tail, phi + h * (bell * 0.3989422804014327)


def column_sum(value):
    return jnp.sum(value, 0, keepdims=True)


UP, DOWN, W = 1, 2, 0
LATE = 1
TAIL = [
    (W, 0), ("rows", 0, 6), (UP, 3), (DOWN, 3), ("trade", 0, "start"), ("lanes", 2), ("trade", 0, "join"), ("trade", 1, "start"), (W, 1), ("trade", 1, "join"), ("trade", 2, "start"), (W, 2),
    ("lanes", 3), ("trade", 2, "join"), ("trade", 3, "start"), (W, 3), (UP, 4), (DOWN, 4), ("trade", 3, "join"), ("trade", 4, "start"), (W, 4), ("give",), (UP, 5), (DOWN, 5),
    (W, 5), (UP, 6), (DOWN, 6), (W, 6), (UP, 7), (DOWN, 7), (W, 7), ("trade", 4, "join"), ("lanes", 4), ("lanes", 5), (UP, 8), (DOWN, 8),
    (W, 8),
]


class Several:
    def __init__(self, copies):
        self.copies = list(copies)

    def start(self):
        for copy in self.copies:
            copy.start()

    def wait(self):
        for copy in self.copies:
            copy.wait()


class Reduction:
    def __init__(
        self, f, hidden, tm, tm_count, masks, bit, across, sums, sends,
        r_core, r_one, r_two, r_more, r_tm, own_chunk, gathered, small, r_small, send_sems, recv_sems, local_sems,
    ):
        self.f, self.hidden, self.tm, self.tm_count = f, hidden, tm, tm_count
        self.masks, self.bit, self.across = masks, bit, across
        self.sums, self.sends = sums, sends
        self.r_core, self.r_one, self.r_two, self.r_more, self.r_tm = r_core, r_one, r_two, r_more, r_tm
        self.own_chunk, self.gathered, self.small, self.r_small = own_chunk, gathered, small, r_small
        self.send_sems, self.recv_sems, self.local_sems = send_sems, recv_sems, local_sems
        half = (len(masks) - 1) // 2
        self.more = masks[2 : 1 + half] + masks[2 + half :]
        one, two = masks[1], masks[1 + half]
        wide = hidden // 2
        self.pieces = [(slice(0, wide), one, two), (slice(wide, hidden), two, one)]
        self.core = bit[1] * (f // 2)
        self.level_one = [self.core + bit[m] * (f // 4) for _, m, _ in self.pieces]
        self.level_two = [at + bit[m] * (f // 8) for at, (_, _, m) in zip(self.level_one, self.pieces)]
        self.used, self.known, self.flying = 0, {}, {}

    def sem(self, name, n=1):
        if name not in self.known:
            self.known[name] = self.used
            self.used += n
        return self.known[name]

    def copy(self, name, src, dst, device):
        at = self.sem(name)
        return pltpu.make_async_remote_copy(
            src_ref=src, dst_ref=dst, send_sem=self.send_sems.at[at], recv_sem=self.recv_sems.at[at],
            device_id=device, device_id_type=MESH,
        )

    def rows(self, at, count):
        return pl.ds(pl.multiple_of(at, 16), count)

    def add(self, a, cols, at, count, got):
        where = self.rows(at, count)
        self.sums[a][where, cols] += got.astype(F32)

    def core_copy(self, a):
        count = self.f // 2
        away = self.rows((1 - self.bit[1]) * count, count)
        return self.copy(("core", a), self.sends[a].at[away, :], self.r_core.at[a], {"clip": self.across[1]})

    def half_copy(self, level, a, i):
        cols, *ms = self.pieces[i]
        count = self.f // (4 * level)
        m = ms[level - 1]
        start = self.core if level == 1 else self.level_one[i]
        away = self.rows(start + (1 - self.bit[m]) * count, count)
        box = (self.r_one, self.r_two)[level - 1]
        return self.copy(
            ("half", level, a, i), self.sends[a].at[away, cols], box.at[a, :, cols], {"clip": self.across[m]}
        )

    def start_half(self, level, a):
        count = self.f // (4 * level)
        for i, (cols, *ms) in enumerate(self.pieces):
            m = ms[level - 1]
            off = (1 - self.bit[m]) * count
            start = self.core if level == 1 else self.level_one[i]
            if level == 1:
                self.add(a, cols, start + off, count, self.r_core[a, self.rows(off, count), cols])
            away = self.rows(start + off, count)
            self.sends[a][away, cols] = self.sums[a][away, cols].astype(BF16)
            self.half_copy(level, a, i).start()
        if level == 1:
            for i, (cols, m, _) in enumerate(self.pieces):
                off = self.bit[m] * count
                self.add(a, cols, self.core + off, count, self.r_core[a, self.rows(off, count), cols])

    def end_half(self, level, a):
        count = self.f // (4 * level)
        for i, (cols, *_) in enumerate(self.pieces):
            self.half_copy(level, a, i).wait()
            at = (self.level_one, self.level_two)[level - 1][i]
            self.add(a, cols, at, count, (self.r_one, self.r_two)[level - 1][a, :, cols])

    def chunk(self, q):
        n = self.hidden // 4
        return slice(q * n, (q + 1) * n), self.rows(self.level_two[q // 2], self.f // 8)

    def chunk_copy(self, a, q):
        cols, here = self.chunk(q)
        return pltpu.make_async_remote_copy(
            src_ref=self.sends[a].at[here, cols], dst_ref=self.r_tm.at[a, self.tm],
            send_sem=self.send_sems.at[self.sem(("leave", a, q))],
            recv_sem=self.recv_sems.at[self.sem(("meet", a), self.tm_count) + self.tm],
            device_id={"tm": q}, device_id_type=MESH,
        )

    def publish(self, a, q, do):
        cols, here = self.chunk(q)
        place, mine = self.gathered.at[a, here, cols], self.own_chunk.at[a]
        local = pltpu.make_async_copy(mine, place, self.local_sems.at[a])
        local.start() if do == "start" else local.wait()
        for other in range(self.tm_count):
            if other != q:
                copy = pltpu.make_async_remote_copy(
                    src_ref=mine, dst_ref=place, send_sem=self.send_sems.at[self.sem(("out", a), self.tm_count) + other],
                    recv_sem=self.recv_sems.at[self.sem(("back", a), self.tm_count) + q],
                    device_id={"tm": other}, device_id_type=MESH,
                )
                copy.start() if do == "start" else copy.wait_send()

    def back_copy(self, level, a, i):
        cols, *ms = self.pieces[i]
        at, count = (self.level_two, self.level_one)[2 - level][i], self.f // (4 * level)
        place = self.gathered.at[a, self.rows(at, count), cols]
        return self.copy(("return", level, a, i), place, place, {"clip": self.across[ms[level - 1]]})

    def core_back(self, a):
        place = self.gathered.at[a, self.rows(self.core, self.f // 2), :]
        return self.copy(("core back", a), place, place, {"clip": self.across[1]})

    def step(self, a, n):
        if n == 0:
            count = self.f // 2
            away = self.rows((1 - self.bit[1]) * count, count)
            self.sends[a][away, :] = self.sums[a][away, :].astype(BF16)
            self.core_copy(a).start()
        elif n == 1:
            self.core_copy(a).wait()
            self.start_half(1, a)
        elif n == 2:
            self.end_half(1, a)
            self.start_half(2, a)
        elif n == 3:
            self.end_half(2, a)
            count = self.f // 8
            for k, m in enumerate(self.more):
                for i, (cols, *_) in enumerate(self.pieces):
                    here = self.rows(self.level_two[i], count)
                    box = self.r_more.at[k, a, :, cols]
                    self.sends[a][here, cols] = self.sums[a][here, cols].astype(BF16)
                    copy = self.copy(("more", k, a, i), self.sends[a].at[here, cols], box, {"clip": self.across[m]})
                    copy.start()
                    copy.wait()
                    self.sums[a][here, cols] = self.sends[a][here, cols].astype(F32) + box[...].astype(F32)
            for q in range(4):

                def send(q=q):
                    cols, here = self.chunk(q)
                    self.sends[a][here, cols] = self.sums[a][here, cols].astype(BF16)
                    self.chunk_copy(a, q).start()

                pl.when(self.tm != q)(send)
        elif n == 4:
            for q in range(4):

                def settle(q=q):
                    cols, here = self.chunk(q)
                    total = self.sums[a][here, cols]
                    for other in range(self.tm_count):
                        if other != q:
                            box = self.r_tm.at[a, other]
                            at = self.sem(("meet", a), self.tm_count) + other
                            pltpu.make_async_copy(box, box, self.recv_sems.at[at]).wait()
                            total += box[...].astype(F32)
                    self.own_chunk[a] = total.astype(BF16)
                    self.publish(a, q, "start")

                pl.when(self.tm == q)(settle)
        elif n == 5:
            for q in range(4):

                def arrive(q=q):
                    self.chunk_copy(a, q).wait_send()
                    cols, here = self.chunk(q)
                    place = self.gathered.at[a, here, cols]
                    at = self.sem(("back", a), self.tm_count) + q
                    pltpu.make_async_copy(place, place, self.recv_sems.at[at]).wait()

                pl.when(self.tm != q)(arrive)
                pl.when(self.tm == q)(functools.partial(self.publish, a, q, "wait"))
            for i in range(2):
                self.back_copy(2, a, i).start()
        elif n == 6:
            for i in range(2):
                self.back_copy(2, a, i).wait()
            for i in range(2):
                self.back_copy(1, a, i).start()
        elif n == 7:
            for i in range(2):
                self.back_copy(1, a, i).wait()
            self.core_back(a).start()
        else:
            self.core_back(a).wait()

    def trade(self, k, do):
        if k < len(self.masks):
            device = {"clip": self.across[self.masks[k]]}
        else:
            m = 1 << (k - len(self.masks))
            device = {"tm": self.tm + m - 2 * m * ((self.tm // m) % 2)}
        copy = self.copy(("small", k), self.small, self.r_small.at[k], device)
        if do == "start":
            copy.start()
        else:
            copy.wait()
            self.small[...] += self.r_small[k]

    def trades(self):
        return len(self.masks) + (self.tm_count - 1).bit_length()


def layer_kernel(
    lanes, spatial, features, hidden, tm_count, clip_count,
    frames_ref, tok_hbm, cot_hbm,
    pre_gain_ref, pre_bias_ref, w_project_hbm, query_bias_ref, value_bias_ref,
    w_out_hbm, out_bias_ref, mid_gain_ref, mid_bias_ref, w_up_hbm, up_bias_ref, w_down_hbm, down_bias_ref,
    out_hbm, grad_hbm, gathered_ref, total_small_ref,
    a_w, a_up, a_down, a_small, a_upb, low_s, up_s, gl_s, above_s, below_s, own_s, raw_s, tok_s, cot_s, out_s,
    w_project_ref, w_out_ref, w_up_ref, w_down_ref, n1_s, k_s, v_s, kt_s, vt_s, qt_s, p_s, inv_s, att_s, attt_s, res_s, n2_s, act_s, gh_s,
    dao_s, dq_s, dkv_s, dt_s,
    send_up, send_down, recv_low, recv_up, send_gl, send_gu, recv_above, recv_below,
    raw_sems, weight_sems, out_sems, own_sems, s_w, r_core, r_one, r_two, r_more, r_tm, own_chunk, r_small, ar_send, ar_recv, ar_local,
):
    f = features
    pad = n1_s.shape[2] // GROUP
    heads = f // HEAD_DIM
    tm = lax.axis_index("tm")
    last = tm_count - 1
    at_low, at_high = tm == 0, tm == last
    higher, lower = lax.rem(tm + 1, tm_count), lax.rem(tm + last, tm_count)
    step_up, step_down = (tm + 1) // tm_count, (tm_count - tm) // tm_count

    def row(ref):
        return ref[...].astype(F32).reshape(1, -1)

    pre_gain, pre_bias, mid_gain, mid_bias = row(pre_gain_ref), row(pre_bias_ref), row(mid_gain_ref), row(mid_bias_ref)
    out_bias, down_bias, up_bias = row(out_bias_ref), row(down_bias_ref), row(up_bias_ref)
    query_bias, value_bias = row(query_bias_ref), row(value_bias_ref)

    def lane_of(g, j):
        return 4 * (g // 2) + (1 - g % 2) * 3 * j + g % 2 * (1 + j)

    def full_lane(l):
        return frames_ref[l] > 0

    def joined(l):
        frames = frames_ref[l]
        inner_low = ((frames == 4 * tm_count) & (l % 2 > 0)) | ((frames == 8 * tm_count) & (l % 4 > 0))
        inner_up = ((frames == 4 * tm_count) & (l % 2 < 1)) | ((frames == 8 * tm_count) & (l % 4 < 3))
        return (frames > 0) & (inner_low | (tm > 0)), (frames > 0) & (inner_up | (tm < last))

    def has_low(l):
        return jnp.logical_or(tm > 0, lax.rem(l, WRAP) != 0)

    def has_up(l):
        return jnp.logical_or(tm < last, lax.rem(l, WRAP) != WRAP - 1)

    def copy(src, dst, send, recv, device):
        return pltpu.make_async_remote_copy(
            src_ref=src, dst_ref=dst, send_sem=send, recv_sem=recv, device_id={"tm": device}, device_id_type=MESH
        )

    def rising(l):
        return copy(gl_s.at[l], low_s.at[l + step_up], send_up.at[l], recv_low.at[l + step_up], higher)

    def falling(l):
        return copy(gl_s.at[l], up_s.at[l - step_down], send_down.at[l], recv_up.at[l - step_down], lower)

    def returning_low(l):
        return copy(gl_s.at[l], above_s.at[l - step_down], send_gl.at[l], recv_above.at[l - step_down], lower)

    def returning_up(l):
        return copy(up_s.at[l], below_s.at[l + step_up], send_gu.at[l], recv_below.at[l + step_up], higher)

    clip = lax.axis_index("clip")
    masks = [1 << i for i in range((clip_count - 1).bit_length())]
    bit = {m: (clip // m) % 2 for m in masks}
    across = {m: clip + m * (1 - 2 * bit[m]) for m in masks}
    others = [lax.rem(tm + i, tm_count) for i in range(1, tm_count)]

    third = spatial // 3 // 16 * 16
    cuts = [(0, third), (third, third), (2 * third, spatial - 2 * third)]

    def raw_copy(hbm, start, count):
        place = pl.ds(start, count)
        return pltpu.make_async_copy(hbm.at[0, place], raw_s.at[place], raw_sems.at[start // third])

    moved = ((w_project_hbm, w_project_ref), (w_out_hbm, w_out_ref), (w_up_hbm, w_up_ref), (w_down_hbm, w_down_ref))
    for start, count in cuts:
        raw_copy(tok_hbm, start, count).start()
    for i, (hbm, ref) in enumerate(moved):
        pltpu.make_async_copy(hbm, ref, weight_sems.at[i]).start()

    barrier = pltpu.get_barrier_semaphore()
    for device in others:
        pl.semaphore_signal(barrier, inc=1, device_id={"tm": device}, device_id_type=MESH)
    for m in masks:
        pl.semaphore_signal(barrier, inc=1, device_id={"clip": across[m]}, device_id_type=MESH)

    def store(g):
        return Several(
            pltpu.make_async_copy(out_s.at[g % 2, j], out_hbm.at[0, lane_of(g, j)], out_sems.at[g % 2, j])
            for j in range(GROUP)
        )

    for start, count in cuts:
        raw_copy(tok_hbm, start, count).wait()
        tok_s[:, start : start + count, :] = jnp.transpose(raw_s[start : start + count], (1, 0, 2))
    for start, count in cuts:
        raw_copy(cot_hbm, start, count).start()
    pl.semaphore_wait(barrier, len(others) + len(masks))

    def start_tokens(block, carry):
        for l in range(WRAP):
            xhat, _ = normalise(tok_s[WRAP * block + l].astype(F32))
            gl_s[WRAP * block + l] = (xhat * pre_gain + pre_bias).astype(BF16)
        for g in range(2):
            for j in range(GROUP):
                k = WRAP * block + lane_of(g, j)
                inner_low, inner_up = lane_of(g, j) != 0, lane_of(g, j) != WRAP - 1
                pl.when(tm < last if not inner_low else tm >= 0)(lambda: rising(k - step_up).start())
                pl.when(tm > 0 if not inner_up else tm >= 0)(lambda: falling(k + step_down).start())
        return carry

    lax.fori_loop(0, lanes // WRAP, start_tokens, 0)
    for start, count in cuts:
        raw_copy(cot_hbm, start, count).wait()
        cot_s[:, start : start + count, :] = jnp.transpose(raw_s[start : start + count], (1, 0, 2))
    for i, (hbm, ref) in enumerate(moved):
        pltpu.make_async_copy(hbm, ref, weight_sems.at[i]).wait()

    def fill(l, carry):
        @pl.when(jnp.logical_not(has_low(l)))
        def _():
            low_s[l] = jnp.zeros(low_s.shape[1:], BF16)
            below_s[l] = jnp.zeros(low_s.shape[1:], BF16)

        @pl.when(jnp.logical_not(has_up(l)))
        def _():
            up_s[l] = jnp.zeros(up_s.shape[1:], BF16)
            above_s[l] = jnp.zeros(up_s.shape[1:], BF16)

        return carry

    lax.fori_loop(0, lanes, fill, 0)

    for new in (a_w, a_up, a_down, a_small, a_upb):
        new[...] = jnp.zeros_like(new)

    vt_s[:, :, :, HEAD_DIM:, :] = jnp.ones((3, GROUP, heads, 16, spatial), BF16)

    def rows_of(j):
        return pl.ds(pl.multiple_of(j * pad, pad), spatial)

    for ref in (n1_s, dq_s, dkv_s):
        ref[...] = jnp.zeros_like(ref)
    for ref in (att_s, dao_s, res_s):
        for j in range(GROUP):
            ref[pl.ds(j * pad + pad - 16, 16), :] = jnp.zeros((16, ref.shape[1]), ref.dtype)

    sums = Reduction(
        f, hidden, tm, tm_count, masks, bit, across, (a_w, a_up, a_down),
        (s_w, act_s.at[pl.ds(0, f), :], gh_s.at[pl.ds(0, f), :]),
        r_core, r_one, r_two, r_more, r_tm, own_chunk, gathered_ref, a_small, r_small, ar_send, ar_recv, ar_local,
    )

    groups = lanes // GROUP

    def in_last(index, *steps):
        @pl.when(index == lanes // GROUP - 1)
        def _():
            for a, n in steps:
                sums.step(a, n)

    def group(index, carry):
        slot = index % 2
        mine = [lane_of(index, j) for j in range(GROUP)]
        pl.when(index >= 2)(lambda: store(index - 2).wait())

        def arrive(j, carry):
            l = lane_of(index, j)
            pl.when(has_low(l))(lambda: copy(gl_s.at[l], low_s.at[l], send_up.at[l], recv_low.at[l], lower).wait_recv())
            pl.when(has_up(l))(lambda: copy(gl_s.at[l], up_s.at[l], send_down.at[l], recv_up.at[l], higher).wait_recv())
            return carry

        lax.fori_loop(0, GROUP, arrive, 0)

        zero_half = jnp.zeros((HEAD_DIM, spatial), BF16)

        def pair_of(h):
            return slice(h // 2 * 2 * HEAD_DIM, (h // 2 + 1) * 2 * HEAD_DIM)

        def mine_of(h):
            return slice(h * HEAD_DIM, (h + 1) * HEAD_DIM)

        def in_pair(h, value):
            return jnp.concatenate([value, zero_half] if h % 2 == 0 else [zero_half, value], 0)

        def project(j, s):
            n1 = (low_s, gl_s, up_s)[s][mine[j]]
            n1_s[slot, s, rows_of(j), :] = n1
            kv = dot(n1, w_project_ref[:, f:])
            k = kv[:, :f].astype(BF16)
            v = (kv[:, f:] + value_bias).astype(BF16)
            k_s[s, j] = k
            v_s[s, j] = v
            kt_s[s, j] = k.T
            vt_s[s, j, :, :HEAD_DIM, :] = v.T.reshape(heads, HEAD_DIM, spatial)
            if s == 1:
                q = (dot(n1, w_project_ref[:, :f]) + query_bias).astype(BF16)
                qt_s[j] = (q * jnp.asarray(HEAD_DIM ** (-0.5), BF16)).T

        def get_scores(j, h):
            qz = in_pair(h, qt_s[j, mine_of(h), :])
            return [dot(k_s[s, j, :, pair_of(h)], qz) for s in range(3)]

        def attend(j, h, scores):
            low_ok, up_ok = joined(mine[j])
            low_far, up_far = jnp.where(low_ok, 0.0, FAR), jnp.where(up_ok, 0.0, FAR)
            tops = [jnp.max(x, 0, keepdims=True) for x in scores]
            top = jnp.maximum(jnp.maximum(tops[0] - low_far, tops[2] - up_far), tops[1])
            attended = None
            for s, shift in enumerate((top + low_far, top, top + up_far)):
                low_prob = jnp.exp(scores[s] - shift).astype(BF16)
                p_s[j, h, s] = low_prob
                got = dot(vt_s[s, j, h], low_prob)
                attended = got if attended is None else attended + got
            inverse = 1.0 / attended[HEAD_DIM : HEAD_DIM + 1, :]
            inv_s[j, h : h + 1, :] = inverse
            attt_s[j, mine_of(h), :] = (attended[:HEAD_DIM, :] * inverse).astype(BF16)

        for s in (1, 0, 2):
            project(0, s)
        steps = [(j, h) for j in range(GROUP) for h in range(heads)]
        beside = {(j, h): [] for j, h in steps}
        for j in range(1, GROUP):
            for s, h in ((1, 0), (0, 2), (2, 4)):
                beside[j - 1, h].append(functools.partial(project, j, s))
        later = get_scores(0, 0)
        for i, (j, h) in enumerate(steps):
            scores = later
            for work in beside[j, h]:
                work()
            if i + 1 < len(steps):
                later = get_scores(*steps[i + 1])
            attend(j, h, scores)
            if h == heads - 1:
                att_s[rows_of(j), :] = attt_s[j].T
                res_s[rows_of(j), :] = tok_s[mine[j]].astype(F32)

        def sent(j, carry):
            l = lane_of(index, j)
            pl.when(has_up(l))(lambda: rising(l).wait_send())
            pl.when(has_low(l))(lambda: falling(l).wait_send())
            return carry

        lax.fori_loop(0, GROUP, sent, 0)

        residual = res_s[...] + dot(att_s[...], w_out_ref[...]) + out_bias
        res_s[...] = residual
        xhat2, rate2 = normalise(residual)
        n2_s[...] = (xhat2 * mid_gain + mid_bias).astype(BF16)
        for j in range(GROUP):
            full = full_lane(mine[j])
            g = cot_s[mine[j]]
            dao_s[pl.ds(j * pad, spatial), :] = jnp.where(full, g.astype(F32), 0.0).astype(BF16)

        wide = 256

        def mlp(c, carry):
            cols = pl.ds(pl.multiple_of(c * wide, wide), wide)
            h = dot(n2_s[...], w_up_ref[:, cols]) + up_bias[:, c * wide : (c + 1) * wide]
            act, slope = gelu_parts(h)
            act_s[:, cols] = act.astype(BF16)
            gh = dot(dao_s[...], w_down_ref[cols, :], NT) * slope
            gh_s[:, cols] = gh.astype(BF16)
            a_upb[:, cols] += column_sum(gh)
            return carry

        before, _, _ = project_back(1 - slot, jnp.maximum(index - 1, 0))
        chunks = hidden // wide
        for c in range(chunks):
            mlp(c, 0)
            for work in before[len(before) * c // chunks : len(before) * (c + 1) // chunks]:
                work()
        a_up[...] += dot(n2_s[...], gh_s[...], TN)
        a_down[...] += dot(dao_s[...], act_s[...], TN)
        total_out = dot(act_s[...], w_down_ref[...]) + down_bias + res_s[...]
        grad_n2 = dot(gh_s[...], w_up_ref[...], NT)
        in_last(index, (1, 0), (2, 0))
        for j in range(GROUP):
            full = full_lane(mine[j])
            rows_out = total_out[j * pad : j * pad + spatial]
            out_s[slot, j] = jnp.where(full, rows_out, tok_s[mine[j]].astype(F32)).astype(BF16)
        store(index).start()
        g = dao_s[...].astype(F32)
        xhat2, rate2 = normalise(res_s[...])
        dres = g + norm_back(grad_n2, xhat2, rate2, mid_gain)
        for j in range(GROUP):
            straight = jnp.where(full_lane(mine[j]), 0.0, cot_s[mine[j]].astype(F32))
            own_s[mine[j]] = (dres[j * pad : j * pad + spatial] + straight).astype(BF16)
        dao = dres.astype(BF16)
        dao_s[...] = dao
        a_small[3:4, :] += column_sum(dao.astype(F32))
        a_small[4:5, :] += column_sum(grad_n2 * xhat2)
        a_small[5:6, :] += column_sum(grad_n2)
        a_small[6:7, :] += column_sum(g)
        a_w[:, 3 * f :] += dot(att_s[...], dao, TN)

        def start_back(j):
            return dot(w_out_ref[...], dao_s[rows_of(j), :], NT).astype(BF16)

        def prepare(j, h, dt):
            dh = dt[mine_of(h), :].astype(F32) * inv_s[j, h : h + 1, :]
            delta = column_sum(dh * attt_s[j, mine_of(h), :].astype(F32))
            dh = dh.astype(BF16)
            dz = in_pair(h, dh)
            return dh, delta, [dot(v_s[s, j, :, pair_of(h)], dz) for s in range(3)]

        def attend_back(j, h, dh, delta, grad_probs):
            place = mine_of(h)
            qh = qt_s[j, place, :]
            probs = [p_s[j, h, s] for s in range(3)]
            for s in range(3):
                dt_s[4 + s, place, :] = dot(dh, probs[s], NT).astype(BF16)
            ds = [(probs[s].astype(F32) * (grad_probs[s] - delta)).astype(BF16) for s in range(3)]
            for s in range(3):
                dt_s[1 + s, place, :] = dot(qh, ds[s], NT).astype(BF16)
            grad_q = None
            for s in range(3):
                got = dot(kt_s[s, j, place, :], ds[s])
                grad_q = got if grad_q is None else grad_q + got
            dt_s[0, place, :] = (grad_q * HEAD_DIM ** (-0.5)).astype(BF16)

        dts = [start_back(j) for j in range(GROUP)]
        later = prepare(0, 0, dts[0])
        for i, (j, h) in enumerate(steps):
            now = later
            if i + 1 < len(steps):
                later = prepare(*steps[i + 1], dts[steps[i + 1][0]])
            attend_back(j, h, *now)
            if (j, h) == steps[len(steps) // 2 - 1]:
                in_last(index, (1, 1), (2, 1))
            if h == heads - 1:
                dq_s[slot, rows_of(j), :] = dt_s[0].T
                for s in range(3):
                    dkv_s[slot, s, rows_of(j), :f] = dt_s[1 + s].T
                    dkv_s[slot, s, rows_of(j), f:] = dt_s[4 + s].T

        in_last(index, (1, 2), (2, 2))
        pl.when(jnp.logical_and(index > 0, index < groups - LATE + 1))(lambda: give_back(index - 1))
        return carry

    def project_back(side, g):
        def weights_q():
            dq = dq_s[side]
            a_w[:, :f] += dot(n1_s[side, 1], dq, TN)
            a_small[2:3, :] += column_sum(dq.astype(F32))

        def weights_kv():
            dkv = dkv_s[side].reshape(3 * GROUP * pad, 2 * f)
            a_w[:, f : 3 * f] += dot(n1_s[side].reshape(3 * GROUP * pad, f), dkv, TN)
            a_small[7:8, :] += column_sum(dkv[:, f:].astype(F32))

        def rows_back(j, s):
            grad = dot(dkv_s[side, s, rows_of(j), :], w_project_ref[:, f:], NT)
            if s == 1:
                grad += dot(dq_s[side, rows_of(j), :], w_project_ref[:, :f], NT)
            a_small[0:1, :] += column_sum(grad * n1_s[side, s, rows_of(j), :].astype(F32))
            a_small[1:2, :] += column_sum(grad)
            (gl_s, low_s, up_s)[s][lane_of(g, j)] = grad.astype(BF16)

        rows_work = [functools.partial(rows_back, j, s) for j in range(GROUP) for s in range(3)]
        return [weights_q] + rows_work[:3] + [weights_kv] + rows_work[3:], [weights_q, weights_kv], rows_work

    def give_back(g):
        def one(j, carry):
            l = lane_of(g, j)
            pl.when(has_low(l))(lambda: returning_low(l).start())
            pl.when(has_up(l))(lambda: returning_up(l).start())
            return carry

        lax.fori_loop(0, GROUP, one, 0)

    lax.fori_loop(0, lanes // GROUP, group, 0)
    _, final_weights, final_rows = project_back((lanes // GROUP - 1) % 2, lanes // GROUP - 1)
    for work in final_weights:
        work()

    def hand_over(pair):
        return Several(
            pltpu.make_async_copy(own_s.at[l], grad_hbm.at[0, l], own_sems.at[l])
            for l in (lane_of(pair, 0), lane_of(pair, 1))
        )

    def handed_over(pair, carry):
        hand_over(pair).wait()
        return carry

    def conclude(pair, carry):
        for l in (lane_of(pair, 0), lane_of(pair, 1)):

            @pl.when(has_up(l))
            def _(l=l):
                returning_up(l).wait_send()
                copy(gl_s.at[l], above_s.at[l], send_gl.at[l], recv_above.at[l], higher).wait_recv()

            @pl.when(has_low(l))
            def _(l=l):
                returning_low(l).wait_send()
                copy(up_s.at[l], below_s.at[l], send_gu.at[l], recv_below.at[l], lower).wait_recv()

        for l in (lane_of(pair, 0), lane_of(pair, 1)):
            grad = low_s[l].astype(F32) + above_s[l].astype(F32) + below_s[l].astype(F32)
            xhat, rate = normalise(tok_s[l].astype(F32))
            own_s[l] = (norm_back(grad, xhat, rate, pre_gain) + own_s[l].astype(F32)).astype(BF16)
        hand_over(pair).start()
        return carry

    for i in range(hidden // f):
        a_small[8 + i : 9 + i, :] = a_upb[:, i * f : (i + 1) * f]
    for g in range(max(lanes // GROUP - 2, 0), lanes // GROUP):
        store(g).wait()
    done = 0
    for what in TAIL:
        if what[0] == "lanes":
            until = lanes // 2 * what[1] // 8
            lax.fori_loop(done, until, conclude, 0)
            done = until
        elif what[0] == "rows":
            for work in final_rows[what[1] : what[2]]:
                work()
        elif what[0] == "give":
            for i in range(LATE, 0, -1):
                give_back(lanes // GROUP - i)
        elif what[0] == "trade":
            sums.trade(what[1], what[2])
        else:
            sums.step(*what)
    lax.fori_loop(done, lanes // 2, conclude, 0)
    for k in range(5, sums.trades()):
        sums.trade(k, "start")
        sums.trade(k, "join")
    lax.fori_loop(0, lanes // 2, handed_over, 0)
    total_small_ref[...] = a_small[...]
    total_small_ref[0:1, :] = (a_small[0:1, :] - pre_bias * a_small[1:2, :]) / pre_gain


def finish_kernel(
    out_hbm, grad_hbm, sums_hbm, small_ref,
    out_to, grad_to, project_to, w_out_to, up_to, down_to,
    pre_gain_ref, pre_bias_ref, query_bias_ref, value_bias_ref, out_bias_ref, mid_gain_ref, mid_bias_ref, up_bias_ref,
    down_bias_ref,
    lane_s, turned_s, sums_s, project_s, w_out_s, up_s, down_s, in_sems, sum_sems, out_sems, wide_sems,
):
    f, spatial = w_out_s.shape[1], lane_s.shape[2]
    third = spatial // 3 // 16 * 16
    cuts = [(0, third), (third, third), (2 * third, spatial - 2 * third)]
    sides = ((out_hbm, out_to), (grad_hbm, grad_to))

    def load(i, k):
        start, count = cuts[k]
        place = pl.ds(start, count)
        return pltpu.make_async_copy(sides[i][0].at[0, :, place], lane_s.at[i, :, place], in_sems.at[i, k])

    def store(i, k):
        start, count = cuts[k]
        place = pl.ds(start, count)
        return pltpu.make_async_copy(turned_s.at[i, place], sides[i][1].at[0, place], out_sems.at[i, k])

    def load_sums(a):
        return pltpu.make_async_copy(sums_hbm.at[a], sums_s.at[a], sum_sems.at[a])

    wide = ((up_s, up_to), (down_s, down_to), (project_s, project_to), (w_out_s, w_out_to))

    def store_wide(i):
        return pltpu.make_async_copy(*wide[i], wide_sems.at[i])

    def turn(i, k):
        load(i, k).wait()
        start, count = cuts[k]
        turned_s[i, start : start + count] = jnp.transpose(lane_s[i, :, start : start + count], (1, 0, 2))
        store(i, k).start()

    load_sums(1).start()
    for k in range(3):
        load(0, k).start()
    load_sums(2).start()
    for k in range(3):
        load(1, k).start()
    load_sums(0).start()
    load_sums(1).wait()
    up_s[...] = sums_s[1].astype(F32)
    store_wide(0).start()
    for k in range(3):
        turn(0, k)
    load_sums(2).wait()
    down_s[...] = sums_s[2].T.astype(F32)
    store_wide(1).start()
    for k in range(3):
        turn(1, k)
    load_sums(0).wait()
    project_s[...] = sums_s[0, :, : 3 * f].astype(F32)
    w_out_s[...] = sums_s[0, :, 3 * f :].astype(F32)
    store_wide(2).start()
    store_wide(3).start()
    vectors = (
        pre_gain_ref, pre_bias_ref, query_bias_ref, out_bias_ref, mid_gain_ref, mid_bias_ref, down_bias_ref,
        value_bias_ref,
    )
    for i, ref in enumerate(vectors):
        ref[...] = small_ref[i]
    for i in range(up_bias_ref.shape[0] // f):
        up_bias_ref[pl.ds(i * f, f)] = small_ref[8 + i]
    for i in range(2):
        for k in range(3):
            store(i, k).wait()
    for i in range(4):
        store_wide(i).wait()


def layer_call(lanes, spatial, f, hidden, tm_count, clip_count, frames, tokens, cotangent, weights):
    pad = -(-spatial // 16) * 16
    rows = GROUP * pad
    smem = pl.BlockSpec(memory_space=pltpu.SMEM)
    vmem = pl.BlockSpec(memory_space=pltpu.VMEM)
    hbm = pl.BlockSpec(memory_space=pl.ANY)
    masks = (clip_count - 1).bit_length()
    sums = [pltpu.VMEM(s, F32) for s in [(f, hidden)] * 3 + [(16, f), (1, hidden)]]
    whole = jax.ShapeDtypeStruct((1, lanes, spatial, f), BF16)
    lane = lambda *s: pltpu.VMEM(s, BF16)
    dma = pltpu.SemaphoreType.DMA((lanes,))
    scratch = sums + [
        lane(lanes, spatial, f), lane(lanes, spatial, f), lane(lanes, spatial, f), lane(lanes, spatial, f),
        lane(lanes, spatial, f),
        lane(lanes, spatial, f), lane(spatial, lanes, f), lane(lanes, spatial, f), lane(lanes, spatial, f), lane(2, GROUP, spatial, f),
        lane(f, 3 * f), lane(f, f), lane(f, hidden), lane(hidden, f),
        lane(2, 3, rows, f), lane(3, GROUP, spatial, f), lane(3, GROUP, spatial, f),
        lane(3, GROUP, f, spatial), lane(3, GROUP, f // HEAD_DIM, HEAD_DIM + 16, spatial), lane(GROUP, f, spatial),
        lane(GROUP, f // HEAD_DIM, 3, spatial, spatial), pltpu.VMEM((GROUP, 8, spatial), F32),
        lane(rows, f), lane(GROUP, f, spatial), pltpu.VMEM((rows, f), F32), lane(rows, f),
        lane(rows, hidden), lane(rows, hidden), lane(rows, f),
        lane(2, rows, f), lane(2, 3, rows, 2 * f), lane(7, f, spatial),
    ] + [dma] * 8 + [pltpu.SemaphoreType.DMA((n,)) for n in (3, 4)] + [
        pltpu.SemaphoreType.DMA((2, GROUP)), pltpu.SemaphoreType.DMA((lanes,))
    ]
    sems = pltpu.SemaphoreType.DMA((96,))
    scratch += [
        lane(f, hidden), lane(3, f // 2, hidden), lane(3, f // 4, hidden),
        lane(3, f // 8, hidden), lane(max(masks - 3, 1), 3, f // 8, hidden), lane(3, tm_count, f // 8, hidden // 4),
        lane(3, f // 8, hidden // 4), pltpu.VMEM((masks + 2, 16, f), F32), sems, sems, pltpu.SemaphoreType.DMA((3,)),
    ]
    return pl.pallas_call(
        functools.partial(layer_kernel, lanes, spatial, f, hidden, tm_count, clip_count),
        in_specs=[smem, hbm, hbm] + [hbm if w.ndim == 2 else vmem for w in weights],
        out_specs=[hbm, hbm, hbm, vmem],
        out_shape=[whole] * 2 + [jax.ShapeDtypeStruct((3, f, hidden), BF16), jax.ShapeDtypeStruct((16, f), F32)],
        scratch_shapes=scratch,
        name="layer",
        compiler_params=pltpu.CompilerParams(
            vmem_limit_bytes=63 * 1024 * 1024, collective_id=0, has_side_effects=True
        ),
        cost_estimate=pl.CostEstimate(flops=100 * 10**9, bytes_accessed=40 * 10**6, transcendentals=0),
    )(frames, tokens, cotangent, *weights)


def body(
    tokens, cotangent, lane_frames, pre_gain, pre_bias, w_project, query_bias, value_bias,
    w_out, out_bias, mid_gain, mid_bias, w_up, up_bias, w_down, down_bias,
):
    lanes, spatial, f = tokens.shape[1:]
    hidden = w_up.shape[1]
    tm_count = lax.axis_size("tm")
    weights = (
        pre_gain, pre_bias, w_project, query_bias, value_bias, w_out, out_bias,
        mid_gain, mid_bias, w_up, up_bias, w_down, down_bias,
    )
    out, input_grad, gathered, small = layer_call(
        lanes, spatial, f, hidden, tm_count, lax.axis_size("clip"), lane_frames,
        tokens.transpose(0, 2, 1, 3), cotangent.transpose(0, 2, 1, 3), weights,
    )
    vmem, hbm = pl.BlockSpec(memory_space=pltpu.VMEM), pl.BlockSpec(memory_space=pl.ANY)
    sizes = [f] * 7 + [hidden, f]
    wide = ((f, 3 * f), (f, f), (f, hidden), (hidden, f))
    dma = lambda *n: pltpu.SemaphoreType.DMA(n)
    got = pl.pallas_call(
        finish_kernel,
        in_specs=[hbm] * 3 + [vmem],
        out_specs=[hbm] * 6 + [vmem] * len(sizes),
        out_shape=[jax.ShapeDtypeStruct((1, spatial, lanes, f), BF16)] * 2
        + [jax.ShapeDtypeStruct(n, F32) for n in wide]
        + [jax.ShapeDtypeStruct((n,), F32) for n in sizes],
        scratch_shapes=[
            pltpu.VMEM((2, lanes, spatial, f), BF16), pltpu.VMEM((2, spatial, lanes, f), BF16),
            pltpu.VMEM((3, f, hidden), BF16),
        ] + [pltpu.VMEM(n, F32) for n in wide] + [dma(2, 3), dma(3), dma(2, 3), dma(4)],
        name="finish",
        compiler_params=pltpu.CompilerParams(vmem_limit_bytes=63 * 1024 * 1024),
    )(out, input_grad, gathered, small)
    out, input_grad = (v.transpose(0, 2, 1, 3) for v in got[:2])
    g_project, g_out, g_up, g_down = got[2:6]
    pre_gain, pre_bias, query_bias, value_bias, out_bias, mid_gain, mid_bias, up_bias, down_bias = got[6:]
    return (
        out, input_grad, pre_gain, pre_bias, g_project, query_bias, value_bias, g_out, out_bias,
        mid_gain, mid_bias, g_up, up_bias, g_down, down_bias,
    )


def solution(mesh):
    spread = P("tm", "clip", None, None)
    return jax.shard_map(
        body,
        mesh=mesh,
        in_specs=(spread, spread, P("clip")) + (P(),) * 13,
        out_specs=(spread, spread) + (P(),) * 13,
        check_vma=False,
    )
```

```python
import functools

import jax
import jax.numpy as jnp
from jax import lax
from jax.experimental import pallas as pl
from jax.experimental.pallas import tpu as pltpu
from jax.sharding import PartitionSpec as P

HEAD_DIM = 64
GROUP = 2
WRAP = 4
MESH = pl.DeviceIdType.MESH
EPSILON = 1e-06
FAR = 1e30
F32 = jnp.float32
BF16 = jnp.bfloat16
NN = (((1,), (0,)), ((), ()))
NT = (((1,), (1,)), ((), ()))
TN = (((0,), (0,)), ((), ()))


def dot(a, b, dims=NN):
    return lax.dot_general(a, b, dims, preferred_element_type=F32)


def row_mean(value):
    return jnp.sum(value, -1, keepdims=True) * (1.0 / value.shape[-1])


def normalise(x):
    center = x - row_mean(x)
    rate = lax.rsqrt(row_mean(center * center) + EPSILON)
    return center * rate, rate


def norm_back(grad, xhat, rate, gain):
    e = grad * gain
    return rate * (e - row_mean(e) - xhat * row_mean(e * xhat))


def gelu_parts(h):
    size = jnp.abs(h)
    bell = jnp.exp(-0.5 * (h * h))
    whole = 1.0 + 0.23164190 * size
    t = pl.reciprocal(whole, approx=True)
    t = t * (2.0 - whole * t)
    poly = t * (0.127414796 + t * (-0.142248368 + t * (0.7107068705 + t * (-0.7265760135 + t * 0.5307027145))))
    tail = poly * bell
    phi = jnp.where(h >= 0.0, 1.0 - tail, tail)
    return jnp.maximum(h, 0.0) - size * tail, phi + h * (bell * 0.3989422804014327)


def column_sum(value):
    return jnp.sum(value, 0, keepdims=True)


UP, DOWN, W = 1, 2, 0
LATE = 1
TAIL = [
    (W, 0), ("rows", 0, 6), (UP, 3), (DOWN, 3), ("trade", 0, "start"), ("lanes", 2), ("trade", 0, "join"), ("trade", 1, "start"), (W, 1), ("trade", 1, "join"), ("trade", 2, "start"), (W, 2),
    ("lanes", 3), ("trade", 2, "join"), ("trade", 3, "start"), (W, 3), (UP, 4), (DOWN, 4), ("trade", 3, "join"), ("trade", 4, "start"), (W, 4), ("give",), (UP, 5), (DOWN, 5),
    (W, 5), (UP, 6), (DOWN, 6), (W, 6), (UP, 7), (DOWN, 7), (W, 7), ("trade", 4, "join"), ("lanes", 4), ("lanes", 5), (UP, 8), (DOWN, 8),
    (W, 8),
]


class Several:
    def __init__(self, copies):
        self.copies = list(copies)

    def start(self):
        for copy in self.copies:
            copy.start()

    def wait(self):
        for copy in self.copies:
            copy.wait()


class Reduction:
    def __init__(
        self, f, hidden, tm, tm_count, masks, bit, across, sums, sends,
        r_core, r_one, r_two, r_more, r_tm, own_chunk, gathered, small, r_small, send_sems, recv_sems, local_sems,
    ):
        self.f, self.hidden, self.tm, self.tm_count = f, hidden, tm, tm_count
        self.masks, self.bit, self.across = masks, bit, across
        self.sums, self.sends = sums, sends
        self.r_core, self.r_one, self.r_two, self.r_more, self.r_tm = r_core, r_one, r_two, r_more, r_tm
        self.own_chunk, self.gathered, self.small, self.r_small = own_chunk, gathered, small, r_small
        self.send_sems, self.recv_sems, self.local_sems = send_sems, recv_sems, local_sems
        half = (len(masks) - 1) // 2
        self.more = masks[2 : 1 + half] + masks[2 + half :]
        one, two = masks[1], masks[1 + half]
        wide = hidden // 2
        self.pieces = [(slice(0, wide), one, two), (slice(wide, hidden), two, one)]
        self.core = bit[1] * (f // 2)
        self.level_one = [self.core + bit[m] * (f // 4) for _, m, _ in self.pieces]
        self.level_two = [at + bit[m] * (f // 8) for at, (_, _, m) in zip(self.level_one, self.pieces)]
        self.used, self.known, self.flying = 0, {}, {}

    def sem(self, name, n=1):
        if name not in self.known:
            self.known[name] = self.used
            self.used += n
        return self.known[name]

    def copy(self, name, src, dst, device):
        at = self.sem(name)
        return pltpu.make_async_remote_copy(
            src_ref=src, dst_ref=dst, send_sem=self.send_sems.at[at], recv_sem=self.recv_sems.at[at],
            device_id=device, device_id_type=MESH,
        )

    def rows(self, at, count):
        return pl.ds(pl.multiple_of(at, 16), count)

    def add(self, a, cols, at, count, got):
        where = self.rows(at, count)
        self.sums[a][where, cols] += got.astype(F32)

    def core_copy(self, a):
        count = self.f // 2
        away = self.rows((1 - self.bit[1]) * count, count)
        return self.copy(("core", a), self.sends[a].at[away, :], self.r_core.at[a], {"clip": self.across[1]})

    def half_copy(self, level, a, i):
        cols, *ms = self.pieces[i]
        count = self.f // (4 * level)
        m = ms[level - 1]
        start = self.core if level == 1 else self.level_one[i]
        away = self.rows(start + (1 - self.bit[m]) * count, count)
        box = (self.r_one, self.r_two)[level - 1]
        return self.copy(
            ("half", level, a, i), self.sends[a].at[away, cols], box.at[a, :, cols], {"clip": self.across[m]}
        )

    def start_half(self, level, a):
        count = self.f // (4 * level)
        for i, (cols, *ms) in enumerate(self.pieces):
            m = ms[level - 1]
            off = (1 - self.bit[m]) * count
            start = self.core if level == 1 else self.level_one[i]
            if level == 1:
                self.add(a, cols, start + off, count, self.r_core[a, self.rows(off, count), cols])
            away = self.rows(start + off, count)
            self.sends[a][away, cols] = self.sums[a][away, cols].astype(BF16)
            self.half_copy(level, a, i).start()
        if level == 1:
            for i, (cols, m, _) in enumerate(self.pieces):
                off = self.bit[m] * count
                self.add(a, cols, self.core + off, count, self.r_core[a, self.rows(off, count), cols])

    def end_half(self, level, a):
        count = self.f // (4 * level)
        for i, (cols, *_) in enumerate(self.pieces):
            self.half_copy(level, a, i).wait()
            at = (self.level_one, self.level_two)[level - 1][i]
            self.add(a, cols, at, count, (self.r_one, self.r_two)[level - 1][a, :, cols])

    def chunk(self, q):
        n = self.hidden // 4
        return slice(q * n, (q + 1) * n), self.rows(self.level_two[q // 2], self.f // 8)

    def chunk_copy(self, a, q):
        cols, here = self.chunk(q)
        return pltpu.make_async_remote_copy(
            src_ref=self.sends[a].at[here, cols], dst_ref=self.r_tm.at[a, self.tm],
            send_sem=self.send_sems.at[self.sem(("leave", a, q))],
            recv_sem=self.recv_sems.at[self.sem(("meet", a), self.tm_count) + self.tm],
            device_id={"tm": q}, device_id_type=MESH,
        )

    def publish(self, a, q, do):
        cols, here = self.chunk(q)
        place, mine = self.gathered.at[a, here, cols], self.own_chunk.at[a]
        local = pltpu.make_async_copy(mine, place, self.local_sems.at[a])
        local.start() if do == "start" else local.wait()
        for other in range(self.tm_count):
            if other != q:
                copy = pltpu.make_async_remote_copy(
                    src_ref=mine, dst_ref=place, send_sem=self.send_sems.at[self.sem(("out", a), self.tm_count) + other],
                    recv_sem=self.recv_sems.at[self.sem(("back", a), self.tm_count) + q],
                    device_id={"tm": other}, device_id_type=MESH,
                )
                copy.start() if do == "start" else copy.wait_send()

    def back_copy(self, level, a, i):
        cols, *ms = self.pieces[i]
        at, count = (self.level_two, self.level_one)[2 - level][i], self.f // (4 * level)
        place = self.gathered.at[a, self.rows(at, count), cols]
        return self.copy(("return", level, a, i), place, place, {"clip": self.across[ms[level - 1]]})

    def core_back(self, a):
        place = self.gathered.at[a, self.rows(self.core, self.f // 2), :]
        return self.copy(("core back", a), place, place, {"clip": self.across[1]})

    def step(self, a, n):
        if n == 0:
            count = self.f // 2
            away = self.rows((1 - self.bit[1]) * count, count)
            self.sends[a][away, :] = self.sums[a][away, :].astype(BF16)
            self.core_copy(a).start()
        elif n == 1:
            self.core_copy(a).wait()
            self.start_half(1, a)
        elif n == 2:
            self.end_half(1, a)
            self.start_half(2, a)
        elif n == 3:
            self.end_half(2, a)
            count = self.f // 8
            for k, m in enumerate(self.more):
                for i, (cols, *_) in enumerate(self.pieces):
                    here = self.rows(self.level_two[i], count)
                    box = self.r_more.at[k, a, :, cols]
                    self.sends[a][here, cols] = self.sums[a][here, cols].astype(BF16)
                    copy = self.copy(("more", k, a, i), self.sends[a].at[here, cols], box, {"clip": self.across[m]})
                    copy.start()
                    copy.wait()
                    self.sums[a][here, cols] = self.sends[a][here, cols].astype(F32) + box[...].astype(F32)
            for q in range(4):

                def send(q=q):
                    cols, here = self.chunk(q)
                    self.sends[a][here, cols] = self.sums[a][here, cols].astype(BF16)
                    self.chunk_copy(a, q).start()

                pl.when(self.tm != q)(send)
        elif n == 4:
            for q in range(4):

                def settle(q=q):
                    cols, here = self.chunk(q)
                    total = self.sums[a][here, cols]
                    for other in range(self.tm_count):
                        if other != q:
                            box = self.r_tm.at[a, other]
                            at = self.sem(("meet", a), self.tm_count) + other
                            pltpu.make_async_copy(box, box, self.recv_sems.at[at]).wait()
                            total += box[...].astype(F32)
                    self.own_chunk[a] = total.astype(BF16)
                    self.publish(a, q, "start")

                pl.when(self.tm == q)(settle)
        elif n == 5:
            for q in range(4):

                def arrive(q=q):
                    self.chunk_copy(a, q).wait_send()
                    cols, here = self.chunk(q)
                    place = self.gathered.at[a, here, cols]
                    at = self.sem(("back", a), self.tm_count) + q
                    pltpu.make_async_copy(place, place, self.recv_sems.at[at]).wait()

                pl.when(self.tm != q)(arrive)
                pl.when(self.tm == q)(functools.partial(self.publish, a, q, "wait"))
            for i in range(2):
                self.back_copy(2, a, i).start()
        elif n == 6:
            for i in range(2):
                self.back_copy(2, a, i).wait()
            for i in range(2):
                self.back_copy(1, a, i).start()
        elif n == 7:
            for i in range(2):
                self.back_copy(1, a, i).wait()
            self.core_back(a).start()
        else:
            self.core_back(a).wait()

    def trade(self, k, do):
        if k < len(self.masks):
            device = {"clip": self.across[self.masks[k]]}
        else:
            m = 1 << (k - len(self.masks))
            device = {"tm": self.tm + m - 2 * m * ((self.tm // m) % 2)}
        copy = self.copy(("small", k), self.small, self.r_small.at[k], device)
        if do == "start":
            copy.start()
        else:
            copy.wait()
            self.small[...] += self.r_small[k]

    def trades(self):
        return len(self.masks) + (self.tm_count - 1).bit_length()


def layer_kernel(
    lanes, spatial, features, hidden, tm_count, clip_count,
    frames_ref, tok_hbm, cot_hbm,
    pre_gain_ref, pre_bias_ref, w_project_hbm, query_bias_ref, value_bias_ref,
    w_out_hbm, out_bias_ref, mid_gain_ref, mid_bias_ref, w_up_hbm, up_bias_ref, w_down_hbm, down_bias_ref,
    out_hbm, grad_hbm, gathered_ref, total_small_ref,
    a_w, a_up, a_down, a_small, a_upb, low_s, up_s, gl_s, above_s, below_s, own_s, raw_s, tok_s, cot_s, out_s,
    w_project_ref, w_out_ref, w_up_ref, w_down_ref, n1_s, k_s, v_s, kt_s, vt_s, qt_s, p_s, inv_s, att_s, attt_s, res_s, n2_s, act_s, gh_s,
    dao_s, dq_s, dkv_s, dt_s,
    send_up, send_down, recv_low, recv_up, send_gl, send_gu, recv_above, recv_below,
    raw_sems, weight_sems, out_sems, own_sems, s_w, r_core, r_one, r_two, r_more, r_tm, own_chunk, r_small, ar_send, ar_recv, ar_local,
):
    f = features
    pad = n1_s.shape[2] // GROUP
    heads = f // HEAD_DIM
    tm = lax.axis_index("tm")
    last = tm_count - 1
    at_low, at_high = tm == 0, tm == last
    higher, lower = lax.rem(tm + 1, tm_count), lax.rem(tm + last, tm_count)
    step_up, step_down = (tm + 1) // tm_count, (tm_count - tm) // tm_count

    def row(ref):
        return ref[...].astype(F32).reshape(1, -1)

    pre_gain, pre_bias, mid_gain, mid_bias = row(pre_gain_ref), row(pre_bias_ref), row(mid_gain_ref), row(mid_bias_ref)
    out_bias, down_bias, up_bias = row(out_bias_ref), row(down_bias_ref), row(up_bias_ref)
    query_bias, value_bias = row(query_bias_ref), row(value_bias_ref)

    def lane_of(g, j):
        four, blocks = g // 2, lanes // 4
        inner = (g + (four + blocks - 1) // blocks) % 2
        return 4 * four + (1 - inner) * 3 * j + inner * (1 + j)

    def full_lane(l):
        return frames_ref[l] > 0

    def joined(l):
        frames = frames_ref[l]
        inner_low = ((frames == 4 * tm_count) & (l % 2 > 0)) | ((frames == 8 * tm_count) & (l % 4 > 0))
        inner_up = ((frames == 4 * tm_count) & (l % 2 < 1)) | ((frames == 8 * tm_count) & (l % 4 < 3))
        return (frames > 0) & (inner_low | (tm > 0)), (frames > 0) & (inner_up | (tm < last))

    def has_low(l):
        return jnp.logical_or(tm > 0, lax.rem(l, WRAP) != 0)

    def has_up(l):
        return jnp.logical_or(tm < last, lax.rem(l, WRAP) != WRAP - 1)

    def copy(src, dst, send, recv, device):
        return pltpu.make_async_remote_copy(
            src_ref=src, dst_ref=dst, send_sem=send, recv_sem=recv, device_id={"tm": device}, device_id_type=MESH
        )

    def rising(l):
        return copy(gl_s.at[l], low_s.at[l + step_up], send_up.at[l], recv_low.at[l + step_up], higher)

    def falling(l):
        return copy(gl_s.at[l], up_s.at[l - step_down], send_down.at[l], recv_up.at[l - step_down], lower)

    def returning_low(l):
        return copy(gl_s.at[l], above_s.at[l - step_down], send_gl.at[l], recv_above.at[l - step_down], lower)

    def returning_up(l):
        return copy(up_s.at[l], below_s.at[l + step_up], send_gu.at[l], recv_below.at[l + step_up], higher)

    clip = lax.axis_index("clip")
    masks = [1 << i for i in range((clip_count - 1).bit_length())]
    bit = {m: (clip // m) % 2 for m in masks}
    across = {m: clip + m * (1 - 2 * bit[m]) for m in masks}
    others = [lax.rem(tm + i, tm_count) for i in range(1, tm_count)]

    third = spatial // 3 // 16 * 16
    cuts = [(0, third), (third, third), (2 * third, spatial - 2 * third)]

    def raw_copy(hbm, start, count):
        place = pl.ds(start, count)
        return pltpu.make_async_copy(hbm.at[0, place], raw_s.at[place], raw_sems.at[start // third])

    moved = ((w_project_hbm, w_project_ref), (w_out_hbm, w_out_ref), (w_up_hbm, w_up_ref), (w_down_hbm, w_down_ref))
    for start, count in cuts:
        raw_copy(tok_hbm, start, count).start()
    for i, (hbm, ref) in enumerate(moved):
        pltpu.make_async_copy(hbm, ref, weight_sems.at[i]).start()

    barrier = pltpu.get_barrier_semaphore()
    for device in others:
        pl.semaphore_signal(barrier, inc=1, device_id={"tm": device}, device_id_type=MESH)
    for m in masks:
        pl.semaphore_signal(barrier, inc=1, device_id={"clip": across[m]}, device_id_type=MESH)

    def store(g):
        return Several(
            pltpu.make_async_copy(out_s.at[g % 2, j], out_hbm.at[0, lane_of(g, j)], out_sems.at[g % 2, j])
            for j in range(GROUP)
        )

    for start, count in cuts:
        raw_copy(tok_hbm, start, count).wait()
        tok_s[:, start : start + count, :] = jnp.transpose(raw_s[start : start + count], (1, 0, 2))
    for start, count in cuts:
        raw_copy(cot_hbm, start, count).start()
    pl.semaphore_wait(barrier, len(others) + len(masks))

    def start_tokens(block, carry, order=(1, 0)):
        for l in range(WRAP):
            xhat, _ = normalise(tok_s[WRAP * block + l].astype(F32))
            gl_s[WRAP * block + l] = (xhat * pre_gain + pre_bias).astype(BF16)
        for g in order:
            for j in range(GROUP):
                k = WRAP * block + lane_of(g, j)
                inner_low, inner_up = lane_of(g, j) != 0, lane_of(g, j) != WRAP - 1
                pl.when(tm < last if not inner_low else tm >= 0)(lambda: rising(k - step_up).start())
                pl.when(tm > 0 if not inner_up else tm >= 0)(lambda: falling(k + step_down).start())
        return carry

    start_tokens(0, 0, (0, 1))
    lax.fori_loop(1, lanes // WRAP, start_tokens, 0)
    for start, count in cuts:
        raw_copy(cot_hbm, start, count).wait()
        cot_s[:, start : start + count, :] = jnp.transpose(raw_s[start : start + count], (1, 0, 2))
    for i, (hbm, ref) in enumerate(moved):
        pltpu.make_async_copy(hbm, ref, weight_sems.at[i]).wait()

    def fill(l, carry):
        @pl.when(jnp.logical_not(has_low(l)))
        def _():
            low_s[l] = jnp.zeros(low_s.shape[1:], BF16)
            below_s[l] = jnp.zeros(low_s.shape[1:], BF16)

        @pl.when(jnp.logical_not(has_up(l)))
        def _():
            up_s[l] = jnp.zeros(up_s.shape[1:], BF16)
            above_s[l] = jnp.zeros(up_s.shape[1:], BF16)

        return carry

    lax.fori_loop(0, lanes, fill, 0)

    for new in (a_w, a_up, a_down, a_small, a_upb):
        new[...] = jnp.zeros_like(new)

    vt_s[:, :, :, HEAD_DIM:, :] = jnp.ones((3, GROUP, heads, 16, spatial), BF16)

    def rows_of(j):
        return pl.ds(pl.multiple_of(j * pad, pad), spatial)

    for ref in (n1_s, dq_s, dkv_s):
        ref[...] = jnp.zeros_like(ref)
    for ref in (att_s, dao_s, res_s):
        for j in range(GROUP):
            ref[pl.ds(j * pad + pad - 16, 16), :] = jnp.zeros((16, ref.shape[1]), ref.dtype)

    sums = Reduction(
        f, hidden, tm, tm_count, masks, bit, across, (a_w, a_up, a_down),
        (s_w, act_s.at[pl.ds(0, f), :], gh_s.at[pl.ds(0, f), :]),
        r_core, r_one, r_two, r_more, r_tm, own_chunk, gathered_ref, a_small, r_small, ar_send, ar_recv, ar_local,
    )

    groups = lanes // GROUP

    def in_last(index, *steps):
        @pl.when(index == lanes // GROUP - 1)
        def _():
            for a, n in steps:
                sums.step(a, n)

    def group(index, carry):
        slot = index % 2
        mine = [lane_of(index, j) for j in range(GROUP)]
        pl.when(index >= 2)(lambda: store(index - 2).wait())

        def arrive(j, carry):
            l = lane_of(index, j)
            pl.when(has_low(l))(lambda: copy(gl_s.at[l], low_s.at[l], send_up.at[l], recv_low.at[l], lower).wait_recv())
            pl.when(has_up(l))(lambda: copy(gl_s.at[l], up_s.at[l], send_down.at[l], recv_up.at[l], higher).wait_recv())
            return carry

        lax.fori_loop(0, GROUP, arrive, 0)

        zero_half = jnp.zeros((HEAD_DIM, spatial), BF16)

        def pair_of(h):
            return slice(h // 2 * 2 * HEAD_DIM, (h // 2 + 1) * 2 * HEAD_DIM)

        def mine_of(h):
            return slice(h * HEAD_DIM, (h + 1) * HEAD_DIM)

        def in_pair(h, value):
            return jnp.concatenate([value, zero_half] if h % 2 == 0 else [zero_half, value], 0)

        def project(j, s):
            n1 = (low_s, gl_s, up_s)[s][mine[j]]
            n1_s[slot, s, rows_of(j), :] = n1
            kv = dot(n1, w_project_ref[:, f:])
            k = kv[:, :f].astype(BF16)
            v = (kv[:, f:] + value_bias).astype(BF16)
            k_s[s, j] = k
            v_s[s, j] = v
            kt_s[s, j] = k.T
            vt_s[s, j, :, :HEAD_DIM, :] = v.T.reshape(heads, HEAD_DIM, spatial)
            if s == 1:
                q = (dot(n1, w_project_ref[:, :f]) + query_bias).astype(BF16)
                qt_s[j] = (q * jnp.asarray(HEAD_DIM ** (-0.5), BF16)).T

        def get_scores(j, h):
            qz = in_pair(h, qt_s[j, mine_of(h), :])
            return [dot(k_s[s, j, :, pair_of(h)], qz) for s in range(3)]

        def attend(j, h, scores):
            low_ok, up_ok = joined(mine[j])
            low_far, up_far = jnp.where(low_ok, 0.0, FAR), jnp.where(up_ok, 0.0, FAR)
            tops = [jnp.max(x, 0, keepdims=True) for x in scores]
            top = jnp.maximum(jnp.maximum(tops[0] - low_far, tops[2] - up_far), tops[1])
            attended = None
            for s, shift in enumerate((top + low_far, top, top + up_far)):
                low_prob = jnp.exp(scores[s] - shift).astype(BF16)
                p_s[j, h, s] = low_prob
                got = dot(vt_s[s, j, h], low_prob)
                attended = got if attended is None else attended + got
            inverse = 1.0 / attended[HEAD_DIM : HEAD_DIM + 1, :]
            inv_s[j, h : h + 1, :] = inverse
            attt_s[j, mine_of(h), :] = (attended[:HEAD_DIM, :] * inverse).astype(BF16)

        for s in (1, 0, 2):
            project(0, s)
        steps = [(j, h) for j in range(GROUP) for h in range(heads)]
        beside = {(j, h): [] for j, h in steps}
        for j in range(1, GROUP):
            for s, h in ((1, 0), (0, 2), (2, 4)):
                beside[j - 1, h].append(functools.partial(project, j, s))
        later = get_scores(0, 0)
        for i, (j, h) in enumerate(steps):
            scores = later
            for work in beside[j, h]:
                work()
            if i + 1 < len(steps):
                later = get_scores(*steps[i + 1])
            attend(j, h, scores)
            if h == heads - 1:
                att_s[rows_of(j), :] = attt_s[j].T
                res_s[rows_of(j), :] = tok_s[mine[j]].astype(F32)

        pl.when(index > 0)(lambda: sent(index - 1))
        residual = res_s[...] + dot(att_s[...], w_out_ref[...]) + out_bias
        res_s[...] = residual
        xhat2, rate2 = normalise(residual)
        n2_s[...] = (xhat2 * mid_gain + mid_bias).astype(BF16)
        for j in range(GROUP):
            full = full_lane(mine[j])
            g = cot_s[mine[j]]
            dao_s[pl.ds(j * pad, spatial), :] = jnp.where(full, g.astype(F32), 0.0).astype(BF16)

        wide = 256

        def mlp(c, carry):
            cols = pl.ds(pl.multiple_of(c * wide, wide), wide)
            h = dot(n2_s[...], w_up_ref[:, cols]) + up_bias[:, c * wide : (c + 1) * wide]
            act, slope = gelu_parts(h)
            act_s[:, cols] = act.astype(BF16)
            gh = dot(dao_s[...], w_down_ref[cols, :], NT) * slope
            gh_s[:, cols] = gh.astype(BF16)
            a_upb[:, cols] += column_sum(gh)
            return carry

        before, _, _ = project_back(1 - slot, jnp.maximum(index - 1, 0), index > 0)
        chunks = hidden // wide
        for c in range(chunks):
            mlp(c, 0)
            for work in before[len(before) * c // chunks : len(before) * (c + 1) // chunks]:
                work()
        a_up[...] += dot(n2_s[...], gh_s[...], TN)
        a_down[...] += dot(dao_s[...], act_s[...], TN)
        total_out = dot(act_s[...], w_down_ref[...]) + down_bias + res_s[...]
        grad_n2 = dot(gh_s[...], w_up_ref[...], NT)
        in_last(index, (1, 0), (2, 0))
        for j in range(GROUP):
            full = full_lane(mine[j])
            rows_out = total_out[j * pad : j * pad + spatial]
            out_s[slot, j] = jnp.where(full, rows_out, tok_s[mine[j]].astype(F32)).astype(BF16)
        store(index).start()
        g = dao_s[...].astype(F32)
        xhat2, rate2 = normalise(res_s[...])
        dres = g + norm_back(grad_n2, xhat2, rate2, mid_gain)
        for j in range(GROUP):
            straight = jnp.where(full_lane(mine[j]), 0.0, cot_s[mine[j]].astype(F32))
            own_s[mine[j]] = (dres[j * pad : j * pad + spatial] + straight).astype(BF16)
        dao = dres.astype(BF16)
        dao_s[...] = dao
        a_small[3:4, :] += column_sum(dao.astype(F32))
        a_small[4:5, :] += column_sum(grad_n2 * xhat2)
        a_small[5:6, :] += column_sum(grad_n2)
        a_small[6:7, :] += column_sum(g)
        a_w[:, 3 * f :] += dot(att_s[...], dao, TN)

        def start_back(j):
            return dot(w_out_ref[...], dao_s[rows_of(j), :], NT).astype(BF16)

        def prepare(j, h, dt):
            dh = dt[mine_of(h), :].astype(F32) * inv_s[j, h : h + 1, :]
            delta = column_sum(dh * attt_s[j, mine_of(h), :].astype(F32))
            dh = dh.astype(BF16)
            dz = in_pair(h, dh)
            return dh, delta, [dot(v_s[s, j, :, pair_of(h)], dz) for s in range(3)]

        def attend_back(j, h, dh, delta, grad_probs):
            place = mine_of(h)
            qh = qt_s[j, place, :]
            probs = [p_s[j, h, s] for s in range(3)]
            for s in range(3):
                dt_s[4 + s, place, :] = dot(dh, probs[s], NT).astype(BF16)
            ds = [(probs[s].astype(F32) * (grad_probs[s] - delta)).astype(BF16) for s in range(3)]
            for s in range(3):
                dt_s[1 + s, place, :] = dot(qh, ds[s], NT).astype(BF16)
            grad_q = None
            for s in range(3):
                got = dot(kt_s[s, j, place, :], ds[s])
                grad_q = got if grad_q is None else grad_q + got
            dt_s[0, place, :] = (grad_q * HEAD_DIM ** (-0.5)).astype(BF16)

        dts = [start_back(j) for j in range(GROUP)]
        later = prepare(0, 0, dts[0])
        for i, (j, h) in enumerate(steps):
            now = later
            if i + 1 < len(steps):
                later = prepare(*steps[i + 1], dts[steps[i + 1][0]])
            attend_back(j, h, *now)
            if (j, h) == steps[len(steps) // 2 - 1]:
                in_last(index, (1, 1), (2, 1))
            if h == heads - 1:
                dq_s[slot, rows_of(j), :] = dt_s[0].T
                for s in range(3):
                    dkv_s[slot, s, rows_of(j), :f] = dt_s[1 + s].T
                    dkv_s[slot, s, rows_of(j), f:] = dt_s[4 + s].T

        in_last(index, (1, 2), (2, 2))
        pl.when(jnp.logical_and(index > 0, index < groups - LATE + 1))(lambda: give_back(index - 1))
        return carry

    def sent(g):
        def one(j, carry):
            l = lane_of(g, j)
            pl.when(has_up(l))(lambda: rising(l).wait_send())
            pl.when(has_low(l))(lambda: falling(l).wait_send())
            return carry

        lax.fori_loop(0, GROUP, one, 0)

    def project_back(side, g, real=True):
        def weights_q():
            dq = dq_s[side]
            a_w[:, :f] += dot(n1_s[side, 1], dq, TN)
            a_small[2:3, :] += column_sum(dq.astype(F32))

        def weights_kv():
            dkv = dkv_s[side].reshape(3 * GROUP * pad, 2 * f)
            a_w[:, f : 3 * f] += dot(n1_s[side].reshape(3 * GROUP * pad, f), dkv, TN)
            a_small[7:8, :] += column_sum(dkv[:, f:].astype(F32))

        def rows_back(j, s):
            grad = dot(dkv_s[side, s, rows_of(j), :], w_project_ref[:, f:], NT)
            if s == 1:
                grad += dot(dq_s[side, rows_of(j), :], w_project_ref[:, :f], NT)
            a_small[0:1, :] += column_sum(grad * n1_s[side, s, rows_of(j), :].astype(F32))
            a_small[1:2, :] += column_sum(grad)
            place = lane_of(g, j)
            if s == 0:
                place = jnp.where(real, place, lanes + j)
            (gl_s, low_s, up_s)[s][place] = grad.astype(BF16)

        rows_work = [functools.partial(rows_back, j, s) for j in range(GROUP) for s in range(3)]
        return [weights_q] + rows_work[:3] + [weights_kv] + rows_work[3:], [weights_q, weights_kv], rows_work

    def give_back(g):
        def one(j, carry):
            l = lane_of(g, j)
            pl.when(has_low(l))(lambda: returning_low(l).start())
            pl.when(has_up(l))(lambda: returning_up(l).start())
            return carry

        lax.fori_loop(0, GROUP, one, 0)

    lax.fori_loop(0, lanes // GROUP, group, 0)
    _, final_weights, final_rows = project_back((lanes // GROUP - 1) % 2, lanes // GROUP - 1)
    for work in final_weights:
        work()
    sent(groups - 1)

    def hand_over(pair):
        return Several(
            pltpu.make_async_copy(own_s.at[l], grad_hbm.at[0, l], own_sems.at[l])
            for l in (lane_of(pair, 0), lane_of(pair, 1))
        )

    def handed_over(pair, carry):
        hand_over(pair).wait()
        return carry

    def conclude(pair, carry):
        for l in (lane_of(pair, 0), lane_of(pair, 1)):

            @pl.when(has_up(l))
            def _(l=l):
                returning_up(l).wait_send()
                copy(gl_s.at[l], above_s.at[l], send_gl.at[l], recv_above.at[l], higher).wait_recv()

            @pl.when(has_low(l))
            def _(l=l):
                returning_low(l).wait_send()
                copy(up_s.at[l], below_s.at[l], send_gu.at[l], recv_below.at[l], lower).wait_recv()

        for l in (lane_of(pair, 0), lane_of(pair, 1)):
            grad = low_s[l].astype(F32) + above_s[l].astype(F32) + below_s[l].astype(F32)
            xhat, rate = normalise(tok_s[l].astype(F32))
            own_s[l] = (norm_back(grad, xhat, rate, pre_gain) + own_s[l].astype(F32)).astype(BF16)
        hand_over(pair).start()
        return carry

    for i in range(hidden // f):
        a_small[8 + i : 9 + i, :] = a_upb[:, i * f : (i + 1) * f]
    for g in range(max(lanes // GROUP - 2, 0), lanes // GROUP):
        store(g).wait()
    done = 0
    for what in TAIL:
        if what[0] == "lanes":
            until = lanes // 2 * what[1] // 8
            lax.fori_loop(done, until, conclude, 0)
            done = until
        elif what[0] == "rows":
            for work in final_rows[what[1] : what[2]]:
                work()
        elif what[0] == "give":
            for i in range(LATE, 0, -1):
                give_back(lanes // GROUP - i)
        elif what[0] == "trade":
            sums.trade(what[1], what[2])
        else:
            sums.step(*what)
    lax.fori_loop(done, lanes // 2, conclude, 0)
    for k in range(5, sums.trades()):
        sums.trade(k, "start")
        sums.trade(k, "join")
    lax.fori_loop(0, lanes // 2, handed_over, 0)
    total_small_ref[...] = a_small[...]
    total_small_ref[0:1, :] = (a_small[0:1, :] - pre_bias * a_small[1:2, :]) / pre_gain


def finish_kernel(
    out_hbm, grad_hbm, sums_hbm, small_ref,
    out_to, grad_to, project_to, w_out_to, up_to, down_to,
    pre_gain_ref, pre_bias_ref, query_bias_ref, value_bias_ref, out_bias_ref, mid_gain_ref, mid_bias_ref, up_bias_ref,
    down_bias_ref,
    lane_s, turned_s, sums_s, project_s, w_out_s, up_s, down_s, in_sems, sum_sems, out_sems, wide_sems,
):
    f, spatial = w_out_s.shape[1], lane_s.shape[2]
    third = spatial // 3 // 16 * 16
    cuts = [(0, third), (third, third), (2 * third, spatial - 2 * third)]
    sides = ((out_hbm, out_to), (grad_hbm, grad_to))

    def load(i, k):
        start, count = cuts[k]
        place = pl.ds(start, count)
        return pltpu.make_async_copy(sides[i][0].at[0, :, place], lane_s.at[i, :, place], in_sems.at[i, k])

    def store(i, k):
        start, count = cuts[k]
        place = pl.ds(start, count)
        return pltpu.make_async_copy(turned_s.at[i, place], sides[i][1].at[0, place], out_sems.at[i, k])

    def load_sums(a):
        return pltpu.make_async_copy(sums_hbm.at[a], sums_s.at[a], sum_sems.at[a])

    wide = ((up_s, up_to), (down_s, down_to), (project_s, project_to), (w_out_s, w_out_to))

    def store_wide(i):
        return pltpu.make_async_copy(*wide[i], wide_sems.at[i])

    def turn(i, k):
        load(i, k).wait()
        start, count = cuts[k]
        turned_s[i, start : start + count] = jnp.transpose(lane_s[i, :, start : start + count], (1, 0, 2))
        store(i, k).start()

    load_sums(1).start()
    for k in range(3):
        load(0, k).start()
    load_sums(2).start()
    for k in range(3):
        load(1, k).start()
    load_sums(0).start()
    load_sums(1).wait()
    up_s[...] = sums_s[1].astype(F32)
    store_wide(0).start()
    for k in range(3):
        turn(0, k)
    load_sums(2).wait()
    down_s[...] = sums_s[2].T.astype(F32)
    store_wide(1).start()
    for k in range(3):
        turn(1, k)
    load_sums(0).wait()
    project_s[...] = sums_s[0, :, : 3 * f].astype(F32)
    w_out_s[...] = sums_s[0, :, 3 * f :].astype(F32)
    store_wide(2).start()
    store_wide(3).start()
    vectors = (
        pre_gain_ref, pre_bias_ref, query_bias_ref, out_bias_ref, mid_gain_ref, mid_bias_ref, down_bias_ref,
        value_bias_ref,
    )
    for i, ref in enumerate(vectors):
        ref[...] = small_ref[i]
    for i in range(up_bias_ref.shape[0] // f):
        up_bias_ref[pl.ds(i * f, f)] = small_ref[8 + i]
    for i in range(2):
        for k in range(3):
            store(i, k).wait()
    for i in range(4):
        store_wide(i).wait()


def layer_call(lanes, spatial, f, hidden, tm_count, clip_count, frames, tokens, cotangent, weights):
    pad = -(-spatial // 16) * 16
    rows = GROUP * pad
    smem = pl.BlockSpec(memory_space=pltpu.SMEM)
    vmem = pl.BlockSpec(memory_space=pltpu.VMEM)
    hbm = pl.BlockSpec(memory_space=pl.ANY)
    masks = (clip_count - 1).bit_length()
    sums = [pltpu.VMEM(s, F32) for s in [(f, hidden)] * 3 + [(16, f), (1, hidden)]]
    whole = jax.ShapeDtypeStruct((1, lanes, spatial, f), BF16)
    lane = lambda *s: pltpu.VMEM(s, BF16)
    dma = pltpu.SemaphoreType.DMA((lanes,))
    scratch = sums + [
        lane(lanes, spatial, f), lane(lanes, spatial, f), lane(lanes + GROUP, spatial, f), lane(lanes, spatial, f),
        lane(lanes, spatial, f),
        lane(lanes, spatial, f), lane(spatial, lanes, f), lane(lanes, spatial, f), lane(lanes, spatial, f), lane(2, GROUP, spatial, f),
        lane(f, 3 * f), lane(f, f), lane(f, hidden), lane(hidden, f),
        lane(2, 3, rows, f), lane(3, GROUP, spatial, f), lane(3, GROUP, spatial, f),
        lane(3, GROUP, f, spatial), lane(3, GROUP, f // HEAD_DIM, HEAD_DIM + 16, spatial), lane(GROUP, f, spatial),
        lane(GROUP, f // HEAD_DIM, 3, spatial, spatial), pltpu.VMEM((GROUP, 8, spatial), F32),
        lane(rows, f), lane(GROUP, f, spatial), pltpu.VMEM((rows, f), F32), lane(rows, f),
        lane(rows, hidden), lane(rows, hidden), lane(rows, f),
        lane(2, rows, f), lane(2, 3, rows, 2 * f), lane(7, f, spatial),
    ] + [dma] * 8 + [pltpu.SemaphoreType.DMA((n,)) for n in (3, 4)] + [
        pltpu.SemaphoreType.DMA((2, GROUP)), pltpu.SemaphoreType.DMA((lanes,))
    ]
    sems = pltpu.SemaphoreType.DMA((96,))
    scratch += [
        lane(f, hidden), lane(3, f // 2, hidden), lane(3, f // 4, hidden),
        lane(3, f // 8, hidden), lane(max(masks - 3, 1), 3, f // 8, hidden), lane(3, tm_count, f // 8, hidden // 4),
        lane(3, f // 8, hidden // 4), pltpu.VMEM((masks + 2, 16, f), F32), sems, sems, pltpu.SemaphoreType.DMA((3,)),
    ]
    return pl.pallas_call(
        functools.partial(layer_kernel, lanes, spatial, f, hidden, tm_count, clip_count),
        in_specs=[smem, hbm, hbm] + [hbm if w.ndim == 2 else vmem for w in weights],
        out_specs=[hbm, hbm, hbm, vmem],
        out_shape=[whole] * 2 + [jax.ShapeDtypeStruct((3, f, hidden), BF16), jax.ShapeDtypeStruct((16, f), F32)],
        scratch_shapes=scratch,
        name="layer",
        compiler_params=pltpu.CompilerParams(
            vmem_limit_bytes=63 * 1024 * 1024, collective_id=0, has_side_effects=True
        ),
        cost_estimate=pl.CostEstimate(flops=100 * 10**9, bytes_accessed=40 * 10**6, transcendentals=0),
    )(frames, tokens, cotangent, *weights)


def body(
    tokens, cotangent, lane_frames, pre_gain, pre_bias, w_project, query_bias, value_bias,
    w_out, out_bias, mid_gain, mid_bias, w_up, up_bias, w_down, down_bias,
):
    lanes, spatial, f = tokens.shape[1:]
    hidden = w_up.shape[1]
    tm_count = lax.axis_size("tm")
    weights = (
        pre_gain, pre_bias, w_project, query_bias, value_bias, w_out, out_bias,
        mid_gain, mid_bias, w_up, up_bias, w_down, down_bias,
    )
    out, input_grad, gathered, small = layer_call(
        lanes, spatial, f, hidden, tm_count, lax.axis_size("clip"), lane_frames,
        tokens.transpose(0, 2, 1, 3), cotangent.transpose(0, 2, 1, 3), weights,
    )
    vmem, hbm = pl.BlockSpec(memory_space=pltpu.VMEM), pl.BlockSpec(memory_space=pl.ANY)
    sizes = [f] * 7 + [hidden, f]
    wide = ((f, 3 * f), (f, f), (f, hidden), (hidden, f))
    dma = lambda *n: pltpu.SemaphoreType.DMA(n)
    got = pl.pallas_call(
        finish_kernel,
        in_specs=[hbm] * 3 + [vmem],
        out_specs=[hbm] * 6 + [vmem] * len(sizes),
        out_shape=[jax.ShapeDtypeStruct((1, spatial, lanes, f), BF16)] * 2
        + [jax.ShapeDtypeStruct(n, F32) for n in wide]
        + [jax.ShapeDtypeStruct((n,), F32) for n in sizes],
        scratch_shapes=[
            pltpu.VMEM((2, lanes, spatial, f), BF16), pltpu.VMEM((2, spatial, lanes, f), BF16),
            pltpu.VMEM((3, f, hidden), BF16),
        ] + [pltpu.VMEM(n, F32) for n in wide] + [dma(2, 3), dma(3), dma(2, 3), dma(4)],
        name="finish",
        compiler_params=pltpu.CompilerParams(vmem_limit_bytes=63 * 1024 * 1024),
    )(out, input_grad, gathered, small)
    out, input_grad = (v.transpose(0, 2, 1, 3) for v in got[:2])
    g_project, g_out, g_up, g_down = got[2:6]
    pre_gain, pre_bias, query_bias, value_bias, out_bias, mid_gain, mid_bias, up_bias, down_bias = got[6:]
    return (
        out, input_grad, pre_gain, pre_bias, g_project, query_bias, value_bias, g_out, out_bias,
        mid_gain, mid_bias, g_up, up_bias, g_down, down_bias,
    )


def solution(mesh):
    spread = P("tm", "clip", None, None)
    return jax.shard_map(
        body,
        mesh=mesh,
        in_specs=(spread, spread, P("clip")) + (P(),) * 13,
        out_specs=(spread, spread) + (P(),) * 13,
        check_vma=False,
    )
```
